256 devices in a mesh: section: 2 (over core), seq: 16 (over z, x_hi), vocab: 8 (over y, x_lo).
Axes of the slice: x: 4 (x_hi: 2, x_lo: 2; x = x_hi * 2 + x_lo), y: 4, z: 8, core: 2. Of those that a mesh axis runs over, the one named last changes fastest.
Arguments:
- hidden: bfloat16 [2, 2048, 4096], P(None, 'seq'), may hold values from -8 to 8
- head_weight: bfloat16 [4096, 20480], P('seq', ('section', 'vocab')), may hold values from -1 to 1
- teacher_logits: bfloat16 [2, 2048, 20480], P(None, 'seq', ('section', 'vocab')), may hold values from -300 to 300
- targets: int32 [2, 2048], P(None, 'seq'), may hold values from 0 to 20479
- span_inputs: bfloat16 [2, 2, 2, 2048, 4096], P('section', None, None, 'seq', 'vocab'), may hold values from -6 to 6
- span_gains: float32 [2, 2, 4096], P('section', None, 'vocab'), may hold values from 0.5 to 1.5
- span_weights: bfloat16 [2, 2, 32, 128, 128], P('section', None, 'vocab'), may hold values from -0.625 to 0.625
Outputs:
- input_grads: bfloat16 [2, 2, 2, 2048, 4096], P('section', None, None, 'seq', 'vocab')
- loss: float32 [], replicated
The draws below stay inside these ranges and needn't reach their ends.
All inputs are finite; a program needn't handle non-finite values.
Results may differ from the reference program's by a relative error of at most 0.0069.
Values may be sent and summed in bfloat16 or wider, within the bound.
A program may use at most 64 MiB of HBM per device.

```python
import jax
import jax.numpy as jnp
from jax import lax

D = 4096
HEADS = 32
HEAD = 128
MB = 2
TOK_DEV = 128
LOSS_SCALE = 16
TOKENS = 2048
VOCAB = 20480
SPANS = 4
N_SECTION = 2
N_SEQ = 16


def position_ramp(top):
    position = jnp.arange(TOKENS, dtype=jnp.float32) / max(TOKENS - 1, 1)
    return jnp.tile(1.0 + (top - 1.0) * position, MB)[:, None]


def draw_hidden(key, part):
    key = jax.random.fold_in(key, 1)
    values = jnp.clip(jax.random.normal(key, (MB * TOKENS, D), jnp.float32), -6.0, 6.0)
    values = jnp.clip(values * position_ramp(3.0), -8.0, 8.0)
    return values.reshape(MB, TOKENS, D).astype(jnp.bfloat16)


def draw_head_weight(key, part):
    key = jax.random.fold_in(key, 2)
    factor = 3.0 * D ** (-0.5)
    values = jnp.clip(jax.random.normal(key, (D, VOCAB), jnp.float32), -5.0, 5.0) * factor
    values = jnp.clip(values, -1.0, 1.0)
    return values.astype(jnp.bfloat16)


def draw_teacher_logits(key, part):
    key = jax.random.fold_in(key, 3)
    values = 3.0 * jnp.clip(jax.random.normal(key, (MB * TOKENS, VOCAB), jnp.float32), -6.0, 6.0)
    values = values * position_ramp(3.0)
    return values.reshape(MB, TOKENS, VOCAB).astype(jnp.bfloat16)


def with_ends(entries, stream_key, least, high):
    index_at = [jax.random.randint(jax.random.fold_in(stream_key, axis), (), 0, length) for axis, length in enumerate(entries.shape)]
    main_axis = entries.shape.index(max(entries.shape))
    beside = index_at[:main_axis] + [(index_at[main_axis] + 1) % entries.shape[main_axis]] + index_at[main_axis + 1:]
    return entries.at[tuple(index_at)].set(least).at[tuple(beside)].set(high)


def block_scale(rng, shape, split, low, largest):
    level, own = 1.0, jax.random.fold_in(rng, 6)
    for axis_at, blocks in split:
        steps = jnp.exp(jax.random.uniform(jax.random.fold_in(own, axis_at), (blocks,), jnp.float32, low / len(split), largest / len(split)))
        level = level * jnp.repeat(steps, shape[axis_at] // blocks).reshape([-1 if axis == axis_at else 1 for axis in range(len(shape))])
    return level


def bell_draw(rng, shape, deviation, limit, split=(), kind=jnp.bfloat16):
    gain = block_scale(rng, shape, split, -0.22, 0.18) if split else 1.0
    values = jax.random.normal(rng, shape, jnp.float32) * deviation * gain
    return jnp.minimum(jnp.maximum(values, -limit), limit).astype(kind)


def setup_inputs(seed: int = 0) -> dict:
    keys = jax.random.split(jax.random.key(seed), 8)
    return {
        "hidden": draw_hidden(jax.random.fold_in(keys[7], 71), 0),
        "head_weight": draw_head_weight(jax.random.fold_in(keys[7], 71), 0),
        "teacher_logits": draw_teacher_logits(jax.random.fold_in(keys[7], 71), 0),
        "targets": with_ends(jax.random.randint(keys[3], (MB, TOKENS), 0, VOCAB), jax.random.fold_in(keys[3], 1), 0, VOCAB - 1).astype(jnp.int32),
        "span_inputs": bell_draw(keys[4], (N_SECTION, 2, MB, TOKENS, D), 1.0, 6.0, ((0, 2), (3, 16), (4, 8))),
        "span_gains": jnp.clip(0.5 + 1.0 * jax.random.uniform(keys[5], (N_SECTION, 2, D), jnp.float32) ** block_scale(keys[5], (N_SECTION, 2, D), ((0, 2), (2, 8)), -0.2, 0.2), 0.5, 1.5),
        "span_weights": bell_draw(keys[6], (N_SECTION, 2, HEADS, HEAD, HEAD), (0.5 / HEAD ** 0.5), 0.625, ((0, 2), (2, 8))),
    }


ce_weight = 0.5
eps = 1e-06

def reference(hidden, head_weight, teacher_logits, targets, span_inputs, span_gains, span_weights):
    row_count = MB * TOKENS
    block_count = MB * N_SEQ

    def head_block(block):
        rows_hidden, rows_teacher, rows_target = block
        logits = jnp.dot(rows_hidden, head_weight, preferred_element_type=jnp.float32)
        teacher = rows_teacher.astype(jnp.float32)
        student_lse = jax.nn.logsumexp(logits, axis=-1, keepdims=True)
        teacher_lse = jax.nn.logsumexp(teacher, axis=-1, keepdims=True)
        teacher_prob = jnp.exp(teacher - teacher_lse)
        student_log = logits - student_lse
        kl_term = lax.optimization_barrier(jnp.sum(teacher_prob * (teacher - teacher_lse - student_log), axis=-1))
        target_hit = rows_target[:, None] == lax.broadcasted_iota(jnp.int32, (1, VOCAB), 1)
        target_logit = lax.optimization_barrier(jnp.sum(jnp.where(target_hit, logits, jnp.float32(0.0)), axis=-1))
        ce_term = student_lse[:, 0] - target_logit
        dlogits = (LOSS_SCALE * ((1.0 + ce_weight) * jnp.exp(student_log) - teacher_prob - ce_weight * target_hit.astype(jnp.float32))).astype(jnp.bfloat16)
        cot_rows = jnp.dot(dlogits, head_weight.T, preferred_element_type=jnp.float32).astype(jnp.bfloat16)
        return (kl_term + ce_weight * ce_term, cot_rows)
    row_terms, cot_blocks = lax.map(head_block, (hidden.reshape(block_count, TOK_DEV, D), teacher_logits.reshape(block_count, TOK_DEV, VOCAB), targets.reshape(block_count, TOK_DEV)))
    loss = jnp.mean(row_terms)
    cotangent = cot_blocks.reshape(row_count, D)
    half_count = SPANS // 2
    kept_grads = {}
    for span_index in range(SPANS - 1, -1, -1):
        if span_index < half_count:
            section_index, slot_index = (span_index, 0)
        else:
            section_index, slot_index = (SPANS - 1 - span_index, 1)
        saved = span_inputs[section_index, slot_index].reshape(row_count, D).astype(jnp.float32)
        gain_row = span_gains[section_index, slot_index]
        weight_heads = span_weights[section_index, slot_index].astype(jnp.float32)
        inv_rms = lax.rsqrt(lax.optimization_barrier(jnp.sum(saved * saved, axis=-1)) / D + eps)
        scaled = (saved * gain_row).astype(jnp.bfloat16).astype(jnp.float32).reshape(row_count, HEADS, HEAD)
        branch = jnp.einsum('rhi,hio->rho', scaled, weight_heads).reshape(row_count, D)
        cot_float = cotangent.astype(jnp.float32)
        grad_in = jnp.einsum('rho,hio->rhi', cot_float.reshape(row_count, HEADS, HEAD), weight_heads).reshape(row_count, D)
        norm_stat = lax.optimization_barrier(jnp.sum(cot_float * branch, axis=-1)) / D
        cotangent = (cot_float + inv_rms[:, None] * gain_row * grad_in - saved * (inv_rms ** 3 * norm_stat)[:, None]).astype(jnp.bfloat16)
        kept_grads[section_index, slot_index] = cotangent.reshape(MB, TOKENS, D)
    input_grads = jnp.stack([jnp.stack([kept_grads[section_index, 0], kept_grads[section_index, 1]]) for section_index in range(half_count)])
    return (input_grads, loss)
```

```python
import functools

import jax
import jax.numpy as jnp
from jax import lax
from jax.experimental import pallas as pl
from jax.experimental.pallas import tpu as pltpu
from jax.sharding import PartitionSpec as P

MESH = pl.DeviceIdType.MESH
F32 = jnp.float32
BF16 = jnp.bfloat16
LOSS_SCALE = 16
CE_WEIGHT = 0.5
EPS = 1e-06
HEAD = 128
SPAN_AT = ((0, 0), (1, 0), (1, 1), (0, 1))


def to_rows(columns, height):
    count = columns[0].shape[0]
    lane = lax.broadcasted_iota(jnp.int32, (count, 128), 1)
    wide = jnp.zeros((count, 128), F32)
    for i, column in enumerate(columns):
        wide = jnp.where(lane == i, column, wide)
    return wide.T[:height]


def to_columns(rows):
    height, count = rows.shape
    return jnp.concatenate([rows, jnp.zeros((128 - height, count), F32)], axis=0).T


def heads_dot(left, weights, transposed):
    dims = (((1,), (1,)), ((), ())) if transposed else (((1,), (0,)), ((), ()))
    parts = []
    for h in range(weights.shape[0]):
        parts.append(
            lax.dot_general(left[:, h * HEAD : (h + 1) * HEAD], weights[h], dims, preferred_element_type=F32)
        )
    return jnp.concatenate(parts, axis=1)


def kernel(
    nz, nv,
    hidden, head, teacher, targets, xin, gains, wspan,
    out, loss_ref,
    wbuf, hid, tea, tgt, logits, texp, dlog, stats, snd, rcv, xs, gs, ws, branch,
    sq, dots, lsend, lrecv, ys,
    loc_sem, zs_sem, zr_sem, ds_sem, dr_sem, ms_sem, mr_sem, sts_sem, str_sem, rss_sem, rsr_sem,
    sqs_sem, sqr_sem, dos_sem, dor_sem, ls_sem, lr_sem, os_sem, or_sem,
):
    core = lax.axis_index("section")
    seq = lax.axis_index("seq")
    voc = lax.axis_index("vocab")
    z, xh = seq // 2, seq % 2
    xl = voc % 2
    other = 1 - core
    half = nz // 2
    tok, width = hid.shape[1], hid.shape[2]
    rows, cols = head.shape[0], wbuf.shape[2]
    slice_width = xs.shape[3]
    plane = 2 * nv
    me = xh * nv + voc

    def at(c, zz, hh, v):
        return (c, zz * 2 + hh, v)

    def plane_peer(index):
        return at(core, z, index // nv, index % nv)

    mate = at(other, z, xh, voc)
    partner = at(core, z, 1 - xh, voc)
    partner_mate = at(other, z, 1 - xh, voc)
    near = at(core, z, 1 - xh, voc + 1 - 2 * xl)
    right = at(core, (z + 1) % nz, xh, voc)
    left = at(core, (z + nz - 1) % nz, xh, voc)
    far = []
    bit = 1
    while bit < nz:
        far.append(at(core, z + bit - 2 * bit * ((z // bit) % 2), xh, voc))
        bit *= 2

    barrier = pltpu.get_barrier_semaphore()
    direct = [mate, partner_mate, right, left] + far[1:]
    for peer in direct:
        pl.semaphore_signal(barrier, inc=1, device_id=peer, device_id_type=MESH)

    def greet(i, carry):
        pl.semaphore_signal(barrier, inc=1, device_id=plane_peer((me + i) % plane), device_id_type=MESH)
        return carry

    lax.fori_loop(1, plane, greet, 0)
    pl.semaphore_wait(barrier, len(direct) + plane - 1)

    def remote(src, dst, send, recv, peer):
        return pltpu.make_async_remote_copy(
            src_ref=src, dst_ref=dst, send_sem=send, recv_sem=recv, device_id=peer, device_id_type=MESH
        )

    sent = []

    def begin(copy):
        copy.start()
        sent.append(copy)

    def chunk(delta, q):
        zz = lax.rem(z + delta + nz, nz)
        hh = xh if q == 0 else 1 - xh
        return wbuf.at[core, pl.ds(pl.multiple_of((zz * 2 + hh) * rows, rows), rows), :]

    def mate_chunk(delta, q):
        zz = lax.rem(z + delta + nz, nz)
        hh = xh if q == 0 else 1 - xh
        return wbuf.at[other, pl.ds(pl.multiple_of((zz * 2 + hh) * rows, rows), rows), :]

    def own_columns(hh):
        return pl.ds(pl.multiple_of(hh * cols, cols), cols)

    own_block = head.at[:, own_columns(xh)]

    def ring_index(k, q):
        return (k - 1) * 2 + (q if k < half else 0)

    def ring_send(way, k, q):
        delta = -(k - 1) if way == 0 else k - 1
        slot = chunk(delta, q)
        src = own_block if k == 1 and q == 0 else slot
        i = ring_index(k, q)
        begin(remote(src, slot, zs_sem.at[way, i], zr_sem.at[way, i], right if way == 0 else left))

    def ring_wait(way, k, q):
        slot = chunk(-k if way == 0 else k, q)
        i = ring_index(k, q)
        remote(slot, slot, zs_sem.at[way, i], zr_sem.at[way, i], right).wait_recv()

    def mate_send(delta, q):
        slot = chunk(delta, q)
        src = own_block if delta == 0 and q == 0 else slot
        i = (delta % nz) * 2 + q
        begin(remote(src, slot, ds_sem.at[i], dr_sem.at[i], mate))

    def mate_wait(delta, q):
        slot = mate_chunk(delta, q)
        i = (delta % nz) * 2 + q
        remote(slot, slot, ds_sem.at[i], dr_sem.at[i], mate).wait_recv()

    my_rows = wbuf.at[core, pl.ds(pl.multiple_of(seq * rows, rows), rows), :]
    begin(remote(head.at[:, own_columns(1 - xh)], my_rows, ms_sem.at[0], mr_sem.at[0], partner))
    ring_send(0, 1, 0)
    if half > 1:
        ring_send(1, 1, 0)
    mate_send(0, 0)

    local = [
        pltpu.make_async_copy(own_block, my_rows, loc_sem.at[0]),
        pltpu.make_async_copy(xin.at[0, :, core], xs.at[core], loc_sem.at[1]),
        pltpu.make_async_copy(gains.at[0], gs.at[core], loc_sem.at[2]),
        pltpu.make_async_copy(wspan.at[0], ws.at[core], loc_sem.at[3]),
        pltpu.make_async_copy(hidden.at[core], hid.at[xh], loc_sem.at[4]),
        pltpu.make_async_copy(teacher.at[core, :, own_columns(xh)], tea.at[core, xh], loc_sem.at[5]),
        pltpu.make_async_copy(targets, tgt.at[xh], loc_sem.at[6]),
    ]
    for copy in local:
        copy.start()
    begin(remote(xin.at[0, :, other], xs.at[core], ms_sem.at[1], mr_sem.at[1], mate))
    begin(remote(gains.at[0], gs.at[core], ms_sem.at[2], mr_sem.at[2], mate))
    begin(remote(wspan.at[0], ws.at[core], ms_sem.at[3], mr_sem.at[3], mate))
    begin(remote(teacher.at[other, :, own_columns(xh)], tea.at[core, xh], ms_sem.at[4], mr_sem.at[4], mate))

    slot = chunk(0, 1)
    remote(slot, slot, ms_sem.at[0], mr_sem.at[0], partner).wait_recv()
    if half > 1:
        ring_send(0, 1, 1)
    ring_send(1, 1, 1)
    mate_send(0, 1)
    begin(remote(hidden.at[core], hid.at[xh], ms_sem.at[5], mr_sem.at[5], near))
    begin(remote(targets, tgt.at[xh], ms_sem.at[6], mr_sem.at[6], partner))
    begin(remote(teacher.at[core, :, own_columns(1 - xh)], tea.at[core, xh], ms_sem.at[7], mr_sem.at[7], partner))
    begin(
        remote(teacher.at[other, :, own_columns(1 - xh)], tea.at[core, xh], ms_sem.at[8], mr_sem.at[8], partner_mate)
    )

    for copy in local:
        copy.wait()
    remote(xs.at[other], xs.at[other], ms_sem.at[1], mr_sem.at[1], mate).wait_recv()
    remote(gs.at[other], gs.at[other], ms_sem.at[2], mr_sem.at[2], mate).wait_recv()
    remote(ws.at[other], ws.at[other], ms_sem.at[3], mr_sem.at[3], mate).wait_recv()

    def saved(c):
        return xs[SPAN_AT[c]].astype(F32)

    def gain(c):
        section, slot_index = SPAN_AT[c]
        return gs[section, slot_index : slot_index + 1, :]

    def exchange(buf, send_sems, recv_sems):
        def send(i, carry):
            peer = at(core, z, xh, (voc + i) % nv)
            remote(buf.at[voc], buf.at[voc], send_sems.at[i], recv_sems.at[i], peer).start()
            return carry

        lax.fori_loop(1, nv, send, 0)

    def exchange_wait(buf, send_sems, recv_sems):
        def wait(i, carry):
            src = (voc + nv - i) % nv
            remote(buf.at[src], buf.at[src], send_sems.at[i], recv_sems.at[i], mate).wait_recv()
            remote(buf.at[voc], buf.at[voc], send_sems.at[i], recv_sems.at[i], mate).wait_send()
            return carry

        lax.fori_loop(1, nv, wait, 0)
        total = buf[0]
        for i in range(1, nv):
            total = total + buf[i]
        return total

    squares = []
    for c in range(4):
        value = saved(c)
        squares.append(jnp.sum(value * value, axis=1, keepdims=True))
    sq[voc] = to_rows(squares, 8)
    exchange(sq, sqs_sem, sqr_sem)
    for c in range(4):
        scaled = (saved(c) * gain(c)).astype(BF16)
        branch[c] = heads_dot(scaled, ws[SPAN_AT[c]], False)

    def ring_turn(k, q):
        for way in (0, 1):
            if k == half and way != q:
                continue
            ring_wait(way, k, q)
            if k + 1 < half or (k + 1 == half and way == q):
                ring_send(way, k + 1, q)
            mate_send(-k if way == 0 else k, q)

    def multiply(delta, first=False):
        for q in (0, 1):
            mate_wait(delta, q)
        zz = lax.rem(z + delta + nz, nz)
        span = pl.ds(pl.multiple_of(zz * 2 * rows, 2 * rows), 2 * rows)
        left_part = hid[:, :, span].reshape(2 * tok, 2 * rows)
        for s in (0, 1):
            product = jnp.dot(left_part, wbuf[s, span, :], preferred_element_type=F32)
            if first:
                logits[s] = product
            else:
                logits[s] += product

    def hidden_wait():
        slot = hid.at[1 - xh]
        remote(slot, slot, ms_sem.at[5], mr_sem.at[5], near).wait_recv()

    def span_ready():
        total = to_columns(exchange_wait(sq, sqs_sem, sqr_sem))
        inv = [lax.rsqrt(total[:, c : c + 1] / width + EPS) for c in range(4)]

        def lift(c, value):
            grad = heads_dot(value.astype(BF16), ws[SPAN_AT[c]], True)
            return value + inv[c] * gain(c) * grad

        def inner(c, value):
            return jnp.sum(value * branch[c], axis=1, keepdims=True)

        u3 = saved(3) * inv[3] ** 3
        e32 = inner(2, u3)
        v = lift(2, u3)
        e31 = inner(1, v)
        v = lift(1, v)
        e30 = inner(0, v)
        u2 = saved(2) * inv[2] ** 3
        e21 = inner(1, u2)
        e20 = inner(0, lift(1, u2))
        e10 = inner(0, saved(1) * inv[1] ** 3)
        return inv, lift, inner, [e32, e31, e30, e21, e20, e10]

    def teacher_ready():
        pairs = ((other, xh, 4, mate), (core, 1 - xh, 7, partner), (other, 1 - xh, 8, partner_mate))
        for s, hh, i, peer in pairs:
            slot = tea.at[s, hh]
            remote(slot, slot, ms_sem.at[i], mr_sem.at[i], peer).wait_recv()
        slot = tgt.at[1 - xh]
        remote(slot, slot, ms_sem.at[6], mr_sem.at[6], partner).wait_recv()
        values = [tea[s].reshape(2 * tok, cols).astype(F32) for s in (0, 1)]
        top = jnp.max(jnp.maximum(values[0], values[1]), axis=1, keepdims=True)
        total = jnp.zeros((2 * tok, 1), F32)
        for s in (0, 1):
            value = jnp.exp(values[s] - top)
            texp[s] = value
            total += jnp.sum(value, axis=1, keepdims=True)
        return top, total

    state = {}
    units = []
    for k in range(1, half + 1):
        for q in (0, 1):
            ring_turn(k, q)
            if k == 1 and q == 1:
                state["spans"] = span_ready()
            if (k == 2 and q == 1) or (half == 1 and q == 1):
                state["teacher"] = teacher_ready()
                hidden_wait()
                multiply(0, first=True)
                for d in range(1, min(2, half)):
                    multiply(-d)
                    multiply(d)
            if k >= 3 and q == 0:
                multiply(-(k - 1))
                multiply(k - 1)
    if half == 2:
        pass
    multiply(half)
    inv, lift, inner, cross_spans = state["spans"]
    teacher_top, teacher_total = state["teacher"]

    def target_column():
        parts = []
        for hh in (0, 1):
            row = jnp.where(core == 0, tgt[hh, 0:1, :], tgt[hh, 1:2, :])
            parts.append(jnp.broadcast_to(row, (128, tok)).T[:, 0:1])
        return jnp.concatenate(parts, axis=0)

    wanted = target_column()

    def hit(s):
        start = (s * nv + voc) * 2 * cols + xh * cols
        return wanted - start == lax.broadcasted_iota(jnp.int32, (2 * tok, cols), 1)

    student_top = jnp.max(jnp.maximum(logits[0], logits[1]), axis=1, keepdims=True)
    student_total = jnp.zeros((2 * tok, 1), F32)
    cross = jnp.zeros((2 * tok, 1), F32)
    target_logit = jnp.zeros((2 * tok, 1), F32)
    for s in (0, 1):
        value = logits[s]
        cross += jnp.sum(texp[s] * (tea[s].reshape(2 * tok, cols).astype(F32) - value), axis=1, keepdims=True)
        target_logit += jnp.sum(jnp.where(hit(s), value, 0.0), axis=1, keepdims=True)
        value = jnp.exp(value - student_top)
        logits[s] = value
        student_total += jnp.sum(value, axis=1, keepdims=True)
    stats[me] = to_rows([student_top, student_total, teacher_top, teacher_total, cross, target_logit], 8)

    def stats_send(i, carry):
        peer = plane_peer((me + i) % plane)
        remote(stats.at[me], stats.at[me], sts_sem.at[i], str_sem.at[i], peer).start()
        return carry

    def stats_wait(i, carry):
        src = (me + plane - i) % plane
        remote(stats.at[src], stats.at[src], sts_sem.at[i], str_sem.at[i], mate).wait_recv()
        remote(stats.at[me], stats.at[me], sts_sem.at[i], str_sem.at[i], mate).wait_send()
        return carry

    lax.fori_loop(1, plane, stats_send, 0)
    lax.fori_loop(1, plane, stats_wait, 0)
    top_s, top_t = stats[0, 0:1, :], stats[0, 2:3, :]
    for i in range(1, plane):
        top_s = jnp.maximum(top_s, stats[i, 0:1, :])
        top_t = jnp.maximum(top_t, stats[i, 2:3, :])
    sum_s, sum_t, sum_x, sum_l = (jnp.zeros_like(top_s) for _ in range(4))
    for i in range(plane):
        part = stats[i]
        sum_s += part[1:2] * jnp.exp(part[0:1] - top_s)
        factor = jnp.exp(part[2:3] - top_t)
        sum_t += part[3:4] * factor
        sum_x += part[4:5] * factor
        sum_l += part[5:6]
    lse_s = top_s + jnp.log(sum_s)
    lse_t = top_t + jnp.log(sum_t)
    terms = sum_x / sum_t - lse_t + lse_s + CE_WEIGHT * (lse_s - sum_l)
    scales = to_columns(jnp.concatenate([lse_s, lse_t], axis=0))
    student_scale = jnp.exp(student_top - scales[:, 0:1])
    teacher_scale = jnp.exp(teacher_top - scales[:, 1:2])

    loss_peers = [mate] + far
    lsend[0] = jnp.broadcast_to(jnp.sum(terms, axis=1, keepdims=True), (8, 128))

    def loss_send(level):
        begin(remote(lsend.at[level], lrecv.at[level], ls_sem.at[level], lr_sem.at[level], loss_peers[level]))

    def loss_wait(level):
        slot = lrecv.at[level]
        remote(slot, slot, ls_sem.at[level], lr_sem.at[level], mate).wait_recv()
        return lsend[level] + lrecv[level]

    loss_send(0)

    for s in (0, 1):
        value = (1.0 + CE_WEIGHT) * (logits[s] * student_scale) - texp[s] * teacher_scale
        value = value - jnp.where(hit(s), CE_WEIGHT, 0.0)
        dlog[s] = (LOSS_SCALE * value).astype(BF16)

    def piece(hh, v):
        return hh * nv + v

    nt = (((1,), (1,)), ((), ()))

    def slice_turn(i, carry):
        v = (voc + i + 1) % nv
        span = pl.ds(pl.multiple_of(v * slice_width, slice_width), slice_width)
        part = lax.dot_general(dlog[0], wbuf[0, span, :], nt, preferred_element_type=F32)
        part += lax.dot_general(dlog[1], wbuf[1, span, :], nt, preferred_element_type=F32)
        part = part.astype(BF16)
        for hh in (0, 1):
            snd[piece(hh, v)] = part[hh * tok : (hh + 1) * tok]

            @pl.when(jnp.logical_or(hh != xh, v != voc))
            def _():
                to = piece(hh, v)
                delta = (to - me + plane) % plane
                remote(snd.at[to], rcv.at[me], rss_sem.at[delta], rsr_sem.at[delta], plane_peer(to)).start()

        return carry

    lax.fori_loop(0, nv, slice_turn, 0)
    rcv[me] = snd[me]
    if len(loss_peers) > 1:
        lsend[1] = loss_wait(0)
        loss_send(1)

    def sum_turn(i, carry):
        src = (me + plane - i) % plane
        remote(rcv.at[src], rcv.at[src], rss_sem.at[i], rsr_sem.at[i], mate).wait_recv()
        to = (me + i) % plane
        remote(snd.at[to], rcv.at[me], rss_sem.at[i], rsr_sem.at[i], mate).wait_send()
        return carry

    lax.fori_loop(1, plane, sum_turn, 0)
    total = rcv[0].astype(F32)
    for i in range(1, plane):
        total = total + rcv[i].astype(F32)
    cotangent = total.astype(BF16)

    value = cotangent.astype(F32)
    products = [inner(3, value)]
    for c in (3, 2, 1):
        value = lift(c, value)
        products.append(inner(c - 1, value))
    dots[voc] = to_rows(products + cross_spans, 16)
    exchange(dots, dos_sem, dor_sem)
    for level in range(2, len(loss_peers)):
        lsend[level] = loss_wait(level - 1)
        loss_send(level)
    loss_total = loss_wait(len(loss_peers) - 1)
    loss_ref[0, 0] = jnp.max(loss_total) / (4 * tok * nz)
    found = to_columns(exchange_wait(dots, dos_sem, dor_sem)) / width
    d3, d2, d1, d0, e32, e31, e30, e21, e20, e10 = (found[:, i : i + 1] for i in range(10))
    s3 = d3
    s2 = d2 - s3 * e32
    s1 = d1 - s3 * e31 - s2 * e21
    s0 = d0 - s3 * e30 - s2 * e20 - s1 * e10
    value = cotangent.astype(F32)

    def hand_out(slot_index):
        pltpu.make_async_copy(ys.at[core, slot_index], out.at[0, slot_index, core], loc_sem.at[slot_index]).start()
        begin(
            remote(
                ys.at[other, slot_index], out.at[0, slot_index, core], os_sem.at[slot_index], or_sem.at[slot_index], mate
            )
        )

    for c, stat in ((3, s3), (2, s2), (1, s1), (0, s0)):
        fresh = (lift(c, value) - saved(c) * (inv[c] ** 3 * stat)).astype(BF16)
        ys[SPAN_AT[c]] = fresh
        value = fresh.astype(F32)
        if c == 2:
            hand_out(1)
    hand_out(0)

    for slot_index in (1, 0):
        pltpu.make_async_copy(
            ys.at[core, slot_index], out.at[0, slot_index, core], loc_sem.at[slot_index]
        ).wait()
        slot = out.at[0, slot_index, other]
        remote(slot, slot, os_sem.at[slot_index], or_sem.at[slot_index], mate).wait_recv()
    for copy in sent:
        copy.wait_send()


def solution(mesh):
    n_seq, n_voc = mesh.shape["seq"], mesh.shape["vocab"]
    nz = n_seq // 2

    def per_device(hidden, head_weight, teacher_logits, targets, span_inputs, span_gains, span_weights):
        _, tok, width = hidden.shape
        rows, shard = head_weight.shape
        cols = shard // 2
        slice_width = span_inputs.shape[4]
        heads = span_weights.shape[2]
        plane = 2 * n_voc
        levels = 1 + (nz.bit_length() - 1)
        half = nz // 2
        dma = pltpu.SemaphoreType.DMA
        any_space = pl.BlockSpec(memory_space=pl.ANY)
        grads, loss = pl.pallas_call(
            functools.partial(kernel, nz, n_voc),
            out_shape=(
                jax.ShapeDtypeStruct((1, 2, 2, tok, slice_width), BF16),
                jax.ShapeDtypeStruct((1, 1), F32),
            ),
            in_specs=[any_space] * 7,
            out_specs=(any_space, pl.BlockSpec(memory_space=pltpu.SMEM)),
            scratch_shapes=[
                pltpu.VMEM((2, width, cols), BF16),
                pltpu.VMEM((2, tok, width), BF16),
                pltpu.VMEM((2, 2, tok, cols), BF16),
                pltpu.VMEM((2, 2, tok), jnp.int32),
                pltpu.VMEM((2, 2 * tok, cols), F32),
                pltpu.VMEM((2, 2 * tok, cols), F32),
                pltpu.VMEM((2, 2 * tok, cols), BF16),
                pltpu.VMEM((plane, 8, 2 * tok), F32),
                pltpu.VMEM((plane, tok, slice_width), BF16),
                pltpu.VMEM((plane, tok, slice_width), BF16),
                pltpu.VMEM((2, 2, tok, slice_width), BF16),
                pltpu.VMEM((2, 2, slice_width), F32),
                pltpu.VMEM((2, 2, heads, HEAD, HEAD), BF16),
                pltpu.VMEM((4, tok, slice_width), F32),
                pltpu.VMEM((n_voc, 8, tok), F32),
                pltpu.VMEM((n_voc, 16, tok), F32),
                pltpu.VMEM((levels, 8, 128), F32),
                pltpu.VMEM((levels, 8, 128), F32),
                pltpu.VMEM((2, 2, tok, slice_width), BF16),
                dma((7,)),
                dma((2, 2 * half - 1)),
                dma((2, 2 * half - 1)),
                dma((2 * nz,)),
                dma((2 * nz,)),
                dma((9,)),
                dma((9,)),
                dma((plane,)),
                dma((plane,)),
                dma((plane,)),
                dma((plane,)),
                dma((n_voc,)),
                dma((n_voc,)),
                dma((n_voc,)),
                dma((n_voc,)),
                dma((levels,)),
                dma((levels,)),
                dma((2,)),
                dma((2,)),
            ],
            compiler_params=pltpu.CompilerParams(
                collective_id=0, has_side_effects=True, vmem_limit_bytes=48 * 1024 * 1024
            ),
        )(hidden, head_weight, teacher_logits, targets, span_inputs, span_gains, span_weights)
        return grads, loss.reshape(())

    placed = (
        P(None, "seq", None),
        P("seq", ("section", "vocab")),
        P(None, "seq", ("section", "vocab")),
        P(None, "seq"),
        P("section", None, None, "seq", "vocab"),
        P("section", None, "vocab"),
        P("section", None, "vocab", None, None),
    )
    return jax.shard_map(
        per_device,
        mesh=mesh,
        in_specs=placed,
        out_specs=(P("section", None, None, "seq", "vocab"), P()),
        check_vma=False,
    )
```

```python
import functools

import jax
import jax.numpy as jnp
from jax import lax
from jax.experimental import pallas as pl
from jax.experimental.pallas import tpu as pltpu
from jax.sharding import PartitionSpec as P

MESH = pl.DeviceIdType.MESH
F32 = jnp.float32
BF16 = jnp.bfloat16
LOSS_SCALE = 16
CE_WEIGHT = 0.5
EPS = 1e-06
HEAD = 128
SPAN_AT = ((0, 0), (1, 0), (1, 1), (0, 1))


def to_rows(columns, height):
    count = columns[0].shape[0]
    lane = lax.broadcasted_iota(jnp.int32, (count, 128), 1)
    wide = jnp.zeros((count, 128), F32)
    for i, column in enumerate(columns):
        wide = jnp.where(lane == i, column, wide)
    return wide.T[:height]


def to_columns(rows):
    height, count = rows.shape
    return jnp.concatenate([rows, jnp.zeros((128 - height, count), F32)], axis=0).T


def heads_dot(left, weights, transposed):
    dims = (((1,), (1,)), ((), ())) if transposed else (((1,), (0,)), ((), ()))
    parts = []
    for h in range(weights.shape[0]):
        parts.append(
            lax.dot_general(left[:, h * HEAD : (h + 1) * HEAD], weights[h], dims, preferred_element_type=F32)
        )
    return jnp.concatenate(parts, axis=1)


def kernel(
    nz, nv,
    hidden, head, teacher, targets, xin, gains, wspan,
    out, loss_ref,
    wbuf, hid, tea, tgt, logits, texp, dlog, stats, snd_x, rcv_x, snd_y, rcv_y, two_x, end_x, two_y, end_y, xs, gs, ws, branch,
    sq, dots, lsend, lrecv, ys,
    loc_sem, zs_sem, zr_sem, ds_sem, dr_sem, ms_sem, mr_sem, sts_sem, str_sem, xs_sem, xr_sem, ys_sem, yr_sem,
    exs_sem, exr_sem, eys_sem, eyr_sem,    sqs_sem, sqr_sem, dos_sem, dor_sem, ls_sem, lr_sem, os_sem, or_sem,
):
    core = lax.axis_index("section")
    seq = lax.axis_index("seq")
    voc = lax.axis_index("vocab")
    z, xh = seq // 2, seq % 2
    xl = voc % 2
    other = 1 - core
    half = nz // 2
    tok, width = hid.shape[1], hid.shape[2]
    rows, cols = head.shape[0], wbuf.shape[2]
    slice_width = xs.shape[3]
    plane = 2 * nv
    me = xh * nv + voc

    def at(c, zz, hh, v):
        return (c, zz * 2 + hh, v)

    def plane_peer(index):
        return at(core, z, index // nv, index % nv)

    mate = at(other, z, xh, voc)
    partner = at(core, z, 1 - xh, voc)
    partner_mate = at(other, z, 1 - xh, voc)
    near = at(core, z, 1 - xh, voc + 1 - 2 * xl)
    right = at(core, (z + 1) % nz, xh, voc)
    left = at(core, (z + nz - 1) % nz, xh, voc)
    far = []
    bit = 1
    while bit < nz:
        far.append(at(core, z + bit - 2 * bit * ((z // bit) % 2), xh, voc))
        bit *= 2

    barrier = pltpu.get_barrier_semaphore()
    direct = [mate, partner_mate, right, left] + far[1:]
    for peer in direct:
        pl.semaphore_signal(barrier, inc=1, device_id=peer, device_id_type=MESH)

    def greet(i, carry):
        pl.semaphore_signal(barrier, inc=1, device_id=plane_peer((me + i) % plane), device_id_type=MESH)
        return carry

    lax.fori_loop(1, plane, greet, 0)
    pl.semaphore_wait(barrier, len(direct) + plane - 1)

    def remote(src, dst, send, recv, peer):
        return pltpu.make_async_remote_copy(
            src_ref=src, dst_ref=dst, send_sem=send, recv_sem=recv, device_id=peer, device_id_type=MESH
        )

    sent = []

    def begin(copy):
        copy.start()
        sent.append(copy)

    part_rows = rows // 2

    def part_at(section, delta, part):
        zz = lax.rem(z + delta + nz, nz)
        hh = xh if part < 2 else 1 - xh
        start = (zz * 2 + hh) * rows + (part % 2) * part_rows
        return wbuf.at[section, pl.ds(pl.multiple_of(start, part_rows), part_rows), :]

    def own_columns(hh):
        return pl.ds(pl.multiple_of(hh * cols, cols), cols)

    own_block = head.at[:, own_columns(xh)]

    def own_part(part, hh):
        return head.at[pl.ds(part * part_rows, part_rows), own_columns(hh)]

    ring_parts = [
        [(k, part) for k in range(1, half) for part in range(4)] + [(half, 2 * way), (half, 2 * way + 1)]
        for way in (0, 1)
    ]
    ring_count = len(ring_parts[0])
    ring_copies = [[], []]

    def ring_send(way, i):
        k, part = ring_parts[way][i]
        slot = part_at(core, -(k - 1) if way == 0 else k - 1, part)
        src = own_part(part, xh) if k == 1 and part < 2 else slot
        if k > 1:
            ring_wait(way, ring_parts[way].index((k - 1, part)))
        if i >= 2:
            ring_copies[way][i - 2].wait_send()
        copy = remote(src, slot, zs_sem.at[way, i], zr_sem.at[way, i], right if way == 0 else left)
        copy.start()
        ring_copies[way].append(copy)

    arrived = [0, 0]

    def ring_wait(way, i):
        while arrived[way] <= i:
            j = arrived[way]
            k, part = ring_parts[way][j]
            delta = -k if way == 0 else k
            slot = part_at(core, delta, part)
            remote(slot, slot, zs_sem.at[way, j], zr_sem.at[way, j], right).wait_recv()
            mate_send(delta, part)
            arrived[way] += 1

    def mate_send(delta, part):
        slot = part_at(core, delta, part)
        src = own_part(part, xh) if delta == 0 and part < 2 else slot
        i = (delta % nz) * 4 + part
        begin(remote(src, slot, ds_sem.at[i], dr_sem.at[i], mate))

    def mate_wait(delta, part):
        slot = part_at(other, delta, part)
        i = (delta % nz) * 4 + part
        remote(slot, slot, ds_sem.at[i], dr_sem.at[i], mate).wait_recv()

    def partner_send(part):
        slot = part_at(core, 0, part)
        copy = remote(own_part(part, 1 - xh), slot, ms_sem.at[9 * part], mr_sem.at[9 * part], partner)
        copy.start()
        return copy

    def partner_wait(part):
        slot = part_at(core, 0, part + 2)
        remote(slot, slot, ms_sem.at[9 * part], mr_sem.at[9 * part], partner).wait_recv()
        mate_send(0, part + 2)

    my_rows = wbuf.at[core, pl.ds(pl.multiple_of(seq * rows, rows), rows), :]
    first = partner_send(0)
    for i in (0, 1):
        for way in (0, 1):
            ring_send(way, i)
        mate_send(0, i)

    local = [
        pltpu.make_async_copy(own_block, my_rows, loc_sem.at[0]),
        pltpu.make_async_copy(xin.at[0, :, core], xs.at[core], loc_sem.at[1]),
        pltpu.make_async_copy(gains.at[0], gs.at[core], loc_sem.at[2]),
        pltpu.make_async_copy(wspan.at[0], ws.at[core], loc_sem.at[3]),
        pltpu.make_async_copy(hidden.at[core], hid.at[xh], loc_sem.at[4]),
        pltpu.make_async_copy(teacher.at[core, :, own_columns(xh)], tea.at[core, xh], loc_sem.at[5]),
        pltpu.make_async_copy(targets, tgt.at[xh], loc_sem.at[6]),
    ]
    for copy in local:
        copy.start()
    begin(remote(xin.at[0, :, other], xs.at[core], ms_sem.at[1], mr_sem.at[1], mate))
    begin(remote(gains.at[0], gs.at[core], ms_sem.at[2], mr_sem.at[2], mate))
    begin(remote(wspan.at[0], ws.at[core], ms_sem.at[3], mr_sem.at[3], mate))
    begin(remote(teacher.at[other, :, own_columns(xh)], tea.at[core, xh], ms_sem.at[4], mr_sem.at[4], mate))

    first.wait_send()
    second = partner_send(1)
    partner_wait(0)
    for way in (0, 1):
        ring_send(way, 2)
    second.wait_send()
    begin(remote(hidden.at[core], hid.at[xh], ms_sem.at[5], mr_sem.at[5], near))
    begin(remote(targets, tgt.at[xh], ms_sem.at[6], mr_sem.at[6], partner))
    begin(remote(teacher.at[core, :, own_columns(1 - xh)], tea.at[core, xh], ms_sem.at[7], mr_sem.at[7], partner))
    begin(
        remote(teacher.at[other, :, own_columns(1 - xh)], tea.at[core, xh], ms_sem.at[8], mr_sem.at[8], partner_mate)
    )

    for copy in local:
        copy.wait()
    remote(xs.at[other], xs.at[other], ms_sem.at[1], mr_sem.at[1], mate).wait_recv()
    remote(gs.at[other], gs.at[other], ms_sem.at[2], mr_sem.at[2], mate).wait_recv()
    remote(ws.at[other], ws.at[other], ms_sem.at[3], mr_sem.at[3], mate).wait_recv()

    def saved(c):
        return xs[SPAN_AT[c]].astype(F32)

    def gain(c):
        section, slot_index = SPAN_AT[c]
        return gs[section, slot_index : slot_index + 1, :]

    def exchange(buf, send_sems, recv_sems):
        def send(i, carry):
            peer = at(core, z, xh, (voc + i) % nv)
            remote(buf.at[voc], buf.at[voc], send_sems.at[i], recv_sems.at[i], peer).start()
            return carry

        lax.fori_loop(1, nv, send, 0)

    def exchange_wait(buf, send_sems, recv_sems):
        def wait(i, carry):
            src = (voc + nv - i) % nv
            remote(buf.at[src], buf.at[src], send_sems.at[i], recv_sems.at[i], mate).wait_recv()
            remote(buf.at[voc], buf.at[voc], send_sems.at[i], recv_sems.at[i], mate).wait_send()
            return carry

        lax.fori_loop(1, nv, wait, 0)
        total = buf[0]
        for i in range(1, nv):
            total = total + buf[i]
        return total

    squares = []
    for c in range(4):
        value = saved(c)
        squares.append(jnp.sum(value * value, axis=1, keepdims=True))
    sq[voc] = to_rows(squares, 8)
    exchange(sq, sqs_sem, sqr_sem)
    for c in range(4):
        scaled = (saved(c) * gain(c)).astype(BF16)
        branch[c] = heads_dot(scaled, ws[SPAN_AT[c]], False)

    def multiply(delta, first=False):
        for part in range(4):
            mate_wait(delta, part)
        zz = lax.rem(z + delta + nz, nz)
        span = pl.ds(pl.multiple_of(zz * 2 * rows, 2 * rows), 2 * rows)
        left_part = hid[:, :, span].reshape(2 * tok, 2 * rows)
        for s in (0, 1):
            product = jnp.dot(left_part, wbuf[s, span, :], preferred_element_type=F32)
            if first:
                logits[s] = product
            else:
                logits[s] += product

    def hidden_wait():
        slot = hid.at[1 - xh]
        remote(slot, slot, ms_sem.at[5], mr_sem.at[5], near).wait_recv()

    def span_ready():
        total = to_columns(exchange_wait(sq, sqs_sem, sqr_sem))
        inv = [lax.rsqrt(total[:, c : c + 1] / width + EPS) for c in range(4)]

        def lift(c, value):
            grad = heads_dot(value.astype(BF16), ws[SPAN_AT[c]], True)
            return value + inv[c] * gain(c) * grad

        def inner(c, value):
            return jnp.sum(value * branch[c], axis=1, keepdims=True)

        u3 = saved(3) * inv[3] ** 3
        e32 = inner(2, u3)
        v = lift(2, u3)
        e31 = inner(1, v)
        v = lift(1, v)
        e30 = inner(0, v)
        u2 = saved(2) * inv[2] ** 3
        e21 = inner(1, u2)
        e20 = inner(0, lift(1, u2))
        e10 = inner(0, saved(1) * inv[1] ** 3)
        return inv, lift, inner, [e32, e31, e30, e21, e20, e10]

    def teacher_ready():
        pairs = ((other, xh, 4, mate), (core, 1 - xh, 7, partner), (other, 1 - xh, 8, partner_mate))
        for s, hh, i, peer in pairs:
            slot = tea.at[s, hh]
            remote(slot, slot, ms_sem.at[i], mr_sem.at[i], peer).wait_recv()
        slot = tgt.at[1 - xh]
        remote(slot, slot, ms_sem.at[6], mr_sem.at[6], partner).wait_recv()
        values = [tea[s].reshape(2 * tok, cols).astype(F32) for s in (0, 1)]
        top = jnp.max(jnp.maximum(values[0], values[1]), axis=1, keepdims=True)
        total = jnp.zeros((2 * tok, 1), F32)
        for s in (0, 1):
            value = jnp.exp(values[s] - top)
            texp[s] = value
            total += jnp.sum(value, axis=1, keepdims=True)
        return top, total

    partner_wait(1)
    for way in (0, 1):
        ring_send(way, 3)
    for i in range(4, ring_count):
        for way in (0, 1):
            ring_send(way, i)
        if i == 5:
            inv, lift, inner, cross_spans = span_ready()
    teacher_top, teacher_total = teacher_ready()
    hidden_wait()
    multiply(0, first=True)
    for i in range(ring_count - 4, ring_count):
        for way in (0, 1):
            ring_wait(way, i)
        if i == ring_count - 3:
            for d in range(1, half):
                multiply(-d)
                multiply(d)
    multiply(half)

    def target_column():
        parts = []
        for hh in (0, 1):
            row = jnp.where(core == 0, tgt[hh, 0:1, :], tgt[hh, 1:2, :])
            parts.append(jnp.broadcast_to(row, (128, tok)).T[:, 0:1])
        return jnp.concatenate(parts, axis=0)

    wanted = target_column()

    def hit(s):
        start = (s * nv + voc) * 2 * cols + xh * cols
        return wanted - start == lax.broadcasted_iota(jnp.int32, (2 * tok, cols), 1)

    student_top = jnp.max(jnp.maximum(logits[0], logits[1]), axis=1, keepdims=True)
    student_total = jnp.zeros((2 * tok, 1), F32)
    cross = jnp.zeros((2 * tok, 1), F32)
    target_logit = jnp.zeros((2 * tok, 1), F32)
    for s in (0, 1):
        value = logits[s]
        cross += jnp.sum(texp[s] * (tea[s].reshape(2 * tok, cols).astype(F32) - value), axis=1, keepdims=True)
        target_logit += jnp.sum(jnp.where(hit(s), value, 0.0), axis=1, keepdims=True)
        value = jnp.exp(value - student_top)
        logits[s] = value
        student_total += jnp.sum(value, axis=1, keepdims=True)
    stats[me] = to_rows([student_top, student_total, teacher_top, teacher_total, cross, target_logit], 8)

    def stats_send(i, carry):
        peer = plane_peer((me + i) % plane)
        remote(stats.at[me], stats.at[me], sts_sem.at[i], str_sem.at[i], peer).start()
        return carry

    def stats_wait(i, carry):
        src = (me + plane - i) % plane
        remote(stats.at[src], stats.at[src], sts_sem.at[i], str_sem.at[i], mate).wait_recv()
        remote(stats.at[me], stats.at[me], sts_sem.at[i], str_sem.at[i], mate).wait_send()
        return carry

    lax.fori_loop(1, plane, stats_send, 0)
    lax.fori_loop(1, plane, stats_wait, 0)
    top_s, top_t = stats[0, 0:1, :], stats[0, 2:3, :]
    for i in range(1, plane):
        top_s = jnp.maximum(top_s, stats[i, 0:1, :])
        top_t = jnp.maximum(top_t, stats[i, 2:3, :])
    sum_s, sum_t, sum_x, sum_l = (jnp.zeros_like(top_s) for _ in range(4))
    for i in range(plane):
        part = stats[i]
        sum_s += part[1:2] * jnp.exp(part[0:1] - top_s)
        factor = jnp.exp(part[2:3] - top_t)
        sum_t += part[3:4] * factor
        sum_x += part[4:5] * factor
        sum_l += part[5:6]
    lse_s = top_s + jnp.log(sum_s)
    lse_t = top_t + jnp.log(sum_t)
    terms = sum_x / sum_t - lse_t + lse_s + CE_WEIGHT * (lse_s - sum_l)
    scales = to_columns(jnp.concatenate([lse_s, lse_t], axis=0))
    student_scale = jnp.exp(student_top - scales[:, 0:1])
    teacher_scale = jnp.exp(teacher_top - scales[:, 1:2])

    loss_peers = [mate] + far
    lsend[0] = jnp.broadcast_to(jnp.sum(terms, axis=1, keepdims=True), (8, 128))

    def loss_send(level):
        begin(remote(lsend.at[level], lrecv.at[level], ls_sem.at[level], lr_sem.at[level], loss_peers[level]))

    def loss_wait(level):
        slot = lrecv.at[level]
        remote(slot, slot, ls_sem.at[level], lr_sem.at[level], mate).wait_recv()
        return lsend[level] + lrecv[level]

    loss_send(0)

    for s in (0, 1):
        value = (1.0 + CE_WEIGHT) * (logits[s] * student_scale) - texp[s] * teacher_scale
        value = value - jnp.where(hit(s), CE_WEIGHT, 0.0)
        dlog[s] = (LOSS_SCALE * value).astype(BF16)

    half_tok = tok // 2
    ny = nv // 2
    xi, yi = xh * 2 + xl, voc // 2
    nt = (((1,), (1,)), ((), ()))

    def in_plane(x, y):
        return at(core, z, x // 2, y * 2 + x % 2)

    def slice_turn(i, carry):
        oy = (i // 2 + 1) % ny
        y = (yi + oy) % ny
        lo = (xl + 1 + i) % 2
        v = y * 2 + lo
        span = pl.ds(pl.multiple_of(v * slice_width, slice_width), slice_width)
        part = lax.dot_general(dlog[0], wbuf[0, span, :], nt, preferred_element_type=F32)
        part += lax.dot_general(dlog[1], wbuf[1, span, :], nt, preferred_element_type=F32)
        part = part.astype(BF16)
        for hh in (0, 1):
            x = hh * 2 + lo
            ox = (x - xi + 4) % 4
            snd_x[x, y] = part[hh * tok : hh * tok + half_tok]
            snd_y[y, x] = part[hh * tok + half_tok : (hh + 1) * tok]

            @pl.when(ox != 0)
            def _():
                remote(
                    snd_x.at[x, y], rcv_x.at[xi, y], xs_sem.at[ox, oy], xr_sem.at[ox, oy], in_plane(x, yi)
                ).start()

            @pl.when(oy != 0)
            def _():
                remote(
                    snd_y.at[y, x], rcv_y.at[yi, x], ys_sem.at[oy, ox], yr_sem.at[oy, ox], in_plane(xi, y)
                ).start()

        return carry

    lax.fori_loop(0, nv, slice_turn, 0)
    if len(loss_peers) > 1:
        lsend[1] = loss_wait(0)
        loss_send(1)

    def sum_x(oy):
        y = (yi + oy) % ny
        total = snd_x[xi, y].astype(F32)
        for ox in range(1, 4):
            slot = rcv_x.at[(xi + 4 - ox) % 4, y]
            remote(slot, slot, xs_sem.at[ox, oy], xr_sem.at[ox, oy], mate).wait_recv()
            total = total + slot[...].astype(F32)
        return total

    def sum_y(ox):
        x = (xi + ox) % 4
        total = snd_y[yi, x].astype(F32)
        for oy in range(1, ny):
            slot = rcv_y.at[(yi + ny - oy) % ny, x]
            remote(slot, slot, ys_sem.at[oy, ox], yr_sem.at[oy, ox], mate).wait_recv()
            total = total + slot[...].astype(F32)
        return total

    for oy in range(1, ny):
        two_y[oy] = sum_x(oy).astype(BF16)
        begin(remote(two_y.at[oy], end_y.at[oy], eys_sem.at[oy], eyr_sem.at[oy], in_plane(xi, (yi + oy) % ny)))
    for ox in range(1, 4):
        two_x[ox] = sum_y(ox).astype(BF16)
        begin(remote(two_x.at[ox], end_x.at[ox], exs_sem.at[ox], exr_sem.at[ox], in_plane((xi + ox) % 4, yi)))
    first_half, second_half = sum_x(0), sum_y(0)
    for oy in range(1, ny):
        remote(end_y.at[oy], end_y.at[oy], eys_sem.at[oy], eyr_sem.at[oy], mate).wait_recv()
        first_half = first_half + end_y[oy].astype(F32)
    for ox in range(1, 4):
        remote(end_x.at[ox], end_x.at[ox], exs_sem.at[ox], exr_sem.at[ox], mate).wait_recv()
        second_half = second_half + end_x[ox].astype(F32)
    cotangent = jnp.concatenate([first_half.astype(BF16), second_half.astype(BF16)], axis=0)

    def slice_sent(i, carry):
        oy, ox = i // 4, i % 4

        @pl.when(ox != 0)
        def _():
            x, y = (xi + ox) % 4, (yi + oy) % ny
            remote(snd_x.at[x, y], rcv_x.at[xi, y], xs_sem.at[ox, oy], xr_sem.at[ox, oy], mate).wait_send()

        @pl.when(oy != 0)
        def _():
            x, y = (xi + ox) % 4, (yi + oy) % ny
            remote(snd_y.at[y, x], rcv_y.at[yi, x], ys_sem.at[oy, ox], yr_sem.at[oy, ox], mate).wait_send()

        return carry

    lax.fori_loop(0, 4 * ny, slice_sent, 0)

    value = cotangent.astype(F32)
    products = [inner(3, value)]
    for c in (3, 2, 1):
        value = lift(c, value)
        products.append(inner(c - 1, value))
    dots[voc] = to_rows(products + cross_spans, 16)
    exchange(dots, dos_sem, dor_sem)
    for level in range(2, len(loss_peers)):
        lsend[level] = loss_wait(level - 1)
        loss_send(level)
    loss_total = loss_wait(len(loss_peers) - 1)
    loss_ref[0, 0] = jnp.max(loss_total) / (4 * tok * nz)
    found = to_columns(exchange_wait(dots, dos_sem, dor_sem)) / width
    d3, d2, d1, d0, e32, e31, e30, e21, e20, e10 = (found[:, i : i + 1] for i in range(10))
    s3 = d3
    s2 = d2 - s3 * e32
    s1 = d1 - s3 * e31 - s2 * e21
    s0 = d0 - s3 * e30 - s2 * e20 - s1 * e10
    value = cotangent.astype(F32)

    def hand_out(slot_index):
        pltpu.make_async_copy(ys.at[core, slot_index], out.at[0, slot_index, core], loc_sem.at[slot_index]).start()
        begin(
            remote(
                ys.at[other, slot_index], out.at[0, slot_index, core], os_sem.at[slot_index], or_sem.at[slot_index], mate
            )
        )

    for c, stat in ((3, s3), (2, s2), (1, s1), (0, s0)):
        fresh = (lift(c, value) - saved(c) * (inv[c] ** 3 * stat)).astype(BF16)
        ys[SPAN_AT[c]] = fresh
        value = fresh.astype(F32)
        if c == 2:
            hand_out(1)
    hand_out(0)

    for slot_index in (1, 0):
        pltpu.make_async_copy(
            ys.at[core, slot_index], out.at[0, slot_index, core], loc_sem.at[slot_index]
        ).wait()
        slot = out.at[0, slot_index, other]
        remote(slot, slot, os_sem.at[slot_index], or_sem.at[slot_index], mate).wait_recv()
    for copies in ring_copies:
        for copy in copies[-2:]:
            copy.wait_send()
    for copy in sent:
        copy.wait_send()


def solution(mesh):
    n_seq, n_voc = mesh.shape["seq"], mesh.shape["vocab"]
    nz = n_seq // 2

    def per_device(hidden, head_weight, teacher_logits, targets, span_inputs, span_gains, span_weights):
        _, tok, width = hidden.shape
        rows, shard = head_weight.shape
        cols = shard // 2
        slice_width = span_inputs.shape[4]
        heads = span_weights.shape[2]
        plane = 2 * n_voc
        levels = 1 + (nz.bit_length() - 1)
        half = nz // 2
        dma = pltpu.SemaphoreType.DMA
        any_space = pl.BlockSpec(memory_space=pltpu.HBM)
        grads, loss = pl.pallas_call(
            functools.partial(kernel, nz, n_voc),
            out_shape=(
                jax.ShapeDtypeStruct((1, 2, 2, tok, slice_width), BF16),
                jax.ShapeDtypeStruct((1, 1), F32),
            ),
            in_specs=[any_space] * 7,
            out_specs=(any_space, pl.BlockSpec(memory_space=pltpu.SMEM)),
            scratch_shapes=[
                pltpu.VMEM((2, width, cols), BF16),
                pltpu.VMEM((2, tok, width), BF16),
                pltpu.VMEM((2, 2, tok, cols), BF16),
                pltpu.VMEM((2, 2, tok), jnp.int32),
                pltpu.VMEM((2, 2 * tok, cols), F32),
                pltpu.VMEM((2, 2 * tok, cols), F32),
                pltpu.VMEM((2, 2 * tok, cols), BF16),
                pltpu.VMEM((plane, 8, 2 * tok), F32),
                pltpu.VMEM((4, n_voc // 2, tok // 2, slice_width), BF16),
                pltpu.VMEM((4, n_voc // 2, tok // 2, slice_width), BF16),
                pltpu.VMEM((n_voc // 2, 4, tok // 2, slice_width), BF16),
                pltpu.VMEM((n_voc // 2, 4, tok // 2, slice_width), BF16),
                pltpu.VMEM((4, tok // 2, slice_width), BF16),
                pltpu.VMEM((4, tok // 2, slice_width), BF16),
                pltpu.VMEM((n_voc // 2, tok // 2, slice_width), BF16),
                pltpu.VMEM((n_voc // 2, tok // 2, slice_width), BF16),
                pltpu.VMEM((2, 2, tok, slice_width), BF16),
                pltpu.VMEM((2, 2, slice_width), F32),
                pltpu.VMEM((2, 2, heads, HEAD, HEAD), BF16),
                pltpu.VMEM((4, tok, slice_width), F32),
                pltpu.VMEM((n_voc, 8, tok), F32),
                pltpu.VMEM((n_voc, 16, tok), F32),
                pltpu.VMEM((levels, 8, 128), F32),
                pltpu.VMEM((levels, 8, 128), F32),
                pltpu.VMEM((2, 2, tok, slice_width), BF16),
                dma((7,)),
                dma((2, 4 * half - 2)),
                dma((2, 4 * half - 2)),
                dma((4 * nz,)),
                dma((4 * nz,)),
                dma((10,)),
                dma((10,)),
                dma((plane,)),
                dma((plane,)),
                dma((4, n_voc // 2)),
                dma((4, n_voc // 2)),
                dma((n_voc // 2, 4)),
                dma((n_voc // 2, 4)),
                dma((4,)),
                dma((4,)),
                dma((n_voc // 2,)),
                dma((n_voc // 2,)),
                dma((n_voc,)),
                dma((n_voc,)),
                dma((n_voc,)),
                dma((n_voc,)),
                dma((levels,)),
                dma((levels,)),
                dma((2,)),
                dma((2,)),
            ],
            compiler_params=pltpu.CompilerParams(
                collective_id=0, has_side_effects=True, vmem_limit_bytes=60 * 1024 * 1024
            ),
        )(hidden, head_weight, teacher_logits, targets, span_inputs, span_gains, span_weights)
        return grads, loss.reshape(())

    placed = (
        P(None, "seq", None),
        P("seq", ("section", "vocab")),
        P(None, "seq", ("section", "vocab")),
        P(None, "seq"),
        P("section", None, None, "seq", "vocab"),
        P("section", None, "vocab"),
        P("section", None, "vocab", None, None),
    )
    return jax.shard_map(
        per_device,
        mesh=mesh,
        in_specs=placed,
        out_specs=(P("section", None, None, "seq", "vocab"), P()),
        check_vma=False,
    )
```

```python
import functools

import jax
import jax.numpy as jnp
from jax import lax
from jax.experimental import pallas as pl
from jax.experimental.pallas import tpu as pltpu
from jax.sharding import PartitionSpec as P

MESH = pl.DeviceIdType.MESH
F32 = jnp.float32
BF16 = jnp.bfloat16
LOSS_SCALE = 16
CE_WEIGHT = 0.5
EPS = 1e-06
HEAD = 128
SPAN_AT = ((0, 0), (1, 0), (1, 1), (0, 1))


def to_rows(columns, height):
    count = columns[0].shape[0]
    lane = lax.broadcasted_iota(jnp.int32, (count, 128), 1)
    wide = jnp.zeros((count, 128), F32)
    for i, column in enumerate(columns):
        wide = jnp.where(lane == i, column, wide)
    return wide.T[:height]


def to_columns(rows):
    height, count = rows.shape
    return jnp.concatenate([rows, jnp.zeros((128 - height, count), F32)], axis=0).T


def heads_dot(left, weights, transposed):
    dims = (((1,), (1,)), ((), ())) if transposed else (((1,), (0,)), ((), ()))
    parts = []
    for h in range(weights.shape[0]):
        parts.append(
            lax.dot_general(left[:, h * HEAD : (h + 1) * HEAD], weights[h], dims, preferred_element_type=F32)
        )
    return jnp.concatenate(parts, axis=1)


def kernel(
    nz, nv,
    hidden, head, teacher, targets, xin, gains, wspan,
    out, loss_ref,
    wbuf, hid, tea, tgt, logits, texp, dlog, stats, snd_x, rcv_x, snd_y, rcv_y, two_x, end_x, two_y, end_y, xs, gs, ws,
    sq, dots, vec_y, vec_x, told, heard, own_loss, losses, ys,
    loc_sem, zs_sem, zr_sem, ds_sem, dr_sem, ms_sem, mr_sem, sts_sem, str_sem, xs_sem, xr_sem, ys_sem, yr_sem,
    exs_sem, exr_sem, eys_sem, eyr_sem,    sqs_sem, sqr_sem, dos_sem, dor_sem, los_sem, lor_sem, vys_sem, vyr_sem, vxs_sem, vxr_sem, tos_sem, tor_sem, os_sem, or_sem,
):
    core = lax.axis_index("section")
    seq = lax.axis_index("seq")
    voc = lax.axis_index("vocab")
    z, xh = seq // 2, seq % 2
    xl = voc % 2
    other = 1 - core
    half = nz // 2
    tok, width = hid.shape[1], hid.shape[2]
    rows, cols = head.shape[0], wbuf.shape[2]
    slice_width = xs.shape[3]
    plane = 2 * nv
    me = xh * nv + voc
    half_tok = tok // 2
    ny = nv // 2
    xi, yi = xh * 2 + xl, voc // 2

    def at(c, zz, hh, v):
        return (c, zz * 2 + hh, v)

    def plane_peer(index):
        return at(core, z, index // nv, index % nv)

    def in_plane(x, y):
        return at(core, z, x // 2, y * 2 + x % 2)

    mate = at(other, z, xh, voc)
    partner = at(core, z, 1 - xh, voc)
    partner_mate = at(other, z, 1 - xh, voc)
    near = at(core, z, 1 - xh, voc + 1 - 2 * xl)
    right = at(core, (z + 1) % nz, xh, voc)
    left = at(core, (z + nz - 1) % nz, xh, voc)
    barrier = pltpu.get_barrier_semaphore()
    direct = [mate, partner_mate, right, left]
    for peer in direct:
        pl.semaphore_signal(barrier, inc=1, device_id=peer, device_id_type=MESH)

    def greet(i, carry):
        pl.semaphore_signal(barrier, inc=1, device_id=plane_peer((me + i) % plane), device_id_type=MESH)
        return carry

    lax.fori_loop(1, plane, greet, 0)
    pl.semaphore_wait(barrier, len(direct) + plane - 1)

    def remote(src, dst, send, recv, peer):
        return pltpu.make_async_remote_copy(
            src_ref=src, dst_ref=dst, send_sem=send, recv_sem=recv, device_id=peer, device_id_type=MESH
        )

    sent = []

    def begin(copy):
        copy.start()
        sent.append(copy)

    part_rows = rows // 2

    def part_at(section, delta, part):
        zz = lax.rem(z + delta + nz, nz)
        hh = xh if part < 2 else 1 - xh
        start = (zz * 2 + hh) * rows + (part % 2) * part_rows
        return wbuf.at[section, pl.ds(pl.multiple_of(start, part_rows), part_rows), :]

    def own_columns(hh):
        return pl.ds(pl.multiple_of(hh * cols, cols), cols)

    own_block = head.at[:, own_columns(xh)]

    def own_part(part, hh):
        return head.at[pl.ds(part * part_rows, part_rows), own_columns(hh)]

    ring_parts = [
        [(k, part) for k in range(1, half) for part in range(4)] + [(half, 2 * way), (half, 2 * way + 1)]
        for way in (0, 1)
    ]
    ring_count = len(ring_parts[0])
    ring_copies = [[], []]

    def ring_send(way, i):
        k, part = ring_parts[way][i]
        slot = part_at(core, -(k - 1) if way == 0 else k - 1, part)
        src = own_part(part, xh) if k == 1 and part < 2 else slot
        if k > 1:
            ring_wait(way, ring_parts[way].index((k - 1, part)))
        if i >= 2:
            ring_copies[way][i - 2].wait_send()
        copy = remote(src, slot, zs_sem.at[way, i], zr_sem.at[way, i], right if way == 0 else left)
        copy.start()
        ring_copies[way].append(copy)

    arrived = [0, 0]

    def ring_wait(way, i):
        while arrived[way] <= i:
            j = arrived[way]
            k, part = ring_parts[way][j]
            delta = -k if way == 0 else k
            slot = part_at(core, delta, part)
            remote(slot, slot, zs_sem.at[way, j], zr_sem.at[way, j], right).wait_recv()
            mate_send(delta, part)
            arrived[way] += 1

    def mate_send(delta, part):
        slot = part_at(core, delta, part)
        src = own_part(part, xh) if delta == 0 and part < 2 else slot
        i = (delta % nz) * 4 + part
        begin(remote(src, slot, ds_sem.at[i], dr_sem.at[i], mate))

    def mate_wait(delta, part):
        slot = part_at(other, delta, part)
        i = (delta % nz) * 4 + part
        remote(slot, slot, ds_sem.at[i], dr_sem.at[i], mate).wait_recv()

    def partner_send(part):
        slot = part_at(core, 0, part)
        copy = remote(own_part(part, 1 - xh), slot, ms_sem.at[9 * part], mr_sem.at[9 * part], partner)
        copy.start()
        return copy

    def partner_wait(part):
        slot = part_at(core, 0, part + 2)
        remote(slot, slot, ms_sem.at[9 * part], mr_sem.at[9 * part], partner).wait_recv()
        mate_send(0, part + 2)

    my_rows = wbuf.at[core, pl.ds(pl.multiple_of(seq * rows, rows), rows), :]
    first = partner_send(0)
    for i in (0, 1):
        for way in (0, 1):
            ring_send(way, i)
        mate_send(0, i)

    local = [
        pltpu.make_async_copy(own_block, my_rows, loc_sem.at[0]),
        pltpu.make_async_copy(xin.at[0, :, core], xs.at[core], loc_sem.at[1]),
        pltpu.make_async_copy(gains.at[0], gs.at[core], loc_sem.at[2]),
        pltpu.make_async_copy(wspan.at[0], ws.at[core], loc_sem.at[3]),
        pltpu.make_async_copy(hidden.at[core], hid.at[xh], loc_sem.at[4]),
        pltpu.make_async_copy(teacher.at[core, :, own_columns(xh)], tea.at[core, xh], loc_sem.at[5]),
        pltpu.make_async_copy(targets, tgt.at[xh], loc_sem.at[6]),
    ]
    for copy in local:
        copy.start()
    begin(remote(xin.at[0, :, other], xs.at[core], ms_sem.at[1], mr_sem.at[1], mate))
    begin(remote(gains.at[0], gs.at[core], ms_sem.at[2], mr_sem.at[2], mate))
    begin(remote(wspan.at[0], ws.at[core], ms_sem.at[3], mr_sem.at[3], mate))
    begin(remote(teacher.at[other, :, own_columns(xh)], tea.at[core, xh], ms_sem.at[4], mr_sem.at[4], mate))

    first.wait_send()
    second = partner_send(1)
    partner_wait(0)
    for way in (0, 1):
        ring_send(way, 2)
    second.wait_send()
    begin(remote(hidden.at[core], hid.at[xh], ms_sem.at[5], mr_sem.at[5], near))
    begin(remote(targets, tgt.at[xh], ms_sem.at[6], mr_sem.at[6], partner))
    begin(remote(teacher.at[core, :, own_columns(1 - xh)], tea.at[core, xh], ms_sem.at[7], mr_sem.at[7], partner))
    begin(
        remote(teacher.at[other, :, own_columns(1 - xh)], tea.at[core, xh], ms_sem.at[8], mr_sem.at[8], partner_mate)
    )

    for copy in local:
        copy.wait()
    remote(xs.at[other], xs.at[other], ms_sem.at[1], mr_sem.at[1], mate).wait_recv()
    remote(gs.at[other], gs.at[other], ms_sem.at[2], mr_sem.at[2], mate).wait_recv()
    remote(ws.at[other], ws.at[other], ms_sem.at[3], mr_sem.at[3], mate).wait_recv()

    def saved(c):
        return xs[SPAN_AT[c]].astype(F32)

    def gain(c):
        section, slot_index = SPAN_AT[c]
        return gs[section, slot_index : slot_index + 1, :]

    def exchange(buf, send_sems, recv_sems):
        def send(i, carry):
            peer = at(core, z, xh, (voc + i) % nv)
            remote(buf.at[voc], buf.at[voc], send_sems.at[i], recv_sems.at[i], peer).start()
            return carry

        lax.fori_loop(1, nv, send, 0)

    def exchange_wait(buf, send_sems, recv_sems):
        def wait(i, carry):
            src = (voc + nv - i) % nv
            remote(buf.at[src], buf.at[src], send_sems.at[i], recv_sems.at[i], mate).wait_recv()
            remote(buf.at[voc], buf.at[voc], send_sems.at[i], recv_sems.at[i], mate).wait_send()
            return carry

        lax.fori_loop(1, nv, wait, 0)
        total = buf[0]
        for i in range(1, nv):
            total = total + buf[i]
        return total

    squares = []
    for c in range(4):
        value = saved(c)
        squares.append(jnp.sum(value * value, axis=1, keepdims=True))
    sq[voc] = to_rows(squares, 8)
    exchange(sq, sqs_sem, sqr_sem)
    def multiply(delta, first=False):
        for part in range(4):
            mate_wait(delta, part)
        zz = lax.rem(z + delta + nz, nz)
        span = pl.ds(pl.multiple_of(zz * 2 * rows, 2 * rows), 2 * rows)
        left_part = hid[:, :, span].reshape(2 * tok, 2 * rows)
        for s in (0, 1):
            product = jnp.dot(left_part, wbuf[s, span, :], preferred_element_type=F32)
            if first:
                logits[s] = product
            else:
                logits[s] += product

    def hidden_wait():
        slot = hid.at[1 - xh]
        remote(slot, slot, ms_sem.at[5], mr_sem.at[5], near).wait_recv()

    def span_ready():
        inv_rows = lax.rsqrt(exchange_wait(sq, sqs_sem, sqr_sem) / width + EPS)
        total = to_columns(inv_rows)
        inv = [total[:, c : c + 1] for c in range(4)]

        def back(c, value):
            return value + inv[c] * heads_dot((value * gain(c)).astype(BF16), ws[SPAN_AT[c]], False)

        def inner(c, value):
            return jnp.sum(saved(c) * inv[c] ** 3 * value, axis=1, keepdims=True)

        products = []
        for c in range(4):
            value = heads_dot((saved(c) * gain(c)).astype(BF16), ws[SPAN_AT[c]], False)
            for upper in range(c + 1, 4):
                products.append(inner(upper, value))
                value = back(upper, value)
            vec_y[yi, c] = value[:half_tok].astype(BF16)
            vec_x[xi, c] = value[half_tok:].astype(BF16)
        dots[voc] = to_rows(products, 8)
        exchange(dots, dos_sem, dor_sem)
        return inv, inv_rows

    def vectors_send():
        for oy in range(1, ny):
            begin(remote(vec_y.at[yi], vec_y.at[yi], vys_sem.at[oy], vyr_sem.at[oy], in_plane(xi, (yi + oy) % ny)))
        for ox in range(1, 4):
            begin(remote(vec_x.at[xi], vec_x.at[xi], vxs_sem.at[ox], vxr_sem.at[ox], in_plane((xi + ox) % 4, yi)))

    def vectors_wait():
        for oy in range(1, ny):
            slot = vec_y.at[(yi + ny - oy) % ny]
            remote(slot, slot, vys_sem.at[oy], vyr_sem.at[oy], mate).wait_recv()
        for ox in range(1, 4):
            slot = vec_x.at[(xi + 4 - ox) % 4]
            remote(slot, slot, vxs_sem.at[ox], vxr_sem.at[ox], mate).wait_recv()

    def teacher_ready():
        pairs = ((other, xh, 4, mate), (core, 1 - xh, 7, partner), (other, 1 - xh, 8, partner_mate))
        for s, hh, i, peer in pairs:
            slot = tea.at[s, hh]
            remote(slot, slot, ms_sem.at[i], mr_sem.at[i], peer).wait_recv()
        slot = tgt.at[1 - xh]
        remote(slot, slot, ms_sem.at[6], mr_sem.at[6], partner).wait_recv()
        values = [tea[s].reshape(2 * tok, cols).astype(F32) for s in (0, 1)]
        top = jnp.max(jnp.maximum(values[0], values[1]), axis=1, keepdims=True)
        total = jnp.zeros((2 * tok, 1), F32)
        for s in (0, 1):
            value = jnp.exp(values[s] - top)
            texp[s] = value
            total += jnp.sum(value, axis=1, keepdims=True)
        return top, total

    partner_wait(1)
    for way in (0, 1):
        ring_send(way, 3)
    for i in range(4, ring_count):
        for way in (0, 1):
            ring_send(way, i)
        if i == 5:
            inv, inv_rows = span_ready()
    teacher_top, teacher_total = teacher_ready()
    hidden_wait()
    vectors_send()
    multiply(0, first=True)
    for i in range(ring_count - 4, ring_count):
        for way in (0, 1):
            ring_wait(way, i)
        if i == ring_count - 3:
            for d in range(1, half):
                multiply(-d)
                multiply(d)
    multiply(half)
    cross_rows = exchange_wait(dots, dos_sem, dor_sem)
    vectors_wait()

    def target_column():
        parts = []
        for hh in (0, 1):
            row = jnp.where(core == 0, tgt[hh, 0:1, :], tgt[hh, 1:2, :])
            parts.append(jnp.broadcast_to(row, (128, tok)).T[:, 0:1])
        return jnp.concatenate(parts, axis=0)

    wanted = target_column()

    def hit(s):
        start = (s * nv + voc) * 2 * cols + xh * cols
        return wanted - start == lax.broadcasted_iota(jnp.int32, (2 * tok, cols), 1)

    student_top = jnp.max(jnp.maximum(logits[0], logits[1]), axis=1, keepdims=True)
    student_total = jnp.zeros((2 * tok, 1), F32)
    cross = jnp.zeros((2 * tok, 1), F32)
    target_logit = jnp.zeros((2 * tok, 1), F32)
    for s in (0, 1):
        value = logits[s]
        cross += jnp.sum(texp[s] * (tea[s].reshape(2 * tok, cols).astype(F32) - value), axis=1, keepdims=True)
        target_logit += jnp.sum(jnp.where(hit(s), value, 0.0), axis=1, keepdims=True)
        value = jnp.exp(value - student_top)
        logits[s] = value
        student_total += jnp.sum(value, axis=1, keepdims=True)
    stats[me] = to_rows([student_top, student_total, teacher_top, teacher_total, cross, target_logit], 8)

    def stats_send(i, carry):
        peer = plane_peer((me + i) % plane)
        remote(stats.at[me], stats.at[me], sts_sem.at[i], str_sem.at[i], peer).start()
        return carry

    def stats_wait(i, carry):
        src = (me + plane - i) % plane
        remote(stats.at[src], stats.at[src], sts_sem.at[i], str_sem.at[i], mate).wait_recv()
        remote(stats.at[me], stats.at[me], sts_sem.at[i], str_sem.at[i], mate).wait_send()
        return carry

    lax.fori_loop(1, plane, stats_send, 0)
    lax.fori_loop(1, plane, stats_wait, 0)
    top_s, top_t = stats[0, 0:1, :], stats[0, 2:3, :]
    for i in range(1, plane):
        top_s = jnp.maximum(top_s, stats[i, 0:1, :])
        top_t = jnp.maximum(top_t, stats[i, 2:3, :])
    sum_s, sum_t, sum_x, sum_l = (jnp.zeros_like(top_s) for _ in range(4))
    for i in range(plane):
        part = stats[i]
        sum_s += part[1:2] * jnp.exp(part[0:1] - top_s)
        factor = jnp.exp(part[2:3] - top_t)
        sum_t += part[3:4] * factor
        sum_x += part[4:5] * factor
        sum_l += part[5:6]
    lse_s = top_s + jnp.log(sum_s)
    lse_t = top_t + jnp.log(sum_t)
    terms = sum_x / sum_t - lse_t + lse_s + CE_WEIGHT * (lse_s - sum_l)
    scales = to_columns(jnp.concatenate([lse_s, lse_t], axis=0))
    student_scale = jnp.exp(student_top - scales[:, 0:1])
    teacher_scale = jnp.exp(teacher_top - scales[:, 1:2])

    own_loss[0] = jnp.broadcast_to(jnp.sum(terms, axis=1, keepdims=True), (8, 128))
    begin(remote(own_loss.at[0], own_loss.at[1], los_sem.at[0, 0], lor_sem.at[0, 0], mate))

    def loss_start():
        remote(own_loss.at[1], own_loss.at[1], los_sem.at[0, 0], lor_sem.at[0, 0], mate).wait_recv()
        losses[z] = own_loss[0] + own_loss[1]
        loss_send(1)

    def loss_send(k):
        for way, peer in ((0, right), (1, left)):
            if k < half or way == 0:
                slot = losses.at[(z + nz - (k - 1)) % nz if way == 0 else (z + k - 1) % nz]
                begin(remote(slot, slot, los_sem.at[way, k], lor_sem.at[way, k], peer))

    def loss_wait(k):
        for way in (0, 1):
            if k < half or way == 0:
                slot = losses.at[(z + nz - k) % nz if way == 0 else (z + k) % nz]
                remote(slot, slot, los_sem.at[way, k], lor_sem.at[way, k], right).wait_recv()
        if k < half:
            loss_send(k + 1)

    for s in (0, 1):
        value = (1.0 + CE_WEIGHT) * (logits[s] * student_scale) - texp[s] * teacher_scale
        value = value - jnp.where(hit(s), CE_WEIGHT, 0.0)
        dlog[s] = (LOSS_SCALE * value).astype(BF16)

    nt = (((1,), (1,)), ((), ()))

    def slice_turn(i, carry):
        oy = (i // 2 + 1) % ny
        y = (yi + oy) % ny
        lo = (xl + 1 + i) % 2
        v = y * 2 + lo
        span = pl.ds(pl.multiple_of(v * slice_width, slice_width), slice_width)
        part = lax.dot_general(dlog[0], wbuf[0, span, :], nt, preferred_element_type=F32)
        part += lax.dot_general(dlog[1], wbuf[1, span, :], nt, preferred_element_type=F32)
        part = part.astype(BF16)
        for hh in (0, 1):
            x = hh * 2 + lo
            ox = (x - xi + 4) % 4
            snd_x[x, y] = part[hh * tok : hh * tok + half_tok]
            snd_y[y, x] = part[hh * tok + half_tok : (hh + 1) * tok]

            @pl.when(ox != 0)
            def _():
                remote(
                    snd_x.at[x, y], rcv_x.at[xi, y], xs_sem.at[ox, oy], xr_sem.at[ox, oy], in_plane(x, yi)
                ).start()

            @pl.when(oy != 0)
            def _():
                remote(
                    snd_y.at[y, x], rcv_y.at[yi, x], ys_sem.at[oy, ox], yr_sem.at[oy, ox], in_plane(xi, y)
                ).start()

        return carry

    lax.fori_loop(0, nv, slice_turn, 0)
    loss_start()

    def sum_x(oy):
        y = (yi + oy) % ny
        total = snd_x[xi, y].astype(F32)
        for ox in range(1, 4):
            slot = rcv_x.at[(xi + 4 - ox) % 4, y]
            remote(slot, slot, xs_sem.at[ox, oy], xr_sem.at[ox, oy], mate).wait_recv()
            total = total + slot[...].astype(F32)
        return total

    def sum_y(ox):
        x = (xi + ox) % 4
        total = snd_y[yi, x].astype(F32)
        for oy in range(1, ny):
            slot = rcv_y.at[(yi + ny - oy) % ny, x]
            remote(slot, slot, ys_sem.at[oy, ox], yr_sem.at[oy, ox], mate).wait_recv()
            total = total + slot[...].astype(F32)
        return total

    def fold(value):
        parts = [value[:, i : i + 128] for i in range(0, slice_width, 128)]
        return functools.reduce(lambda a, b: a + b, parts)

    def products_with(vectors, value):
        return [fold(vectors[c].astype(F32) * value) for c in range(4)]

    def add(left_list, right_list):
        return [a + b for a, b in zip(left_list, right_list)]

    first_products = [jnp.zeros((half_tok, 128), F32)] * 4
    for oy in range(1, ny):
        value = sum_x(oy)
        two_y[oy] = value.astype(BF16)
        begin(remote(two_y.at[oy], end_y.at[oy], eys_sem.at[oy], eyr_sem.at[oy], in_plane(xi, (yi + oy) % ny)))
        first_products = add(first_products, products_with(vec_y[(yi + oy) % ny], value))
    loss_wait(1)
    first_half = sum_x(0)
    first_products = add(first_products, products_with(vec_y[yi], first_half))
    column_sums = {}
    for ox in range(1, 4):
        column_sums[ox] = sum_y(ox)
        two_x[ox] = column_sums[ox].astype(BF16)
        begin(remote(two_x.at[ox], end_x.at[ox], exs_sem.at[ox], exr_sem.at[ox], in_plane((xi + ox) % 4, yi)))
    second_half = sum_y(0)
    column_sums[0] = second_half
    near_products = [jnp.zeros((half_tok, 128), F32)] * 4
    away_products = near_products
    for ox in range(4):
        x = (xi + ox) % 4
        found = products_with(vec_x[x], column_sums[ox])
        same = x // 2 == xh
        near_products = [a + jnp.where(same, b, 0.0) for a, b in zip(near_products, found)]
        away_products = [a + jnp.where(same, 0.0, b) for a, b in zip(away_products, found)]

    def message(first_part, second_part):
        columns = [
            jnp.sum(jnp.concatenate([a, b], axis=0), axis=1, keepdims=True) for a, b in zip(first_part, second_part)
        ]
        return to_rows(columns, 8)

    away = message([jnp.zeros((half_tok, 128), F32)] * 4, away_products)
    close = message(first_products, near_products)
    told[0] = jnp.where(xh == 0, close, away)
    told[1] = jnp.where(xh == 0, away, close)

    def told_send(i, carry):
        to = (me + i) % plane
        remote(told.at[to // nv], heard.at[me], tos_sem.at[i], tor_sem.at[i], plane_peer(to)).start()
        return carry

    def told_wait(i, carry):
        src = (me + plane - i) % plane
        remote(heard.at[src], heard.at[src], tos_sem.at[i], tor_sem.at[i], mate).wait_recv()
        remote(told.at[0], heard.at[me], tos_sem.at[i], tor_sem.at[i], mate).wait_send()
        return carry

    lax.fori_loop(1, plane, told_send, 0)
    heard[me] = close

    def slice_sent(i, carry):
        oy, ox = i // 4, i % 4

        @pl.when(ox != 0)
        def _():
            x, y = (xi + ox) % 4, (yi + oy) % ny
            remote(snd_x.at[x, y], rcv_x.at[xi, y], xs_sem.at[ox, oy], xr_sem.at[ox, oy], mate).wait_send()

        @pl.when(oy != 0)
        def _():
            x, y = (xi + ox) % 4, (yi + oy) % ny
            remote(snd_y.at[y, x], rcv_y.at[yi, x], ys_sem.at[oy, ox], yr_sem.at[oy, ox], mate).wait_send()

        return carry

    lax.fori_loop(0, 4 * ny, slice_sent, 0)

    loss_wait(2)
    for copies in ring_copies:
        for copy in copies[-2:]:
            copy.wait_send()
    for copy in sent:
        copy.wait_send()
    sent.clear()
    for oy in range(1, ny):
        remote(end_y.at[oy], end_y.at[oy], eys_sem.at[oy], eyr_sem.at[oy], mate).wait_recv()
        first_half = first_half + end_y[oy].astype(F32)
    for ox in range(1, 4):
        remote(end_x.at[ox], end_x.at[ox], exs_sem.at[ox], exr_sem.at[ox], mate).wait_recv()
        second_half = second_half + end_x[ox].astype(F32)
    cotangent = jnp.concatenate([first_half.astype(BF16), second_half.astype(BF16)], axis=0)

    lax.fori_loop(1, plane, told_wait, 0)
    found = heard[0]
    for i in range(1, plane):
        found = found + heard[i]
    d0, d1, d2, d3 = (found[c : c + 1] / width for c in range(4))
    e10, e20, e30, e21, e31, e32 = (cross_rows[c : c + 1] / width for c in range(6))
    s3 = d3
    s2 = d2 - s3 * e32
    s1 = d1 - s3 * e31 - s2 * e21
    s0 = d0 - s3 * e30 - s2 * e20 - s1 * e10
    pull = to_columns(inv_rows[0:4] ** 3 * jnp.concatenate([s0, s1, s2, s3], axis=0))
    value = cotangent

    def hand_out(slot_index):
        pltpu.make_async_copy(ys.at[core, slot_index], out.at[0, slot_index, core], loc_sem.at[slot_index]).start()
        begin(
            remote(
                ys.at[other, slot_index], out.at[0, slot_index, core], os_sem.at[slot_index], or_sem.at[slot_index], mate
            )
        )

    for c in (3, 2, 1, 0):
        grad = heads_dot(value, ws[SPAN_AT[c]], True)
        fresh = value.astype(F32) + inv[c] * gain(c) * grad - saved(c) * pull[:, c : c + 1]
        value = fresh.astype(BF16)
        ys[SPAN_AT[c]] = value
        if c == 2:
            hand_out(1)
    hand_out(0)
    for k in range(3, half + 1):
        loss_wait(k)
    loss_total = losses[0]
    for i in range(1, nz):
        loss_total = loss_total + losses[i]
    loss_ref[0, 0] = jnp.max(loss_total) / (4 * tok * nz)
    for slot_index in (1, 0):
        pltpu.make_async_copy(
            ys.at[core, slot_index], out.at[0, slot_index, core], loc_sem.at[slot_index]
        ).wait()
        slot = out.at[0, slot_index, other]
        remote(slot, slot, os_sem.at[slot_index], or_sem.at[slot_index], mate).wait_recv()
    for copy in sent:
        copy.wait_send()


def solution(mesh):
    n_seq, n_voc = mesh.shape["seq"], mesh.shape["vocab"]
    nz = n_seq // 2

    def per_device(hidden, head_weight, teacher_logits, targets, span_inputs, span_gains, span_weights):
        _, tok, width = hidden.shape
        rows, shard = head_weight.shape
        cols = shard // 2
        slice_width = span_inputs.shape[4]
        heads = span_weights.shape[2]
        plane = 2 * n_voc
        half = nz // 2
        dma = pltpu.SemaphoreType.DMA
        any_space = pl.BlockSpec(memory_space=pl.ANY)
        operands = [
            pltpu.with_memory_space_constraint(a, pltpu.HBM)
            for a in (hidden, head_weight, teacher_logits, targets, span_inputs, span_gains, span_weights)
        ]
        grads, loss = pl.pallas_call(
            functools.partial(kernel, nz, n_voc),
            out_shape=(
                jax.ShapeDtypeStruct((1, 2, 2, tok, slice_width), BF16),
                jax.ShapeDtypeStruct((1, 1), F32),
            ),
            in_specs=[any_space] * 7,
            out_specs=(any_space, pl.BlockSpec(memory_space=pltpu.SMEM)),
            scratch_shapes=[
                pltpu.VMEM((2, width, cols), BF16),
                pltpu.VMEM((2, tok, width), BF16),
                pltpu.VMEM((2, 2, tok, cols), BF16),
                pltpu.VMEM((2, 2, tok), jnp.int32),
                pltpu.VMEM((2, 2 * tok, cols), F32),
                pltpu.VMEM((2, 2 * tok, cols), F32),
                pltpu.VMEM((2, 2 * tok, cols), BF16),
                pltpu.VMEM((plane, 8, 2 * tok), F32),
                pltpu.VMEM((4, n_voc // 2, tok // 2, slice_width), BF16),
                pltpu.VMEM((4, n_voc // 2, tok // 2, slice_width), BF16),
                pltpu.VMEM((n_voc // 2, 4, tok // 2, slice_width), BF16),
                pltpu.VMEM((n_voc // 2, 4, tok // 2, slice_width), BF16),
                pltpu.VMEM((4, tok // 2, slice_width), BF16),
                pltpu.VMEM((4, tok // 2, slice_width), BF16),
                pltpu.VMEM((n_voc // 2, tok // 2, slice_width), BF16),
                pltpu.VMEM((n_voc // 2, tok // 2, slice_width), BF16),
                pltpu.VMEM((2, 2, tok, slice_width), BF16),
                pltpu.VMEM((2, 2, slice_width), F32),
                pltpu.VMEM((2, 2, heads, HEAD, HEAD), BF16),
                pltpu.VMEM((n_voc, 8, tok), F32),
                pltpu.VMEM((n_voc, 8, tok), F32),
                pltpu.VMEM((n_voc // 2, 4, tok // 2, slice_width), BF16),
                pltpu.VMEM((4, 4, tok // 2, slice_width), BF16),
                pltpu.VMEM((2, 8, tok), F32),
                pltpu.VMEM((plane, 8, tok), F32),
                pltpu.VMEM((2, 8, 128), F32),
                pltpu.VMEM((nz, 8, 128), F32),
                pltpu.VMEM((2, 2, tok, slice_width), BF16),
                dma((7,)),
                dma((2, 4 * half - 2)),
                dma((2, 4 * half - 2)),
                dma((4 * nz,)),
                dma((4 * nz,)),
                dma((10,)),
                dma((10,)),
                dma((plane,)),
                dma((plane,)),
                dma((4, n_voc // 2)),
                dma((4, n_voc // 2)),
                dma((n_voc // 2, 4)),
                dma((n_voc // 2, 4)),
                dma((4,)),
                dma((4,)),
                dma((n_voc // 2,)),
                dma((n_voc // 2,)),
                dma((n_voc,)),
                dma((n_voc,)),
                dma((n_voc,)),
                dma((n_voc,)),
                dma((2, half + 1)),
                dma((2, half + 1)),
                dma((n_voc // 2,)),
                dma((n_voc // 2,)),
                dma((4,)),
                dma((4,)),
                dma((plane,)),
                dma((plane,)),
                dma((2,)),
                dma((2,)),
            ],
            compiler_params=pltpu.CompilerParams(
                collective_id=0, has_side_effects=True, vmem_limit_bytes=48 * 1024 * 1024
            ),
        )(*operands)
        return grads, loss.reshape(())

    placed = (
        P(None, "seq", None),
        P("seq", ("section", "vocab")),
        P(None, "seq", ("section", "vocab")),
        P(None, "seq"),
        P("section", None, None, "seq", "vocab"),
        P("section", None, "vocab"),
        P("section", None, "vocab", None, None),
    )
    return jax.shard_map(
        per_device,
        mesh=mesh,
        in_specs=placed,
        out_specs=(P("section", None, None, "seq", "vocab"), P()),
        check_vma=False,
    )
```

```python
import functools

import jax
import jax.numpy as jnp
from jax import lax
from jax.experimental import pallas as pl
from jax.experimental.pallas import tpu as pltpu
from jax.sharding import PartitionSpec as P

MESH = pl.DeviceIdType.MESH
F32 = jnp.float32
BF16 = jnp.bfloat16
LOSS_SCALE = 16
CE_WEIGHT = 0.5
EPS = 1e-06
HEAD = 128
SPAN_AT = ((0, 0), (1, 0), (1, 1), (0, 1))


def to_rows(columns, height):
    count = columns[0].shape[0]
    lane = lax.broadcasted_iota(jnp.int32, (count, 128), 1)
    wide = jnp.zeros((count, 128), F32)
    for i, column in enumerate(columns):
        wide = jnp.where(lane == i, column, wide)
    return wide.T[:height]


def to_columns(rows):
    height, count = rows.shape
    return jnp.concatenate([rows, jnp.zeros((128 - height, count), F32)], axis=0).T


def heads_dot(left, weights, transposed):
    dims = (((1,), (1,)), ((), ())) if transposed else (((1,), (0,)), ((), ()))
    parts = []
    for h in range(weights.shape[0]):
        parts.append(
            lax.dot_general(left[:, h * HEAD : (h + 1) * HEAD], weights[h], dims, preferred_element_type=F32)
        )
    return jnp.concatenate(parts, axis=1)


def kernel(
    nz, nv,
    hidden, head, teacher, targets, xin, gains, wspan,
    out, loss_ref,
    wbuf, hid, tea, tgt, logits, texp, dlog, stats, snd_x, rcv_x, pass_x, snd_y, rcv_y, pass_y, two_x, end_x, two_y, end_y, xs, gs, ws,
    sq, dots, vec_y, vec_x, told, heard, own_loss, losses, ys,
    loc_sem, zs_sem, zr_sem, ds_sem, dr_sem, ms_sem, mr_sem, sts_sem, str_sem, xs_sem, xr_sem, ys_sem, yr_sem,
    exs_sem, exr_sem, eys_sem, eyr_sem,    sqs_sem, sqr_sem, dos_sem, dor_sem, los_sem, lor_sem, vys_sem, vyr_sem, vxs_sem, vxr_sem, tos_sem, tor_sem, os_sem, or_sem,
):
    core = lax.axis_index("section")
    seq = lax.axis_index("seq")
    voc = lax.axis_index("vocab")
    z, xh = seq // 2, seq % 2
    xl = voc % 2
    other = 1 - core
    half = nz // 2
    tok, width = hid.shape[1], hid.shape[2]
    rows, cols = head.shape[0], wbuf.shape[2]
    slice_width = xs.shape[3]
    plane = 2 * nv
    me = xh * nv + voc
    half_tok = tok // 2
    ny = nv // 2
    xi, yi = xh * 2 + xl, voc // 2

    def at(c, zz, hh, v):
        return (c, zz * 2 + hh, v)

    def plane_peer(index):
        return at(core, z, index // nv, index % nv)

    def in_plane(x, y):
        return at(core, z, x // 2, y * 2 + x % 2)

    mate = at(other, z, xh, voc)
    partner = at(core, z, 1 - xh, voc)
    partner_mate = at(other, z, 1 - xh, voc)
    near = at(core, z, 1 - xh, voc + 1 - 2 * xl)
    right = at(core, (z + 1) % nz, xh, voc)
    left = at(core, (z + nz - 1) % nz, xh, voc)
    barrier = pltpu.get_barrier_semaphore()
    direct = [mate, partner_mate, right, left]
    for peer in direct:
        pl.semaphore_signal(barrier, inc=1, device_id=peer, device_id_type=MESH)

    def greet(i, carry):
        pl.semaphore_signal(barrier, inc=1, device_id=plane_peer((me + i) % plane), device_id_type=MESH)
        return carry

    lax.fori_loop(1, plane, greet, 0)
    pl.semaphore_wait(barrier, len(direct) + plane - 1)

    def remote(src, dst, send, recv, peer):
        return pltpu.make_async_remote_copy(
            src_ref=src, dst_ref=dst, send_sem=send, recv_sem=recv, device_id=peer, device_id_type=MESH
        )

    sent = []

    def begin(copy):
        copy.start()
        sent.append(copy)

    part_rows = rows // 2

    def part_at(section, delta, part):
        zz = lax.rem(z + delta + nz, nz)
        hh = xh if part < 2 else 1 - xh
        start = (zz * 2 + hh) * rows + (part % 2) * part_rows
        return wbuf.at[section, pl.ds(pl.multiple_of(start, part_rows), part_rows), :]

    def own_columns(hh):
        return pl.ds(pl.multiple_of(hh * cols, cols), cols)

    own_block = head.at[:, own_columns(xh)]

    def own_part(part, hh):
        return head.at[pl.ds(part * part_rows, part_rows), own_columns(hh)]

    ring_parts = [
        [(k, part) for k in range(1, half) for part in range(4)] + [(half, 2 * way), (half, 2 * way + 1)]
        for way in (0, 1)
    ]
    ring_count = len(ring_parts[0])
    ring_copies = [[], []]

    def ring_send(way, i):
        k, part = ring_parts[way][i]
        slot = part_at(core, -(k - 1) if way == 0 else k - 1, part)
        src = own_part(part, xh) if k == 1 and part < 2 else slot
        if k > 1:
            ring_wait(way, ring_parts[way].index((k - 1, part)))
        if i >= 2:
            ring_copies[way][i - 2].wait_send()
        copy = remote(src, slot, zs_sem.at[way, i], zr_sem.at[way, i], right if way == 0 else left)
        copy.start()
        ring_copies[way].append(copy)

    arrived = [0, 0]

    def ring_wait(way, i):
        while arrived[way] <= i:
            j = arrived[way]
            k, part = ring_parts[way][j]
            delta = -k if way == 0 else k
            slot = part_at(core, delta, part)
            remote(slot, slot, zs_sem.at[way, j], zr_sem.at[way, j], right).wait_recv()
            mate_send(delta, part)
            arrived[way] += 1

    def mate_send(delta, part):
        slot = part_at(core, delta, part)
        src = own_part(part, xh) if delta == 0 and part < 2 else slot
        i = (delta % nz) * 4 + part
        begin(remote(src, slot, ds_sem.at[i], dr_sem.at[i], mate))

    def mate_wait(delta, part):
        slot = part_at(other, delta, part)
        i = (delta % nz) * 4 + part
        remote(slot, slot, ds_sem.at[i], dr_sem.at[i], mate).wait_recv()

    def partner_send(part):
        slot = part_at(core, 0, part)
        copy = remote(own_part(part, 1 - xh), slot, ms_sem.at[9 * part], mr_sem.at[9 * part], partner)
        copy.start()
        return copy

    def partner_wait(part):
        slot = part_at(core, 0, part + 2)
        remote(slot, slot, ms_sem.at[9 * part], mr_sem.at[9 * part], partner).wait_recv()
        mate_send(0, part + 2)

    my_rows = wbuf.at[core, pl.ds(pl.multiple_of(seq * rows, rows), rows), :]
    first = partner_send(0)
    for i in (0, 1):
        for way in (0, 1):
            ring_send(way, i)
        mate_send(0, i)

    local = [
        pltpu.make_async_copy(own_block, my_rows, loc_sem.at[0]),
        pltpu.make_async_copy(xin.at[0, :, core], xs.at[core], loc_sem.at[1]),
        pltpu.make_async_copy(gains.at[0], gs.at[core], loc_sem.at[2]),
        pltpu.make_async_copy(wspan.at[0], ws.at[core], loc_sem.at[3]),
        pltpu.make_async_copy(hidden.at[core], hid.at[xh], loc_sem.at[4]),
        pltpu.make_async_copy(teacher.at[core, :, own_columns(xh)], tea.at[core, xh], loc_sem.at[5]),
        pltpu.make_async_copy(targets, tgt.at[xh], loc_sem.at[6]),
    ]
    for copy in local:
        copy.start()
    begin(remote(xin.at[0, :, other], xs.at[core], ms_sem.at[1], mr_sem.at[1], mate))
    begin(remote(gains.at[0], gs.at[core], ms_sem.at[2], mr_sem.at[2], mate))
    begin(remote(wspan.at[0], ws.at[core], ms_sem.at[3], mr_sem.at[3], mate))
    begin(remote(teacher.at[other, :, own_columns(xh)], tea.at[core, xh], ms_sem.at[4], mr_sem.at[4], mate))

    first.wait_send()
    second = partner_send(1)
    partner_wait(0)
    for way in (0, 1):
        ring_send(way, 2)
    second.wait_send()
    begin(remote(hidden.at[core], hid.at[xh], ms_sem.at[5], mr_sem.at[5], near))
    begin(remote(targets, tgt.at[xh], ms_sem.at[6], mr_sem.at[6], partner))
    begin(remote(teacher.at[core, :, own_columns(1 - xh)], tea.at[core, xh], ms_sem.at[7], mr_sem.at[7], partner))
    begin(
        remote(teacher.at[other, :, own_columns(1 - xh)], tea.at[core, xh], ms_sem.at[8], mr_sem.at[8], partner_mate)
    )

    for copy in local:
        copy.wait()
    remote(xs.at[other], xs.at[other], ms_sem.at[1], mr_sem.at[1], mate).wait_recv()
    remote(gs.at[other], gs.at[other], ms_sem.at[2], mr_sem.at[2], mate).wait_recv()
    remote(ws.at[other], ws.at[other], ms_sem.at[3], mr_sem.at[3], mate).wait_recv()

    def saved(c):
        return xs[SPAN_AT[c]].astype(F32)

    def gain(c):
        section, slot_index = SPAN_AT[c]
        return gs[section, slot_index : slot_index + 1, :]

    def exchange(buf, send_sems, recv_sems):
        def send(i, carry):
            peer = at(core, z, xh, (voc + i) % nv)
            remote(buf.at[voc], buf.at[voc], send_sems.at[i], recv_sems.at[i], peer).start()
            return carry

        lax.fori_loop(1, nv, send, 0)

    def exchange_wait(buf, send_sems, recv_sems):
        def wait(i, carry):
            src = (voc + nv - i) % nv
            remote(buf.at[src], buf.at[src], send_sems.at[i], recv_sems.at[i], mate).wait_recv()
            remote(buf.at[voc], buf.at[voc], send_sems.at[i], recv_sems.at[i], mate).wait_send()
            return carry

        lax.fori_loop(1, nv, wait, 0)
        total = buf[0]
        for i in range(1, nv):
            total = total + buf[i]
        return total

    squares = []
    for c in range(4):
        value = saved(c)
        squares.append(jnp.sum(value * value, axis=1, keepdims=True))
    sq[voc] = to_rows(squares, 8)
    exchange(sq, sqs_sem, sqr_sem)
    def multiply(delta, first=False):
        for part in range(4):
            mate_wait(delta, part)
        zz = lax.rem(z + delta + nz, nz)
        span = pl.ds(pl.multiple_of(zz * 2 * rows, 2 * rows), 2 * rows)
        left_part = hid[:, :, span].reshape(2 * tok, 2 * rows)
        for s in (0, 1):
            product = jnp.dot(left_part, wbuf[s, span, :], preferred_element_type=F32)
            if first:
                logits[s] = product
            else:
                logits[s] += product

    def hidden_wait():
        slot = hid.at[1 - xh]
        remote(slot, slot, ms_sem.at[5], mr_sem.at[5], near).wait_recv()

    def span_ready():
        inv_rows = lax.rsqrt(exchange_wait(sq, sqs_sem, sqr_sem) / width + EPS)
        total = to_columns(inv_rows)
        inv = [total[:, c : c + 1] for c in range(4)]

        def back(c, value):
            return value + inv[c] * heads_dot((value * gain(c)).astype(BF16), ws[SPAN_AT[c]], False)

        def inner(c, value):
            return jnp.sum(saved(c) * inv[c] ** 3 * value, axis=1, keepdims=True)

        products = []
        for c in range(4):
            value = heads_dot((saved(c) * gain(c)).astype(BF16), ws[SPAN_AT[c]], False)
            for upper in range(c + 1, 4):
                products.append(inner(upper, value))
                value = back(upper, value)
            vec_y[yi, c] = value[:half_tok].astype(BF16)
            vec_x[xi, c] = value[half_tok:].astype(BF16)
        dots[voc] = to_rows(products, 8)
        exchange(dots, dos_sem, dor_sem)
        return inv, inv_rows

    def vectors_y_send():
        for oy in range(1, ny):
            begin(remote(vec_y.at[yi], vec_y.at[yi], vys_sem.at[oy], vyr_sem.at[oy], in_plane(xi, (yi + oy) % ny)))

    def vectors_x_send():
        for ox in range(1, 4):
            begin(remote(vec_x.at[xi], vec_x.at[xi], vxs_sem.at[ox], vxr_sem.at[ox], in_plane((xi + ox) % 4, yi)))

    def vectors_wait():
        for oy in range(1, ny):
            slot = vec_y.at[(yi + ny - oy) % ny]
            remote(slot, slot, vys_sem.at[oy], vyr_sem.at[oy], mate).wait_recv()
        for ox in range(1, 4):
            slot = vec_x.at[(xi + 4 - ox) % 4]
            remote(slot, slot, vxs_sem.at[ox], vxr_sem.at[ox], mate).wait_recv()

    def teacher_ready():
        pairs = ((other, xh, 4, mate), (core, 1 - xh, 7, partner), (other, 1 - xh, 8, partner_mate))
        for s, hh, i, peer in pairs:
            slot = tea.at[s, hh]
            remote(slot, slot, ms_sem.at[i], mr_sem.at[i], peer).wait_recv()
        slot = tgt.at[1 - xh]
        remote(slot, slot, ms_sem.at[6], mr_sem.at[6], partner).wait_recv()
        values = [tea[s].reshape(2 * tok, cols).astype(F32) for s in (0, 1)]
        top = jnp.max(jnp.maximum(values[0], values[1]), axis=1, keepdims=True)
        total = jnp.zeros((2 * tok, 1), F32)
        for s in (0, 1):
            value = jnp.exp(values[s] - top)
            texp[s] = value
            total += jnp.sum(value, axis=1, keepdims=True)
        return top, total

    partner_wait(1)
    for way in (0, 1):
        ring_send(way, 3)
    for i in range(4, ring_count):
        for way in (0, 1):
            ring_send(way, i)
        if i == 5:
            inv, inv_rows = span_ready()
            vectors_y_send()
        if i == ring_count - 2:
            teacher_top, teacher_total = teacher_ready()
            hidden_wait()
            vectors_x_send()
            multiply(0, first=True)
            for d in range(1, half - 2):
                multiply(-d)
                multiply(d)
    for i in range(ring_count - 4, ring_count):
        for way in (0, 1):
            ring_wait(way, i)
        if i == ring_count - 4:
            for d in range(max(1, half - 2), half - 1):
                multiply(-d)
                multiply(d)
        if i == ring_count - 3:
            multiply(1 - half)
            multiply(half - 1)
    multiply(half)

    def target_column():
        parts = []
        for hh in (0, 1):
            row = jnp.where(core == 0, tgt[hh, 0:1, :], tgt[hh, 1:2, :])
            parts.append(jnp.broadcast_to(row, (128, tok)).T[:, 0:1])
        return jnp.concatenate(parts, axis=0)

    wanted = target_column()

    def hit(s):
        start = (s * nv + voc) * 2 * cols + xh * cols
        return wanted - start == lax.broadcasted_iota(jnp.int32, (2 * tok, cols), 1)

    student_top = jnp.max(jnp.maximum(logits[0], logits[1]), axis=1, keepdims=True)
    student_total = jnp.zeros((2 * tok, 1), F32)
    cross = jnp.zeros((2 * tok, 1), F32)
    target_logit = jnp.zeros((2 * tok, 1), F32)
    for s in (0, 1):
        value = logits[s]
        cross += jnp.sum(texp[s] * (tea[s].reshape(2 * tok, cols).astype(F32) - value), axis=1, keepdims=True)
        target_logit += jnp.sum(jnp.where(hit(s), value, 0.0), axis=1, keepdims=True)
        value = jnp.exp(value - student_top)
        logits[s] = value
        student_total += jnp.sum(value, axis=1, keepdims=True)
    stats[me] = to_rows([student_top, student_total, teacher_top, teacher_total, cross, target_logit], 8)

    def stats_send(i, carry):
        peer = plane_peer((me + i) % plane)
        remote(stats.at[me], stats.at[me], sts_sem.at[i], str_sem.at[i], peer).start()
        return carry

    def stats_wait(i, carry):
        src = (me + plane - i) % plane
        remote(stats.at[src], stats.at[src], sts_sem.at[i], str_sem.at[i], mate).wait_recv()
        remote(stats.at[me], stats.at[me], sts_sem.at[i], str_sem.at[i], mate).wait_send()
        return carry

    lax.fori_loop(1, plane, stats_send, 0)
    lax.fori_loop(1, plane, stats_wait, 0)
    top_s, top_t = stats[0, 0:1, :], stats[0, 2:3, :]
    for i in range(1, plane):
        top_s = jnp.maximum(top_s, stats[i, 0:1, :])
        top_t = jnp.maximum(top_t, stats[i, 2:3, :])
    sum_s, sum_t, sum_x, sum_l = (jnp.zeros_like(top_s) for _ in range(4))
    for i in range(plane):
        part = stats[i]
        sum_s += part[1:2] * jnp.exp(part[0:1] - top_s)
        factor = jnp.exp(part[2:3] - top_t)
        sum_t += part[3:4] * factor
        sum_x += part[4:5] * factor
        sum_l += part[5:6]
    lse_s = top_s + jnp.log(sum_s)
    lse_t = top_t + jnp.log(sum_t)
    terms = sum_x / sum_t - lse_t + lse_s + CE_WEIGHT * (lse_s - sum_l)
    scales = to_columns(jnp.concatenate([lse_s, lse_t], axis=0))
    student_scale = jnp.exp(student_top - scales[:, 0:1])
    teacher_scale = jnp.exp(teacher_top - scales[:, 1:2])

    own_loss[0] = jnp.broadcast_to(jnp.sum(terms, axis=1, keepdims=True), (8, 128))
    begin(remote(own_loss.at[0], own_loss.at[1], los_sem.at[0, 0], lor_sem.at[0, 0], mate))

    def loss_start():
        remote(own_loss.at[1], own_loss.at[1], los_sem.at[0, 0], lor_sem.at[0, 0], mate).wait_recv()
        losses[z] = own_loss[0] + own_loss[1]
        loss_send(1)

    def loss_send(k):
        for way, peer in ((0, right), (1, left)):
            if k < half or way == 0:
                slot = losses.at[(z + nz - (k - 1)) % nz if way == 0 else (z + k - 1) % nz]
                begin(remote(slot, slot, los_sem.at[way, k], lor_sem.at[way, k], peer))

    def loss_wait(k):
        for way in (0, 1):
            if k < half or way == 0:
                slot = losses.at[(z + nz - k) % nz if way == 0 else (z + k) % nz]
                remote(slot, slot, los_sem.at[way, k], lor_sem.at[way, k], right).wait_recv()
        if k < half:
            loss_send(k + 1)

    for s in (0, 1):
        value = (1.0 + CE_WEIGHT) * (logits[s] * student_scale) - texp[s] * teacher_scale
        value = value - jnp.where(hit(s), CE_WEIGHT, 0.0)
        dlog[s] = (LOSS_SCALE * value).astype(BF16)

    quarter = tok // 4
    upper, lower = pl.ds(0, quarter), pl.ds(quarter, quarter)
    nt = (((1,), (1,)), ((), ()))

    def x_peer(step):
        return in_plane((xi + step + 4) % 4, yi)

    def y_peer(step):
        return in_plane(xi, (yi + step + ny) % ny)

    def stage_x(kind, way, y):
        step = 1 - 2 * way
        part = (upper, lower)[way if kind != 1 else 1 - way]
        source = snd_x.at[(xi + 2) % 4 if kind == 0 else (xi + step + 4) % 4, y, part]
        target = pass_x.at[way, y] if kind == 0 else rcv_x.at[way, y, part]
        return remote(source, target, xs_sem.at[kind, way, y], xr_sem.at[kind, way, y], x_peer(step))

    def stage_y(kind, way, x):
        step = 1 - 2 * way
        part = (upper, lower)[way if kind != 1 else 1 - way]
        source = snd_y.at[(yi + 2) % ny if kind == 0 else (yi + step + ny) % ny, x, part]
        target = pass_y.at[way, x] if kind == 0 else rcv_y.at[way, x, part]
        return remote(source, target, ys_sem.at[kind, way, x], yr_sem.at[kind, way, x], y_peer(step))

    def offset(i):
        return jnp.where(i == 0, 2, jnp.where(i == 1, 1, jnp.where(i == 2, 3, 0)))

    def slice_turn(i, carry):
        oy = offset(i // 2)
        y = (yi + oy) % ny
        lo = (xl + i) % 2
        v = y * 2 + lo
        span = pl.ds(pl.multiple_of(v * slice_width, slice_width), slice_width)
        part = lax.dot_general(dlog[0], wbuf[0, span, :], nt, preferred_element_type=F32)
        part += lax.dot_general(dlog[1], wbuf[1, span, :], nt, preferred_element_type=F32)
        part = part.astype(BF16)
        for hh in (0, 1):
            x = hh * 2 + lo
            snd_x[x, y] = part[hh * tok : hh * tok + half_tok]
            snd_y[y, x] = part[hh * tok + half_tok : (hh + 1) * tok]

        @pl.when(i % 2 == 0)
        def _():
            for way in (0, 1):
                stage_x(0, way, y).start()

        @pl.when(i % 2 == 1)
        def _():
            for way in (0, 1):
                stage_x(1, way, y).start()

        for hh in (0, 1):

            @pl.when(oy == 2)
            def _():
                for way in (0, 1):
                    stage_y(0, way, hh * 2 + lo).start()

            @pl.when(oy == 1)
            def _():
                stage_y(1, 0, hh * 2 + lo).start()

            @pl.when(oy == 3)
            def _():
                stage_y(1, 1, hh * 2 + lo).start()

        return carry

    lax.fori_loop(0, nv, slice_turn, 0)

    def pass_turn(i, carry):
        y = (yi + offset(i)) % ny
        for way in (0, 1):
            step = 1 - 2 * way
            part = (upper, lower)[way]
            stage_x(0, way, y).wait_recv()
            x = (xi + step + 4) % 4
            total = snd_x[x, y, part].astype(F32) + pass_x[way, y].astype(F32)
            snd_x[x, y, part] = total.astype(BF16)
            stage_x(2, way, y).start()
            stage_y(0, way, i).wait_recv()
            to = (yi + step + ny) % ny
            total = snd_y[to, i, part].astype(F32) + pass_y[way, i].astype(F32)
            snd_y[to, i, part] = total.astype(BF16)
            stage_y(2, way, i).start()
        return carry

    lax.fori_loop(0, ny, pass_turn, 0)
    loss_start()
    vectors_wait()
    cross_rows = exchange_wait(dots, dos_sem, dor_sem)

    def sum_x(oy):
        y = (yi + oy) % ny
        total = snd_x[xi, y].astype(F32)
        for way in (0, 1):
            for kind in (1, 2):
                stage_x(kind, way, y).wait_recv()
            total = total + rcv_x[way, y].astype(F32)
        return total

    def sum_y(ox):
        x = (xi + ox) % 4
        total = snd_y[yi, x].astype(F32)
        for way in (0, 1):
            for kind in (1, 2):
                stage_y(kind, way, x).wait_recv()
            total = total + rcv_y[way, x].astype(F32)
        return total

    def fold(value):
        parts = [value[:, i : i + 128] for i in range(0, slice_width, 128)]
        return functools.reduce(lambda a, b: a + b, parts)

    def products_with(vectors, value):
        return [fold(vectors[c].astype(F32) * value) for c in range(4)]

    def add(left_list, right_list):
        return [a + b for a, b in zip(left_list, right_list)]

    first_products = [jnp.zeros((half_tok, 128), F32)] * 4
    for oy in (2, 1, 3):
        value = sum_x(oy)
        two_y[oy] = value.astype(BF16)
        begin(remote(two_y.at[oy], end_y.at[oy], eys_sem.at[oy], eyr_sem.at[oy], in_plane(xi, (yi + oy) % ny)))
        first_products = add(first_products, products_with(vec_y[(yi + oy) % ny], value))
    loss_wait(1)
    first_half = sum_x(0)
    first_products = add(first_products, products_with(vec_y[yi], first_half))
    column_sums = {}
    for ox in range(1, 4):
        column_sums[ox] = sum_y(ox)
        two_x[ox] = column_sums[ox].astype(BF16)
        begin(remote(two_x.at[ox], end_x.at[ox], exs_sem.at[ox], exr_sem.at[ox], in_plane((xi + ox) % 4, yi)))
    second_half = sum_y(0)
    column_sums[0] = second_half
    near_products = [jnp.zeros((half_tok, 128), F32)] * 4
    away_products = near_products
    for ox in range(4):
        x = (xi + ox) % 4
        found = products_with(vec_x[x], column_sums[ox])
        same = x // 2 == xh
        near_products = [a + jnp.where(same, b, 0.0) for a, b in zip(near_products, found)]
        away_products = [a + jnp.where(same, 0.0, b) for a, b in zip(away_products, found)]

    def message(first_part, second_part):
        columns = [
            jnp.sum(jnp.concatenate([a, b], axis=0), axis=1, keepdims=True) for a, b in zip(first_part, second_part)
        ]
        return to_rows(columns, 8)

    away = message([jnp.zeros((half_tok, 128), F32)] * 4, away_products)
    close = message(first_products, near_products)
    told[0] = jnp.where(xh == 0, close, away)
    told[1] = jnp.where(xh == 0, away, close)

    def told_send(i, carry):
        to = (me + i) % plane
        remote(told.at[to // nv], heard.at[me], tos_sem.at[i], tor_sem.at[i], plane_peer(to)).start()
        return carry

    def told_wait(i, carry):
        src = (me + plane - i) % plane
        remote(heard.at[src], heard.at[src], tos_sem.at[i], tor_sem.at[i], mate).wait_recv()
        remote(told.at[0], heard.at[me], tos_sem.at[i], tor_sem.at[i], mate).wait_send()
        return carry

    lax.fori_loop(1, plane, told_send, 0)
    heard[me] = close

    def slice_sent(i, carry):
        for kind in range(3):
            for way in (0, 1):
                stage_x(kind, way, i).wait_send()
                stage_y(kind, way, i).wait_send()
        return carry

    lax.fori_loop(0, ny, slice_sent, 0)

    loss_wait(2)
    for copies in ring_copies:
        for copy in copies[-2:]:
            copy.wait_send()
    for copy in sent:
        copy.wait_send()
    sent.clear()
    for oy in range(1, ny):
        remote(end_y.at[oy], end_y.at[oy], eys_sem.at[oy], eyr_sem.at[oy], mate).wait_recv()
        first_half = first_half + end_y[oy].astype(F32)
    for ox in range(1, 4):
        remote(end_x.at[ox], end_x.at[ox], exs_sem.at[ox], exr_sem.at[ox], mate).wait_recv()
        second_half = second_half + end_x[ox].astype(F32)
    cotangent = jnp.concatenate([first_half.astype(BF16), second_half.astype(BF16)], axis=0)

    lax.fori_loop(1, plane, told_wait, 0)
    found = heard[0]
    for i in range(1, plane):
        found = found + heard[i]
    d0, d1, d2, d3 = (found[c : c + 1] / width for c in range(4))
    e10, e20, e30, e21, e31, e32 = (cross_rows[c : c + 1] / width for c in range(6))
    s3 = d3
    s2 = d2 - s3 * e32
    s1 = d1 - s3 * e31 - s2 * e21
    s0 = d0 - s3 * e30 - s2 * e20 - s1 * e10
    pull = to_columns(inv_rows[0:4] ** 3 * jnp.concatenate([s0, s1, s2, s3], axis=0))
    value = cotangent

    def hand_out(slot_index):
        pltpu.make_async_copy(ys.at[core, slot_index], out.at[0, slot_index, core], loc_sem.at[slot_index]).start()
        begin(
            remote(
                ys.at[other, slot_index], out.at[0, slot_index, core], os_sem.at[slot_index], or_sem.at[slot_index], mate
            )
        )

    for c in (3, 2, 1, 0):
        grad = heads_dot(value, ws[SPAN_AT[c]], True)
        fresh = value.astype(F32) + inv[c] * gain(c) * grad - saved(c) * pull[:, c : c + 1]
        value = fresh.astype(BF16)
        ys[SPAN_AT[c]] = value
        if c == 2:
            hand_out(1)
    hand_out(0)
    for k in range(3, half + 1):
        loss_wait(k)
    loss_total = losses[0]
    for i in range(1, nz):
        loss_total = loss_total + losses[i]
    loss_ref[0, 0] = jnp.max(loss_total) / (4 * tok * nz)
    for slot_index in (1, 0):
        pltpu.make_async_copy(
            ys.at[core, slot_index], out.at[0, slot_index, core], loc_sem.at[slot_index]
        ).wait()
        slot = out.at[0, slot_index, other]
        remote(slot, slot, os_sem.at[slot_index], or_sem.at[slot_index], mate).wait_recv()
    for copy in sent:
        copy.wait_send()


def solution(mesh):
    n_seq, n_voc = mesh.shape["seq"], mesh.shape["vocab"]
    nz = n_seq // 2

    def per_device(hidden, head_weight, teacher_logits, targets, span_inputs, span_gains, span_weights):
        _, tok, width = hidden.shape
        rows, shard = head_weight.shape
        cols = shard // 2
        slice_width = span_inputs.shape[4]
        heads = span_weights.shape[2]
        plane = 2 * n_voc
        half = nz // 2
        dma = pltpu.SemaphoreType.DMA
        any_space = pl.BlockSpec(memory_space=pl.ANY)
        operands = [
            pltpu.with_memory_space_constraint(a, pltpu.HBM)
            for a in (hidden, head_weight, teacher_logits, targets, span_inputs, span_gains, span_weights)
        ]
        grads, loss = pl.pallas_call(
            functools.partial(kernel, nz, n_voc),
            out_shape=(
                jax.ShapeDtypeStruct((1, 2, 2, tok, slice_width), BF16),
                jax.ShapeDtypeStruct((1, 1), F32),
            ),
            in_specs=[any_space] * 7,
            out_specs=(any_space, pl.BlockSpec(memory_space=pltpu.SMEM)),
            scratch_shapes=[
                pltpu.VMEM((2, width, cols), BF16),
                pltpu.VMEM((2, tok, width), BF16),
                pltpu.VMEM((2, 2, tok, cols), BF16),
                pltpu.VMEM((2, 2, tok), jnp.int32),
                pltpu.VMEM((2, 2 * tok, cols), F32),
                pltpu.VMEM((2, 2 * tok, cols), F32),
                pltpu.VMEM((2, 2 * tok, cols), BF16),
                pltpu.VMEM((plane, 8, 2 * tok), F32),
                pltpu.VMEM((4, n_voc // 2, tok // 2, slice_width), BF16),
                pltpu.VMEM((2, n_voc // 2, tok // 2, slice_width), BF16),
                pltpu.VMEM((2, n_voc // 2, tok // 4, slice_width), BF16),
                pltpu.VMEM((n_voc // 2, 4, tok // 2, slice_width), BF16),
                pltpu.VMEM((2, 4, tok // 2, slice_width), BF16),
                pltpu.VMEM((2, 4, tok // 4, slice_width), BF16),
                pltpu.VMEM((4, tok // 2, slice_width), BF16),
                pltpu.VMEM((4, tok // 2, slice_width), BF16),
                pltpu.VMEM((n_voc // 2, tok // 2, slice_width), BF16),
                pltpu.VMEM((n_voc // 2, tok // 2, slice_width), BF16),
                pltpu.VMEM((2, 2, tok, slice_width), BF16),
                pltpu.VMEM((2, 2, slice_width), F32),
                pltpu.VMEM((2, 2, heads, HEAD, HEAD), BF16),
                pltpu.VMEM((n_voc, 8, tok), F32),
                pltpu.VMEM((n_voc, 8, tok), F32),
                pltpu.VMEM((n_voc // 2, 4, tok // 2, slice_width), BF16),
                pltpu.VMEM((4, 4, tok // 2, slice_width), BF16),
                pltpu.VMEM((2, 8, tok), F32),
                pltpu.VMEM((plane, 8, tok), F32),
                pltpu.VMEM((2, 8, 128), F32),
                pltpu.VMEM((nz, 8, 128), F32),
                pltpu.VMEM((2, 2, tok, slice_width), BF16),
                dma((7,)),
                dma((2, 4 * half - 2)),
                dma((2, 4 * half - 2)),
                dma((4 * nz,)),
                dma((4 * nz,)),
                dma((10,)),
                dma((10,)),
                dma((plane,)),
                dma((plane,)),
                dma((3, 2, n_voc // 2)),
                dma((3, 2, n_voc // 2)),
                dma((3, 2, 4)),
                dma((3, 2, 4)),
                dma((4,)),
                dma((4,)),
                dma((n_voc // 2,)),
                dma((n_voc // 2,)),
                dma((n_voc,)),
                dma((n_voc,)),
                dma((n_voc,)),
                dma((n_voc,)),
                dma((2, half + 1)),
                dma((2, half + 1)),
                dma((n_voc // 2,)),
                dma((n_voc // 2,)),
                dma((4,)),
                dma((4,)),
                dma((plane,)),
                dma((plane,)),
                dma((2,)),
                dma((2,)),
            ],
            compiler_params=pltpu.CompilerParams(
                collective_id=0, has_side_effects=True, vmem_limit_bytes=48 * 1024 * 1024
            ),
        )(*operands)
        return grads, loss.reshape(())

    placed = (
        P(None, "seq", None),
        P("seq", ("section", "vocab")),
        P(None, "seq", ("section", "vocab")),
        P(None, "seq"),
        P("section", None, None, "seq", "vocab"),
        P("section", None, "vocab"),
        P("section", None, "vocab", None, None),
    )
    return jax.shard_map(
        per_device,
        mesh=mesh,
        in_specs=placed,
        out_specs=(P("section", None, None, "seq", "vocab"), P()),
        check_vma=False,
    )
```

```python
import functools

import jax
import jax.numpy as jnp
from jax import lax
from jax.experimental import pallas as pl
from jax.experimental.pallas import tpu as pltpu
from jax.sharding import PartitionSpec as P

MESH = pl.DeviceIdType.MESH
F32 = jnp.float32
BF16 = jnp.bfloat16
LOSS_SCALE = 16
CE_WEIGHT = 0.5
EPS = 1e-06
HEAD = 128
SPAN_AT = ((0, 0), (1, 0), (1, 1), (0, 1))


def to_rows(columns, height):
    count = columns[0].shape[0]
    lane = lax.broadcasted_iota(jnp.int32, (count, 128), 1)
    wide = jnp.zeros((count, 128), F32)
    for i, column in enumerate(columns):
        wide = jnp.where(lane == i, column, wide)
    return wide.T[:height]


def to_columns(rows):
    height, count = rows.shape
    return jnp.concatenate([rows, jnp.zeros((128 - height, count), F32)], axis=0).T


def heads_dot(left, weights, transposed):
    dims = (((1,), (1,)), ((), ())) if transposed else (((1,), (0,)), ((), ()))
    parts = []
    for h in range(weights.shape[0]):
        parts.append(
            lax.dot_general(left[:, h * HEAD : (h + 1) * HEAD], weights[h], dims, preferred_element_type=F32)
        )
    return jnp.concatenate(parts, axis=1)


def kernel(
    nz, nv,
    hidden, head, teacher, targets, xin, gains, wspan,
    out, loss_ref,
    wbuf, hid, tea, tgt, logits, texp, dlog, stats, snd_x, rcv_x, pass_x, snd_y, rcv_y, pass_y, two_x, end_x, two_y, end_y, xs, gs, ws,
    sq, dots, vec_y, vec_x, told, heard, own_loss, losses, ys,
    loc_sem, zs_sem, zr_sem, ds_sem, dr_sem, ms_sem, mr_sem, sts_sem, str_sem, xs_sem, xr_sem, ys_sem, yr_sem,
    exs_sem, exr_sem, eys_sem, eyr_sem,    sqs_sem, sqr_sem, dos_sem, dor_sem, los_sem, lor_sem, vys_sem, vyr_sem, vxs_sem, vxr_sem, tos_sem, tor_sem, os_sem, or_sem,
):
    core = lax.axis_index("section")
    seq = lax.axis_index("seq")
    voc = lax.axis_index("vocab")
    z, xh = seq // 2, seq % 2
    xl = voc % 2
    other = 1 - core
    half = nz // 2
    tok, width = hid.shape[1], hid.shape[2]
    rows, cols = head.shape[0], wbuf.shape[2]
    slice_width = xs.shape[3]
    plane = 2 * nv
    me = xh * nv + voc
    half_tok = tok // 2
    ny = nv // 2
    xi, yi = xh * 2 + xl, voc // 2

    def at(c, zz, hh, v):
        return (c, zz * 2 + hh, v)

    def plane_peer(index):
        return at(core, z, index // nv, index % nv)

    def in_plane(x, y):
        return at(core, z, x // 2, y * 2 + x % 2)

    mate = at(other, z, xh, voc)
    partner = at(core, z, 1 - xh, voc)
    partner_mate = at(other, z, 1 - xh, voc)
    near = at(core, z, 1 - xh, voc + 1 - 2 * xl)
    right = at(core, (z + 1) % nz, xh, voc)
    left = at(core, (z + nz - 1) % nz, xh, voc)
    barrier = pltpu.get_barrier_semaphore()
    direct = [mate, partner_mate, right, left]
    for peer in direct:
        pl.semaphore_signal(barrier, inc=1, device_id=peer, device_id_type=MESH)

    def greet(i, carry):
        pl.semaphore_signal(barrier, inc=1, device_id=plane_peer((me + i) % plane), device_id_type=MESH)
        return carry

    lax.fori_loop(1, plane, greet, 0)
    pl.semaphore_wait(barrier, len(direct) + plane - 1)

    def remote(src, dst, send, recv, peer):
        return pltpu.make_async_remote_copy(
            src_ref=src, dst_ref=dst, send_sem=send, recv_sem=recv, device_id=peer, device_id_type=MESH
        )

    sent = []

    def begin(copy):
        copy.start()
        sent.append(copy)

    part_rows = rows // 2

    def part_at(section, delta, part):
        zz = lax.rem(z + delta + nz, nz)
        hh = xh if part < 2 else 1 - xh
        start = (zz * 2 + hh) * rows + (part % 2) * part_rows
        return wbuf.at[section, pl.ds(pl.multiple_of(start, part_rows), part_rows), :]

    def own_columns(hh):
        return pl.ds(pl.multiple_of(hh * cols, cols), cols)

    own_block = head.at[:, own_columns(xh)]

    def own_part(part, hh):
        return head.at[pl.ds(part * part_rows, part_rows), own_columns(hh)]

    ring_parts = [
        [(k, part) for k in range(1, half) for part in range(4)] + [(half, 2 * way), (half, 2 * way + 1)]
        for way in (0, 1)
    ]
    ring_count = len(ring_parts[0])
    ring_copies = [[], []]

    def ring_send(way, i):
        k, part = ring_parts[way][i]
        slot = part_at(core, -(k - 1) if way == 0 else k - 1, part)
        src = own_part(part, xh) if k == 1 and part < 2 else slot
        held = []
        if k > 1:
            held = ring_wait(way, ring_parts[way].index((k - 1, part)))
        if i >= 2:
            ring_copies[way][i - 2].wait_send()
        copy = remote(src, slot, zs_sem.at[way, i], zr_sem.at[way, i], right if way == 0 else left)
        copy.start()
        ring_copies[way].append(copy)
        for come in held:
            mate_send(*come)

    arrived = [0, 0]

    def ring_wait(way, i):
        come = []
        while arrived[way] <= i:
            j = arrived[way]
            k, part = ring_parts[way][j]
            delta = -k if way == 0 else k
            slot = part_at(core, delta, part)
            remote(slot, slot, zs_sem.at[way, j], zr_sem.at[way, j], right).wait_recv()
            come.append((delta, part))
            arrived[way] += 1
        return come

    def mate_send(delta, part):
        slot = part_at(core, delta, part)
        src = own_part(part, xh) if delta == 0 and part < 2 else slot
        i = (delta % nz) * 4 + part
        begin(remote(src, slot, ds_sem.at[i], dr_sem.at[i], mate))

    def mate_wait(delta, part):
        slot = part_at(other, delta, part)
        i = (delta % nz) * 4 + part
        remote(slot, slot, ds_sem.at[i], dr_sem.at[i], mate).wait_recv()

    def partner_send(part):
        slot = part_at(core, 0, part)
        copy = remote(own_part(part, 1 - xh), slot, ms_sem.at[9 * part], mr_sem.at[9 * part], partner)
        copy.start()
        return copy

    def partner_wait(part):
        slot = part_at(core, 0, part + 2)
        remote(slot, slot, ms_sem.at[9 * part], mr_sem.at[9 * part], partner).wait_recv()
        mate_send(0, part + 2)

    my_rows = wbuf.at[core, pl.ds(pl.multiple_of(seq * rows, rows), rows), :]
    first = partner_send(0)
    for i in (0, 1):
        for way in (0, 1):
            ring_send(way, i)
        mate_send(0, i)

    local = [
        pltpu.make_async_copy(own_block, my_rows, loc_sem.at[0]),
        pltpu.make_async_copy(xin.at[0, :, core], xs.at[core], loc_sem.at[1]),
        pltpu.make_async_copy(gains.at[0], gs.at[core], loc_sem.at[2]),
        pltpu.make_async_copy(wspan.at[0], ws.at[core], loc_sem.at[3]),
        pltpu.make_async_copy(hidden.at[core], hid.at[xh], loc_sem.at[4]),
        pltpu.make_async_copy(teacher.at[core, :, own_columns(xh)], tea.at[core, xh], loc_sem.at[5]),
        pltpu.make_async_copy(targets, tgt.at[xh], loc_sem.at[6]),
    ]
    for copy in local:
        copy.start()
    begin(remote(xin.at[0, :, other], xs.at[core], ms_sem.at[1], mr_sem.at[1], mate))
    begin(remote(gains.at[0], gs.at[core], ms_sem.at[2], mr_sem.at[2], mate))
    begin(remote(wspan.at[0], ws.at[core], ms_sem.at[3], mr_sem.at[3], mate))
    begin(remote(teacher.at[other, :, own_columns(xh)], tea.at[core, xh], ms_sem.at[4], mr_sem.at[4], mate))

    first.wait_send()
    second = partner_send(1)
    partner_wait(0)
    for way in (0, 1):
        ring_send(way, 2)
    second.wait_send()
    begin(remote(hidden.at[core], hid.at[xh], ms_sem.at[5], mr_sem.at[5], near))
    begin(remote(targets, tgt.at[xh], ms_sem.at[6], mr_sem.at[6], partner))
    begin(remote(teacher.at[core, :, own_columns(1 - xh)], tea.at[core, xh], ms_sem.at[7], mr_sem.at[7], partner))
    begin(
        remote(teacher.at[other, :, own_columns(1 - xh)], tea.at[core, xh], ms_sem.at[8], mr_sem.at[8], partner_mate)
    )

    for copy in local:
        copy.wait()
    remote(xs.at[other], xs.at[other], ms_sem.at[1], mr_sem.at[1], mate).wait_recv()
    remote(gs.at[other], gs.at[other], ms_sem.at[2], mr_sem.at[2], mate).wait_recv()
    remote(ws.at[other], ws.at[other], ms_sem.at[3], mr_sem.at[3], mate).wait_recv()

    def saved(c):
        return xs[SPAN_AT[c]].astype(F32)

    def gain(c):
        section, slot_index = SPAN_AT[c]
        return gs[section, slot_index : slot_index + 1, :]

    def exchange(buf, send_sems, recv_sems):
        def send(i, carry):
            peer = at(core, z, xh, (voc + i) % nv)
            remote(buf.at[voc], buf.at[voc], send_sems.at[i], recv_sems.at[i], peer).start()
            return carry

        lax.fori_loop(1, nv, send, 0)

    def exchange_wait(buf, send_sems, recv_sems):
        def wait(i, carry):
            src = (voc + nv - i) % nv
            remote(buf.at[src], buf.at[src], send_sems.at[i], recv_sems.at[i], mate).wait_recv()
            remote(buf.at[voc], buf.at[voc], send_sems.at[i], recv_sems.at[i], mate).wait_send()
            return carry

        lax.fori_loop(1, nv, wait, 0)
        total = buf[0]
        for i in range(1, nv):
            total = total + buf[i]
        return total

    squares = []
    for c in range(4):
        value = saved(c)
        squares.append(jnp.sum(value * value, axis=1, keepdims=True))
    sq[voc] = to_rows(squares, 8)
    exchange(sq, sqs_sem, sqr_sem)
    def multiply(delta, first=False):
        zz = lax.rem(z + delta + nz, nz)
        span = pl.ds(pl.multiple_of(zz * 2 * rows, 2 * rows), 2 * rows)
        left_part = hid[:, :, span].reshape(2 * tok, 2 * rows)
        for s in (core, other):
            if s is other:
                for part in range(4):
                    mate_wait(delta, part)
            product = jnp.dot(left_part, wbuf[s, span, :], preferred_element_type=F32)
            if first:
                logits[s] = product
            else:
                logits[s] += product

    def hidden_wait():
        slot = hid.at[1 - xh]
        remote(slot, slot, ms_sem.at[5], mr_sem.at[5], near).wait_recv()

    def span_ready():
        inv_rows = lax.rsqrt(exchange_wait(sq, sqs_sem, sqr_sem) / width + EPS)
        total = to_columns(inv_rows)
        inv = [total[:, c : c + 1] for c in range(4)]

        def back(c, value):
            return value + inv[c] * heads_dot((value * gain(c)).astype(BF16), ws[SPAN_AT[c]], False)

        def inner(c, value):
            return jnp.sum(saved(c) * inv[c] ** 3 * value, axis=1, keepdims=True)

        products = []
        for c in range(4):
            value = heads_dot((saved(c) * gain(c)).astype(BF16), ws[SPAN_AT[c]], False)
            for upper in range(c + 1, 4):
                products.append(inner(upper, value))
                value = back(upper, value)
            vec_y[yi, c] = value[:half_tok].astype(BF16)
            vec_x[xi, c] = value[half_tok:].astype(BF16)
        dots[voc] = to_rows(products, 8)
        exchange(dots, dos_sem, dor_sem)
        return inv, inv_rows

    def vectors_y_send():
        for oy in range(1, ny):
            begin(remote(vec_y.at[yi], vec_y.at[yi], vys_sem.at[oy], vyr_sem.at[oy], in_plane(xi, (yi + oy) % ny)))

    def vectors_x_send():
        for ox in range(1, 4):
            begin(remote(vec_x.at[xi], vec_x.at[xi], vxs_sem.at[ox], vxr_sem.at[ox], in_plane((xi + ox) % 4, yi)))

    def vectors_wait():
        for oy in range(1, ny):
            slot = vec_y.at[(yi + ny - oy) % ny]
            remote(slot, slot, vys_sem.at[oy], vyr_sem.at[oy], mate).wait_recv()
        for ox in range(1, 4):
            slot = vec_x.at[(xi + 4 - ox) % 4]
            remote(slot, slot, vxs_sem.at[ox], vxr_sem.at[ox], mate).wait_recv()

    def teacher_ready():
        pairs = ((other, xh, 4, mate), (core, 1 - xh, 7, partner), (other, 1 - xh, 8, partner_mate))
        for s, hh, i, peer in pairs:
            slot = tea.at[s, hh]
            remote(slot, slot, ms_sem.at[i], mr_sem.at[i], peer).wait_recv()
        slot = tgt.at[1 - xh]
        remote(slot, slot, ms_sem.at[6], mr_sem.at[6], partner).wait_recv()
        values = [tea[s].reshape(2 * tok, cols).astype(F32) for s in (0, 1)]
        top = jnp.max(jnp.maximum(values[0], values[1]), axis=1, keepdims=True)
        total = jnp.zeros((2 * tok, 1), F32)
        for s in (0, 1):
            value = jnp.exp(values[s] - top)
            texp[s] = value
            total += jnp.sum(value, axis=1, keepdims=True)
        return top, total

    partner_wait(1)
    for way in (0, 1):
        ring_send(way, 3)
    for i in range(4, ring_count):
        for way in (0, 1):
            ring_send(way, i)
        if i == 5:
            inv, inv_rows = span_ready()
            vectors_y_send()
        if i == ring_count - 2:
            teacher_top, teacher_total = teacher_ready()
            hidden_wait()
            vectors_x_send()
            multiply(0, first=True)
            for d in range(1, half - 2):
                multiply(-d)
                multiply(d)
    for i in range(ring_count - 4, ring_count):
        for way in (0, 1):
            for come in ring_wait(way, i):
                mate_send(*come)
        if i == ring_count - 4:
            for d in range(max(1, half - 2), half - 1):
                multiply(-d)
                multiply(d)
        if i == ring_count - 3:
            multiply(1 - half)
            multiply(half - 1)
    multiply(half)

    def target_column():
        parts = []
        for hh in (0, 1):
            row = jnp.where(core == 0, tgt[hh, 0:1, :], tgt[hh, 1:2, :])
            parts.append(jnp.broadcast_to(row, (128, tok)).T[:, 0:1])
        return jnp.concatenate(parts, axis=0)

    wanted = target_column()

    def hit(s):
        start = (s * nv + voc) * 2 * cols + xh * cols
        return wanted - start == lax.broadcasted_iota(jnp.int32, (2 * tok, cols), 1)

    student_top = jnp.max(jnp.maximum(logits[0], logits[1]), axis=1, keepdims=True)
    student_total = jnp.zeros((2 * tok, 1), F32)
    cross = jnp.zeros((2 * tok, 1), F32)
    target_logit = jnp.zeros((2 * tok, 1), F32)
    for s in (0, 1):
        value = logits[s]
        cross += jnp.sum(texp[s] * (tea[s].reshape(2 * tok, cols).astype(F32) - value), axis=1, keepdims=True)
        target_logit += jnp.sum(jnp.where(hit(s), value, 0.0), axis=1, keepdims=True)
        value = jnp.exp(value - student_top)
        logits[s] = value
        student_total += jnp.sum(value, axis=1, keepdims=True)
    stats[me] = to_rows([student_top, student_total, teacher_top, teacher_total, cross, target_logit], 8)

    def stats_send(i, carry):
        peer = plane_peer((me + i) % plane)
        remote(stats.at[me], stats.at[me], sts_sem.at[i], str_sem.at[i], peer).start()
        return carry

    def stats_wait(i, carry):
        src = (me + plane - i) % plane
        remote(stats.at[src], stats.at[src], sts_sem.at[i], str_sem.at[i], mate).wait_recv()
        remote(stats.at[me], stats.at[me], sts_sem.at[i], str_sem.at[i], mate).wait_send()
        return carry

    lax.fori_loop(1, plane, stats_send, 0)
    for copies in ring_copies:
        for copy in copies[-2:]:
            copy.wait_send()
    for copy in sent:
        copy.wait_send()
    sent.clear()
    lax.fori_loop(1, plane, stats_wait, 0)
    top_s, top_t = stats[0, 0:1, :], stats[0, 2:3, :]
    for i in range(1, plane):
        top_s = jnp.maximum(top_s, stats[i, 0:1, :])
        top_t = jnp.maximum(top_t, stats[i, 2:3, :])
    sum_s, sum_t, sum_x, sum_l = (jnp.zeros_like(top_s) for _ in range(4))
    for i in range(plane):
        part = stats[i]
        sum_s += part[1:2] * jnp.exp(part[0:1] - top_s)
        factor = jnp.exp(part[2:3] - top_t)
        sum_t += part[3:4] * factor
        sum_x += part[4:5] * factor
        sum_l += part[5:6]
    lse_s = top_s + jnp.log(sum_s)
    lse_t = top_t + jnp.log(sum_t)
    terms = sum_x / sum_t - lse_t + lse_s + CE_WEIGHT * (lse_s - sum_l)
    scales = to_columns(jnp.concatenate([lse_s, lse_t], axis=0))
    student_scale = jnp.exp(student_top - scales[:, 0:1])
    teacher_scale = jnp.exp(teacher_top - scales[:, 1:2])

    own_loss[0] = jnp.broadcast_to(jnp.sum(terms, axis=1, keepdims=True), (8, 128))
    begin(remote(own_loss.at[0], own_loss.at[1], los_sem.at[0, 0], lor_sem.at[0, 0], mate))

    def loss_start():
        remote(own_loss.at[1], own_loss.at[1], los_sem.at[0, 0], lor_sem.at[0, 0], mate).wait_recv()
        losses[z] = own_loss[0] + own_loss[1]
        loss_send(1)

    def loss_send(k):
        for way, peer in ((0, right), (1, left)):
            if k < half or way == 0:
                slot = losses.at[(z + nz - (k - 1)) % nz if way == 0 else (z + k - 1) % nz]
                begin(remote(slot, slot, los_sem.at[way, k], lor_sem.at[way, k], peer))

    def loss_wait(k):
        for way in (0, 1):
            if k < half or way == 0:
                slot = losses.at[(z + nz - k) % nz if way == 0 else (z + k) % nz]
                remote(slot, slot, los_sem.at[way, k], lor_sem.at[way, k], right).wait_recv()
        if k < half:
            loss_send(k + 1)

    for s in (0, 1):
        value = (1.0 + CE_WEIGHT) * (logits[s] * student_scale) - texp[s] * teacher_scale
        value = value - jnp.where(hit(s), CE_WEIGHT, 0.0)
        dlog[s] = (LOSS_SCALE * value).astype(BF16)

    quarter = tok // 4
    upper, lower = pl.ds(0, quarter), pl.ds(quarter, quarter)
    nt = (((1,), (1,)), ((), ()))

    def x_peer(step):
        return in_plane((xi + step + 4) % 4, yi)

    def y_peer(step):
        return in_plane(xi, (yi + step + ny) % ny)

    def stage_x(kind, way, y):
        step = 1 - 2 * way
        part = (upper, lower)[way if kind != 1 else 1 - way]
        source = snd_x.at[(xi + 2) % 4 if kind == 0 else (xi + step + 4) % 4, y, part]
        target = pass_x.at[way, y] if kind == 0 else rcv_x.at[way, y, part]
        return remote(source, target, xs_sem.at[kind, way, y], xr_sem.at[kind, way, y], x_peer(step))

    def stage_y(kind, way, x):
        step = 1 - 2 * way
        part = (upper, lower)[way if kind != 1 else 1 - way]
        source = snd_y.at[(yi + 2) % ny if kind == 0 else (yi + step + ny) % ny, x, part]
        target = pass_y.at[way, x] if kind == 0 else rcv_y.at[way, x, part]
        return remote(source, target, ys_sem.at[kind, way, x], yr_sem.at[kind, way, x], y_peer(step))

    def offset(i):
        return jnp.where(i == 0, 2, jnp.where(i == 1, 1, jnp.where(i == 2, 3, 0)))

    def slice_turn(i, carry):
        oy = offset(i // 2)
        y = (yi + oy) % ny
        lo = (xl + i) % 2
        v = y * 2 + lo
        span = pl.ds(pl.multiple_of(v * slice_width, slice_width), slice_width)
        part = lax.dot_general(dlog[0], wbuf[0, span, :], nt, preferred_element_type=F32)
        part += lax.dot_general(dlog[1], wbuf[1, span, :], nt, preferred_element_type=F32)
        part = part.astype(BF16)
        for hh in (0, 1):
            x = hh * 2 + lo
            snd_x[x, y] = part[hh * tok : hh * tok + half_tok]
            snd_y[y, x] = part[hh * tok + half_tok : (hh + 1) * tok]

        @pl.when(i % 2 == 0)
        def _():
            for way in (0, 1):
                stage_x(0, way, y).start()

        @pl.when(i % 2 == 1)
        def _():
            for way in (0, 1):
                stage_x(1, way, y).start()

        for hh in (0, 1):

            @pl.when(oy == 2)
            def _():
                for way in (0, 1):
                    stage_y(0, way, hh * 2 + lo).start()

            @pl.when(oy == 1)
            def _():
                stage_y(1, 0, hh * 2 + lo).start()

            @pl.when(oy == 3)
            def _():
                stage_y(1, 1, hh * 2 + lo).start()

        return carry

    lax.fori_loop(0, nv, slice_turn, 0)

    def pass_turn(i, carry):
        y = (yi + offset(i)) % ny
        for way in (0, 1):
            step = 1 - 2 * way
            part = (upper, lower)[way]
            stage_x(0, way, y).wait_recv()
            x = (xi + step + 4) % 4
            total = snd_x[x, y, part].astype(F32) + pass_x[way, y].astype(F32)
            snd_x[x, y, part] = total.astype(BF16)
            stage_x(2, way, y).start()
            stage_y(0, way, i).wait_recv()
            to = (yi + step + ny) % ny
            total = snd_y[to, i, part].astype(F32) + pass_y[way, i].astype(F32)
            snd_y[to, i, part] = total.astype(BF16)
            stage_y(2, way, i).start()
        return carry

    lax.fori_loop(0, ny, pass_turn, 0)
    loss_start()
    vectors_wait()
    cross_rows = exchange_wait(dots, dos_sem, dor_sem)

    def sum_x(oy):
        y = (yi + oy) % ny
        total = snd_x[xi, y].astype(F32)
        for way in (0, 1):
            for kind in (1, 2):
                stage_x(kind, way, y).wait_recv()
            total = total + rcv_x[way, y].astype(F32)
        return total

    def sum_y(ox):
        x = (xi + ox) % 4
        total = snd_y[yi, x].astype(F32)
        for way in (0, 1):
            for kind in (1, 2):
                stage_y(kind, way, x).wait_recv()
            total = total + rcv_y[way, x].astype(F32)
        return total

    def fold(value):
        parts = [value[:, i : i + 128] for i in range(0, slice_width, 128)]
        return functools.reduce(lambda a, b: a + b, parts)

    def products_with(vectors, value):
        return [fold(vectors[c].astype(F32) * value) for c in range(4)]

    def add(left_list, right_list):
        return [a + b for a, b in zip(left_list, right_list)]

    first_products = [jnp.zeros((half_tok, 128), F32)] * 4
    for oy in (2, 1, 3):
        value = sum_x(oy)
        two_y[oy] = value.astype(BF16)
        begin(remote(two_y.at[oy], end_y.at[oy], eys_sem.at[oy], eyr_sem.at[oy], in_plane(xi, (yi + oy) % ny)))
        first_products = add(first_products, products_with(vec_y[(yi + oy) % ny], value))
    loss_wait(1)
    first_half = sum_x(0)
    first_products = add(first_products, products_with(vec_y[yi], first_half))
    column_sums = {}
    for ox in range(1, 4):
        column_sums[ox] = sum_y(ox)
        two_x[ox] = column_sums[ox].astype(BF16)
    second_half = sum_y(0)
    column_sums[0] = second_half
    near_products = [jnp.zeros((half_tok, 128), F32)] * 4
    away_products = near_products
    for ox in range(4):
        x = (xi + ox) % 4
        found = products_with(vec_x[x], column_sums[ox])
        same = x // 2 == xh
        near_products = [a + jnp.where(same, b, 0.0) for a, b in zip(near_products, found)]
        away_products = [a + jnp.where(same, 0.0, b) for a, b in zip(away_products, found)]

    def message(first_part, second_part):
        columns = [
            jnp.sum(jnp.concatenate([a, b], axis=0), axis=1, keepdims=True) for a, b in zip(first_part, second_part)
        ]
        return to_rows(columns, 8)

    away = message([jnp.zeros((half_tok, 128), F32)] * 4, away_products)
    close = message(first_products, near_products)
    told[0] = jnp.where(xh == 0, close, away)
    told[1] = jnp.where(xh == 0, away, close)

    def told_send(i, carry):
        to = (me + i) % plane
        remote(told.at[to // nv], heard.at[me], tos_sem.at[i], tor_sem.at[i], plane_peer(to)).start()
        return carry

    def told_wait(i, carry):
        src = (me + plane - i) % plane
        remote(heard.at[src], heard.at[src], tos_sem.at[i], tor_sem.at[i], mate).wait_recv()
        remote(told.at[0], heard.at[me], tos_sem.at[i], tor_sem.at[i], mate).wait_send()
        return carry

    lax.fori_loop(1, plane, told_send, 0)
    for ox in (2, 1, 3):
        begin(remote(two_x.at[ox], end_x.at[ox], exs_sem.at[ox], exr_sem.at[ox], in_plane((xi + ox) % 4, yi)))
    heard[me] = close

    def slice_sent(i, carry):
        for kind in range(3):
            for way in (0, 1):
                stage_x(kind, way, i).wait_send()
                stage_y(kind, way, i).wait_send()
        return carry

    lax.fori_loop(0, ny, slice_sent, 0)

    loss_wait(2)
    for oy in range(1, ny):
        remote(end_y.at[oy], end_y.at[oy], eys_sem.at[oy], eyr_sem.at[oy], mate).wait_recv()
        first_half = first_half + end_y[oy].astype(F32)
    for ox in range(1, 4):
        remote(end_x.at[ox], end_x.at[ox], exs_sem.at[ox], exr_sem.at[ox], mate).wait_recv()
        second_half = second_half + end_x[ox].astype(F32)
    cotangent = jnp.concatenate([first_half.astype(BF16), second_half.astype(BF16)], axis=0)

    lax.fori_loop(1, plane, told_wait, 0)
    found = heard[0]
    for i in range(1, plane):
        found = found + heard[i]
    d0, d1, d2, d3 = (found[c : c + 1] / width for c in range(4))
    e10, e20, e30, e21, e31, e32 = (cross_rows[c : c + 1] / width for c in range(6))
    s3 = d3
    s2 = d2 - s3 * e32
    s1 = d1 - s3 * e31 - s2 * e21
    s0 = d0 - s3 * e30 - s2 * e20 - s1 * e10
    pull = to_columns(inv_rows[0:4] ** 3 * jnp.concatenate([s0, s1, s2, s3], axis=0))
    value = cotangent

    def hand_out(slot_index):
        pltpu.make_async_copy(ys.at[core, slot_index], out.at[0, slot_index, core], loc_sem.at[slot_index]).start()
        begin(
            remote(
                ys.at[other, slot_index], out.at[0, slot_index, core], os_sem.at[slot_index], or_sem.at[slot_index], mate
            )
        )

    for c in (3, 2, 1, 0):
        grad = heads_dot(value, ws[SPAN_AT[c]], True)
        fresh = value.astype(F32) + inv[c] * gain(c) * grad - saved(c) * pull[:, c : c + 1]
        value = fresh.astype(BF16)
        ys[SPAN_AT[c]] = value
        if c == 2:
            hand_out(1)
    hand_out(0)
    for k in range(3, half + 1):
        loss_wait(k)
    loss_total = losses[0]
    for i in range(1, nz):
        loss_total = loss_total + losses[i]
    loss_ref[0, 0] = jnp.max(loss_total) / (4 * tok * nz)
    for slot_index in (1, 0):
        pltpu.make_async_copy(
            ys.at[core, slot_index], out.at[0, slot_index, core], loc_sem.at[slot_index]
        ).wait()
        slot = out.at[0, slot_index, other]
        remote(slot, slot, os_sem.at[slot_index], or_sem.at[slot_index], mate).wait_recv()
    for copy in sent:
        copy.wait_send()


def solution(mesh):
    n_seq, n_voc = mesh.shape["seq"], mesh.shape["vocab"]
    nz = n_seq // 2

    def per_device(hidden, head_weight, teacher_logits, targets, span_inputs, span_gains, span_weights):
        _, tok, width = hidden.shape
        rows, shard = head_weight.shape
        cols = shard // 2
        slice_width = span_inputs.shape[4]
        heads = span_weights.shape[2]
        plane = 2 * n_voc
        half = nz // 2
        dma = pltpu.SemaphoreType.DMA
        any_space = pl.BlockSpec(memory_space=pl.ANY)
        operands = [
            pltpu.with_memory_space_constraint(a, pltpu.HBM)
            for a in (hidden, head_weight, teacher_logits, targets, span_inputs, span_gains, span_weights)
        ]
        grads, loss = pl.pallas_call(
            functools.partial(kernel, nz, n_voc),
            out_shape=(
                jax.ShapeDtypeStruct((1, 2, 2, tok, slice_width), BF16),
                jax.ShapeDtypeStruct((1, 1), F32),
            ),
            in_specs=[any_space] * 7,
            out_specs=(any_space, pl.BlockSpec(memory_space=pltpu.SMEM)),
            scratch_shapes=[
                pltpu.VMEM((2, width, cols), BF16),
                pltpu.VMEM((2, tok, width), BF16),
                pltpu.VMEM((2, 2, tok, cols), BF16),
                pltpu.VMEM((2, 2, tok), jnp.int32),
                pltpu.VMEM((2, 2 * tok, cols), F32),
                pltpu.VMEM((2, 2 * tok, cols), F32),
                pltpu.VMEM((2, 2 * tok, cols), BF16),
                pltpu.VMEM((plane, 8, 2 * tok), F32),
                pltpu.VMEM((4, n_voc // 2, tok // 2, slice_width), BF16),
                pltpu.VMEM((2, n_voc // 2, tok // 2, slice_width), BF16),
                pltpu.VMEM((2, n_voc // 2, tok // 4, slice_width), BF16),
                pltpu.VMEM((n_voc // 2, 4, tok // 2, slice_width), BF16),
                pltpu.VMEM((2, 4, tok // 2, slice_width), BF16),
                pltpu.VMEM((2, 4, tok // 4, slice_width), BF16),
                pltpu.VMEM((4, tok // 2, slice_width), BF16),
                pltpu.VMEM((4, tok // 2, slice_width), BF16),
                pltpu.VMEM((n_voc // 2, tok // 2, slice_width), BF16),
                pltpu.VMEM((n_voc // 2, tok // 2, slice_width), BF16),
                pltpu.VMEM((2, 2, tok, slice_width), BF16),
                pltpu.VMEM((2, 2, slice_width), F32),
                pltpu.VMEM((2, 2, heads, HEAD, HEAD), BF16),
                pltpu.VMEM((n_voc, 8, tok), F32),
                pltpu.VMEM((n_voc, 8, tok), F32),
                pltpu.VMEM((n_voc // 2, 4, tok // 2, slice_width), BF16),
                pltpu.VMEM((4, 4, tok // 2, slice_width), BF16),
                pltpu.VMEM((2, 8, tok), F32),
                pltpu.VMEM((plane, 8, tok), F32),
                pltpu.VMEM((2, 8, 128), F32),
                pltpu.VMEM((nz, 8, 128), F32),
                pltpu.VMEM((2, 2, tok, slice_width), BF16),
                dma((7,)),
                dma((2, 4 * half - 2)),
                dma((2, 4 * half - 2)),
                dma((4 * nz,)),
                dma((4 * nz,)),
                dma((10,)),
                dma((10,)),
                dma((plane,)),
                dma((plane,)),
                dma((3, 2, n_voc // 2)),
                dma((3, 2, n_voc // 2)),
                dma((3, 2, 4)),
                dma((3, 2, 4)),
                dma((4,)),
                dma((4,)),
                dma((n_voc // 2,)),
                dma((n_voc // 2,)),
                dma((n_voc,)),
                dma((n_voc,)),
                dma((n_voc,)),
                dma((n_voc,)),
                dma((2, half + 1)),
                dma((2, half + 1)),
                dma((n_voc // 2,)),
                dma((n_voc // 2,)),
                dma((4,)),
                dma((4,)),
                dma((plane,)),
                dma((plane,)),
                dma((2,)),
                dma((2,)),
            ],
            compiler_params=pltpu.CompilerParams(
                collective_id=0, has_side_effects=True, vmem_limit_bytes=48 * 1024 * 1024
            ),
        )(*operands)
        return grads, loss.reshape(())

    placed = (
        P(None, "seq", None),
        P("seq", ("section", "vocab")),
        P(None, "seq", ("section", "vocab")),
        P(None, "seq"),
        P("section", None, None, "seq", "vocab"),
        P("section", None, "vocab"),
        P("section", None, "vocab", None, None),
    )
    return jax.shard_map(
        per_device,
        mesh=mesh,
        in_specs=placed,
        out_specs=(P("section", None, None, "seq", "vocab"), P()),
        check_vma=False,
    )
```

```python
import functools

import jax
import jax.numpy as jnp
from jax import lax
from jax.experimental import pallas as pl
from jax.experimental.pallas import tpu as pltpu
from jax.sharding import PartitionSpec as P

MESH = pl.DeviceIdType.MESH
F32 = jnp.float32
BF16 = jnp.bfloat16
LOSS_SCALE = 16
CE_WEIGHT = 0.5
EPS = 1e-06
HEAD = 128
SPAN_AT = ((0, 0), (1, 0), (1, 1), (0, 1))


def to_rows(columns, height):
    count = columns[0].shape[0]
    lane = lax.broadcasted_iota(jnp.int32, (count, 128), 1)
    wide = jnp.zeros((count, 128), F32)
    for i, column in enumerate(columns):
        wide = jnp.where(lane == i, column, wide)
    return wide.T[:height]


def to_columns(rows):
    height, count = rows.shape
    return jnp.concatenate([rows, jnp.zeros((128 - height, count), F32)], axis=0).T


def heads_dot(left, weights, transposed):
    dims = (((1,), (1,)), ((), ())) if transposed else (((1,), (0,)), ((), ()))
    parts = []
    for h in range(weights.shape[0]):
        parts.append(
            lax.dot_general(left[:, h * HEAD : (h + 1) * HEAD], weights[h], dims, preferred_element_type=F32)
        )
    return jnp.concatenate(parts, axis=1)


def kernel(
    nz, nv,
    hidden, head, teacher, targets, xin, gains, wspan,
    out, loss_ref,
    wbuf, hid, tea, tgt, logits, texp, dlog, stats, snd_x, rcv_x, pass_x, snd_y, rcv_y, pass_y, two_x, end_x, two_y, end_y, xs, gs, ws,
    sq, dots, vec_y, vec_x, told, heard, own_loss, losses, ys,
    loc_sem, zs_sem, zr_sem, ds_sem, dr_sem, ms_sem, mr_sem, sts_sem, str_sem, xs_sem, xr_sem, ys_sem, yr_sem,
    exs_sem, exr_sem, eys_sem, eyr_sem,    sqs_sem, sqr_sem, dos_sem, dor_sem, los_sem, lor_sem, vys_sem, vyr_sem, vxs_sem, vxr_sem, tos_sem, tor_sem, os_sem, or_sem,
):
    core = lax.axis_index("section")
    seq = lax.axis_index("seq")
    voc = lax.axis_index("vocab")
    z, xh = seq // 2, seq % 2
    xl = voc % 2
    other = 1 - core
    half = nz // 2
    tok, width = hid.shape[1], hid.shape[2]
    rows, cols = head.shape[0], wbuf.shape[2]
    slice_width = xs.shape[3]
    plane = 2 * nv
    me = xh * nv + voc
    half_tok = tok // 2
    ny = nv // 2
    xi, yi = xh * 2 + xl, voc // 2

    def at(c, zz, hh, v):
        return (c, zz * 2 + hh, v)

    def plane_peer(index):
        return at(core, z, index // nv, index % nv)

    def in_plane(x, y):
        return at(core, z, x // 2, y * 2 + x % 2)

    mate = at(other, z, xh, voc)
    partner = at(core, z, 1 - xh, voc)
    partner_mate = at(other, z, 1 - xh, voc)
    near = at(core, z, 1 - xh, voc + 1 - 2 * xl)
    right = at(core, (z + 1) % nz, xh, voc)
    left = at(core, (z + nz - 1) % nz, xh, voc)
    barrier = pltpu.get_barrier_semaphore()
    direct = [mate, partner_mate, right, left]
    for peer in direct:
        pl.semaphore_signal(barrier, inc=1, device_id=peer, device_id_type=MESH)

    def greet(i, carry):
        pl.semaphore_signal(barrier, inc=1, device_id=plane_peer((me + i) % plane), device_id_type=MESH)
        return carry

    lax.fori_loop(1, plane, greet, 0)
    pl.semaphore_wait(barrier, len(direct) + plane - 1)

    def remote(src, dst, send, recv, peer):
        return pltpu.make_async_remote_copy(
            src_ref=src, dst_ref=dst, send_sem=send, recv_sem=recv, device_id=peer, device_id_type=MESH
        )

    sent = []

    def begin(copy):
        copy.start()
        sent.append(copy)

    part_rows = rows // 2

    def part_at(section, delta, part):
        zz = lax.rem(z + delta + nz, nz)
        hh = xh if part < 2 else 1 - xh
        start = (zz * 2 + hh) * rows + (part % 2) * part_rows
        return wbuf.at[section, pl.ds(pl.multiple_of(start, part_rows), part_rows), :]

    def own_columns(hh):
        return pl.ds(pl.multiple_of(hh * cols, cols), cols)

    own_block = head.at[:, own_columns(xh)]

    def own_part(part, hh):
        return head.at[pl.ds(part * part_rows, part_rows), own_columns(hh)]

    ring_parts = [
        [(k, part) for k in range(1, half) for part in range(4)] + [(half, 2 * way), (half, 2 * way + 1)]
        for way in (0, 1)
    ]
    ring_count = len(ring_parts[0])
    ring_copies = [[], []]

    def ring_send(way, i):
        k, part = ring_parts[way][i]
        slot = part_at(core, -(k - 1) if way == 0 else k - 1, part)
        src = own_part(part, xh) if k == 1 and part < 2 else slot
        held = []
        if k > 1:
            held = ring_wait(way, ring_parts[way].index((k - 1, part)))
        if i >= 1:
            ring_copies[way][i - 1].wait_send()
        copy = remote(src, slot, zs_sem.at[way, i], zr_sem.at[way, i], right if way == 0 else left)
        copy.start()
        ring_copies[way].append(copy)
        for come in held:
            mate_send(*come)

    arrived = [0, 0]

    def ring_wait(way, i):
        come = []
        while arrived[way] <= i:
            j = arrived[way]
            k, part = ring_parts[way][j]
            delta = -k if way == 0 else k
            slot = part_at(core, delta, part)
            remote(slot, slot, zs_sem.at[way, j], zr_sem.at[way, j], right).wait_recv()
            come.append((delta, part))
            arrived[way] += 1
        return come

    def mate_send(delta, part):
        slot = part_at(core, delta, part)
        src = own_part(part, xh) if delta == 0 and part < 2 else slot
        i = (delta % nz) * 4 + part
        begin(remote(src, slot, ds_sem.at[i], dr_sem.at[i], mate))

    def mate_wait(delta, part):
        slot = part_at(other, delta, part)
        i = (delta % nz) * 4 + part
        remote(slot, slot, ds_sem.at[i], dr_sem.at[i], mate).wait_recv()

    def partner_send(part):
        slot = part_at(core, 0, part)
        copy = remote(own_part(part, 1 - xh), slot, ms_sem.at[9 * part], mr_sem.at[9 * part], partner)
        copy.start()
        return copy

    def partner_wait(part):
        slot = part_at(core, 0, part + 2)
        remote(slot, slot, ms_sem.at[9 * part], mr_sem.at[9 * part], partner).wait_recv()
        mate_send(0, part + 2)

    my_rows = wbuf.at[core, pl.ds(pl.multiple_of(seq * rows, rows), rows), :]
    first = partner_send(0)
    for i in (0, 1):
        for way in (0, 1):
            ring_send(way, i)
        mate_send(0, i)

    local = [
        pltpu.make_async_copy(own_block, my_rows, loc_sem.at[0]),
        pltpu.make_async_copy(xin.at[0, :, core], xs.at[core], loc_sem.at[1]),
        pltpu.make_async_copy(gains.at[0], gs.at[core], loc_sem.at[2]),
        pltpu.make_async_copy(wspan.at[0], ws.at[core], loc_sem.at[3]),
        pltpu.make_async_copy(hidden.at[core], hid.at[xh], loc_sem.at[4]),
        pltpu.make_async_copy(teacher.at[core, :, own_columns(xh)], tea.at[core, xh], loc_sem.at[5]),
        pltpu.make_async_copy(targets, tgt.at[xh], loc_sem.at[6]),
    ]
    for copy in local:
        copy.start()
    begin(remote(xin.at[0, :, other], xs.at[core], ms_sem.at[1], mr_sem.at[1], mate))
    begin(remote(gains.at[0], gs.at[core], ms_sem.at[2], mr_sem.at[2], mate))
    begin(remote(wspan.at[0], ws.at[core], ms_sem.at[3], mr_sem.at[3], mate))
    begin(remote(teacher.at[other, :, own_columns(xh)], tea.at[core, xh], ms_sem.at[4], mr_sem.at[4], mate))

    first.wait_send()
    second = partner_send(1)
    partner_wait(0)
    for way in (0, 1):
        ring_send(way, 2)
    second.wait_send()
    begin(remote(hidden.at[core], hid.at[xh], ms_sem.at[5], mr_sem.at[5], near))
    begin(remote(targets, tgt.at[xh], ms_sem.at[6], mr_sem.at[6], partner))
    begin(remote(teacher.at[core, :, own_columns(1 - xh)], tea.at[core, xh], ms_sem.at[7], mr_sem.at[7], partner))
    begin(
        remote(teacher.at[other, :, own_columns(1 - xh)], tea.at[core, xh], ms_sem.at[8], mr_sem.at[8], partner_mate)
    )

    for copy in local:
        copy.wait()
    remote(xs.at[other], xs.at[other], ms_sem.at[1], mr_sem.at[1], mate).wait_recv()
    remote(gs.at[other], gs.at[other], ms_sem.at[2], mr_sem.at[2], mate).wait_recv()
    remote(ws.at[other], ws.at[other], ms_sem.at[3], mr_sem.at[3], mate).wait_recv()

    def saved(c):
        return xs[SPAN_AT[c]].astype(F32)

    def gain(c):
        section, slot_index = SPAN_AT[c]
        return gs[section, slot_index : slot_index + 1, :]

    def exchange(buf, send_sems, recv_sems):
        def send(i, carry):
            peer = at(core, z, xh, (voc + i) % nv)
            remote(buf.at[voc], buf.at[voc], send_sems.at[i], recv_sems.at[i], peer).start()
            return carry

        lax.fori_loop(1, nv, send, 0)

    def exchange_wait(buf, send_sems, recv_sems):
        def wait(i, carry):
            src = (voc + nv - i) % nv
            remote(buf.at[src], buf.at[src], send_sems.at[i], recv_sems.at[i], mate).wait_recv()
            remote(buf.at[voc], buf.at[voc], send_sems.at[i], recv_sems.at[i], mate).wait_send()
            return carry

        lax.fori_loop(1, nv, wait, 0)
        total = buf[0]
        for i in range(1, nv):
            total = total + buf[i]
        return total

    squares = []
    for c in range(4):
        value = saved(c)
        squares.append(jnp.sum(value * value, axis=1, keepdims=True))
    sq[voc] = to_rows(squares, 8)
    exchange(sq, sqs_sem, sqr_sem)
    def multiply(delta, first=False):
        zz = lax.rem(z + delta + nz, nz)
        span = pl.ds(pl.multiple_of(zz * 2 * rows, 2 * rows), 2 * rows)
        left_part = hid[:, :, span].reshape(2 * tok, 2 * rows)
        for s in (core, other):
            if s is other:
                for part in range(4):
                    mate_wait(delta, part)
            product = jnp.dot(left_part, wbuf[s, span, :], preferred_element_type=F32)
            if first:
                logits[s] = product
            else:
                logits[s] += product

    def hidden_wait():
        slot = hid.at[1 - xh]
        remote(slot, slot, ms_sem.at[5], mr_sem.at[5], near).wait_recv()

    def span_ready():
        inv_rows = lax.rsqrt(exchange_wait(sq, sqs_sem, sqr_sem) / width + EPS)
        total = to_columns(inv_rows)
        inv = [total[:, c : c + 1] for c in range(4)]

        def back(c, value):
            return value + inv[c] * heads_dot((value * gain(c)).astype(BF16), ws[SPAN_AT[c]], False)

        def inner(c, value):
            return jnp.sum(saved(c) * inv[c] ** 3 * value, axis=1, keepdims=True)

        products = []
        for c in range(4):
            value = heads_dot((saved(c) * gain(c)).astype(BF16), ws[SPAN_AT[c]], False)
            for upper in range(c + 1, 4):
                products.append(inner(upper, value))
                value = back(upper, value)
            vec_y[yi, c] = value[:half_tok].astype(BF16)
            vec_x[xi, c] = value[half_tok:].astype(BF16)
        dots[voc] = to_rows(products, 8)
        exchange(dots, dos_sem, dor_sem)
        return inv, inv_rows

    def vectors_y_send():
        for oy in range(1, ny):
            begin(remote(vec_y.at[yi], vec_y.at[yi], vys_sem.at[oy], vyr_sem.at[oy], in_plane(xi, (yi + oy) % ny)))

    def vectors_x_send():
        for ox in range(1, 4):
            begin(remote(vec_x.at[xi], vec_x.at[xi], vxs_sem.at[ox], vxr_sem.at[ox], in_plane((xi + ox) % 4, yi)))

    def vectors_wait():
        for oy in range(1, ny):
            slot = vec_y.at[(yi + ny - oy) % ny]
            remote(slot, slot, vys_sem.at[oy], vyr_sem.at[oy], mate).wait_recv()
        for ox in range(1, 4):
            slot = vec_x.at[(xi + 4 - ox) % 4]
            remote(slot, slot, vxs_sem.at[ox], vxr_sem.at[ox], mate).wait_recv()

    def teacher_ready():
        pairs = ((other, xh, 4, mate), (core, 1 - xh, 7, partner), (other, 1 - xh, 8, partner_mate))
        for s, hh, i, peer in pairs:
            slot = tea.at[s, hh]
            remote(slot, slot, ms_sem.at[i], mr_sem.at[i], peer).wait_recv()
        slot = tgt.at[1 - xh]
        remote(slot, slot, ms_sem.at[6], mr_sem.at[6], partner).wait_recv()
        values = [tea[s].reshape(2 * tok, cols).astype(F32) for s in (0, 1)]
        top = jnp.max(jnp.maximum(values[0], values[1]), axis=1, keepdims=True)
        total = jnp.zeros((2 * tok, 1), F32)
        for s in (0, 1):
            value = jnp.exp(values[s] - top)
            texp[s] = value
            total += jnp.sum(value, axis=1, keepdims=True)
        return top, total

    partner_wait(1)
    for way in (0, 1):
        ring_send(way, 3)
    for i in range(4, ring_count):
        for way in (0, 1):
            ring_send(way, i)
        if i == 5:
            inv, inv_rows = span_ready()
            vectors_y_send()
        if i == ring_count - 2:
            teacher_top, teacher_total = teacher_ready()
            hidden_wait()
            vectors_x_send()
            multiply(0, first=True)
            for d in range(1, half - 2):
                multiply(-d)
                multiply(d)
    for i in range(ring_count - 4, ring_count):
        for way in (0, 1):
            for come in ring_wait(way, i):
                mate_send(*come)
        if i == ring_count - 4:
            for d in range(max(1, half - 2), half - 1):
                multiply(-d)
                multiply(d)
        if i == ring_count - 3:
            multiply(1 - half)
            multiply(half - 1)
    multiply(half)

    def target_column():
        parts = []
        for hh in (0, 1):
            row = jnp.where(core == 0, tgt[hh, 0:1, :], tgt[hh, 1:2, :])
            parts.append(jnp.broadcast_to(row, (128, tok)).T[:, 0:1])
        return jnp.concatenate(parts, axis=0)

    wanted = target_column()

    def hit(s):
        start = (s * nv + voc) * 2 * cols + xh * cols
        return wanted - start == lax.broadcasted_iota(jnp.int32, (2 * tok, cols), 1)

    student_top = jnp.max(jnp.maximum(logits[0], logits[1]), axis=1, keepdims=True)
    student_total = jnp.zeros((2 * tok, 1), F32)
    cross = jnp.zeros((2 * tok, 1), F32)
    target_logit = jnp.zeros((2 * tok, 1), F32)
    for s in (0, 1):
        value = logits[s]
        cross += jnp.sum(texp[s] * (tea[s].reshape(2 * tok, cols).astype(F32) - value), axis=1, keepdims=True)
        target_logit += jnp.sum(jnp.where(hit(s), value, 0.0), axis=1, keepdims=True)
        value = jnp.exp(value - student_top)
        logits[s] = value
        student_total += jnp.sum(value, axis=1, keepdims=True)
    stats[me] = to_rows([student_top, student_total, teacher_top, teacher_total, cross, target_logit], 8)

    def stats_send(i, carry):
        peer = plane_peer((me + i) % plane)
        remote(stats.at[me], stats.at[me], sts_sem.at[i], str_sem.at[i], peer).start()
        return carry

    def stats_wait(i, carry):
        src = (me + plane - i) % plane
        remote(stats.at[src], stats.at[src], sts_sem.at[i], str_sem.at[i], mate).wait_recv()
        remote(stats.at[me], stats.at[me], sts_sem.at[i], str_sem.at[i], mate).wait_send()
        return carry

    lax.fori_loop(1, plane, stats_send, 0)
    for copies in ring_copies:
        for copy in copies[-1:]:
            copy.wait_send()
    for copy in sent:
        copy.wait_send()
    sent.clear()
    lax.fori_loop(1, plane, stats_wait, 0)
    top_s, top_t = stats[0, 0:1, :], stats[0, 2:3, :]
    for i in range(1, plane):
        top_s = jnp.maximum(top_s, stats[i, 0:1, :])
        top_t = jnp.maximum(top_t, stats[i, 2:3, :])
    sum_s, sum_t, sum_x, sum_l = (jnp.zeros_like(top_s) for _ in range(4))
    for i in range(plane):
        part = stats[i]
        sum_s += part[1:2] * jnp.exp(part[0:1] - top_s)
        factor = jnp.exp(part[2:3] - top_t)
        sum_t += part[3:4] * factor
        sum_x += part[4:5] * factor
        sum_l += part[5:6]
    lse_s = top_s + jnp.log(sum_s)
    lse_t = top_t + jnp.log(sum_t)
    terms = sum_x / sum_t - lse_t + lse_s + CE_WEIGHT * (lse_s - sum_l)
    scales = to_columns(jnp.concatenate([lse_s, lse_t], axis=0))
    student_scale = jnp.exp(student_top - scales[:, 0:1])
    teacher_scale = jnp.exp(teacher_top - scales[:, 1:2])

    own_loss[0] = jnp.broadcast_to(jnp.sum(terms, axis=1, keepdims=True), (8, 128))
    begin(remote(own_loss.at[0], own_loss.at[1], los_sem.at[0, 0], lor_sem.at[0, 0], mate))

    def loss_start():
        remote(own_loss.at[1], own_loss.at[1], los_sem.at[0, 0], lor_sem.at[0, 0], mate).wait_recv()
        losses[z] = own_loss[0] + own_loss[1]
        loss_send(1)

    def loss_send(k):
        for way, peer in ((0, right), (1, left)):
            if k < half or way == 0:
                slot = losses.at[(z + nz - (k - 1)) % nz if way == 0 else (z + k - 1) % nz]
                begin(remote(slot, slot, los_sem.at[way, k], lor_sem.at[way, k], peer))

    def loss_wait(k):
        for way in (0, 1):
            if k < half or way == 0:
                slot = losses.at[(z + nz - k) % nz if way == 0 else (z + k) % nz]
                remote(slot, slot, los_sem.at[way, k], lor_sem.at[way, k], right).wait_recv()
        if k < half:
            loss_send(k + 1)

    for s in (0, 1):
        value = (1.0 + CE_WEIGHT) * (logits[s] * student_scale) - texp[s] * teacher_scale
        value = value - jnp.where(hit(s), CE_WEIGHT, 0.0)
        dlog[s] = (LOSS_SCALE * value).astype(BF16)

    quarter = tok // 4
    upper, lower = pl.ds(0, quarter), pl.ds(quarter, quarter)
    nt = (((1,), (1,)), ((), ()))

    def x_peer(step):
        return in_plane((xi + step + 4) % 4, yi)

    def y_peer(step):
        return in_plane(xi, (yi + step + ny) % ny)

    def stage_x(kind, way, y):
        step = 1 - 2 * way
        part = (upper, lower)[way if kind != 1 else 1 - way]
        source = snd_x.at[(xi + 2) % 4 if kind == 0 else (xi + step + 4) % 4, y, part]
        target = pass_x.at[way, y] if kind == 0 else rcv_x.at[way, y, part]
        return remote(source, target, xs_sem.at[kind, way, y], xr_sem.at[kind, way, y], x_peer(step))

    def stage_y(kind, way, x):
        step = 1 - 2 * way
        part = (upper, lower)[way if kind != 1 else 1 - way]
        source = snd_y.at[(yi + 2) % ny if kind == 0 else (yi + step + ny) % ny, x, part]
        target = pass_y.at[way, x] if kind == 0 else rcv_y.at[way, x, part]
        return remote(source, target, ys_sem.at[kind, way, x], yr_sem.at[kind, way, x], y_peer(step))

    def offset(i):
        return jnp.where(i == 0, 2, jnp.where(i == 1, 1, jnp.where(i == 2, 3, 0)))

    def slice_turn(i, carry):
        oy = offset(i // 2)
        y = (yi + oy) % ny
        lo = (xl + i) % 2
        v = y * 2 + lo
        span = pl.ds(pl.multiple_of(v * slice_width, slice_width), slice_width)
        part = lax.dot_general(dlog[0], wbuf[0, span, :], nt, preferred_element_type=F32)
        part += lax.dot_general(dlog[1], wbuf[1, span, :], nt, preferred_element_type=F32)
        part = part.astype(BF16)
        for hh in (0, 1):
            x = hh * 2 + lo
            snd_x[x, y] = part[hh * tok : hh * tok + half_tok]
            snd_y[y, x] = part[hh * tok + half_tok : (hh + 1) * tok]

        @pl.when(i % 2 == 0)
        def _():
            for way in (0, 1):
                stage_x(0, way, y).start()

        @pl.when(i % 2 == 1)
        def _():
            for way in (0, 1):
                stage_x(1, way, y).start()

        for hh in (0, 1):

            @pl.when(oy == 2)
            def _():
                for way in (0, 1):
                    stage_y(0, way, hh * 2 + lo).start()

            @pl.when(oy == 1)
            def _():
                stage_y(1, 0, hh * 2 + lo).start()

            @pl.when(oy == 3)
            def _():
                stage_y(1, 1, hh * 2 + lo).start()

        return carry

    lax.fori_loop(0, nv, slice_turn, 0)

    def pass_turn(i, carry):
        y = (yi + offset(i)) % ny
        for way in (0, 1):
            step = 1 - 2 * way
            part = (upper, lower)[way]
            stage_x(0, way, y).wait_recv()
            x = (xi + step + 4) % 4
            total = snd_x[x, y, part].astype(F32) + pass_x[way, y].astype(F32)
            snd_x[x, y, part] = total.astype(BF16)
            stage_x(2, way, y).start()
            stage_y(0, way, i).wait_recv()
            to = (yi + step + ny) % ny
            total = snd_y[to, i, part].astype(F32) + pass_y[way, i].astype(F32)
            snd_y[to, i, part] = total.astype(BF16)
            stage_y(2, way, i).start()
        return carry

    lax.fori_loop(0, ny, pass_turn, 0)
    loss_start()
    vectors_wait()
    cross_rows = exchange_wait(dots, dos_sem, dor_sem)

    def sum_x(oy):
        y = (yi + oy) % ny
        total = snd_x[xi, y].astype(F32)
        for way in (0, 1):
            for kind in (1, 2):
                stage_x(kind, way, y).wait_recv()
            total = total + rcv_x[way, y].astype(F32)
        return total

    def sum_y(ox):
        x = (xi + ox) % 4
        total = snd_y[yi, x].astype(F32)
        for way in (0, 1):
            for kind in (1, 2):
                stage_y(kind, way, x).wait_recv()
            total = total + rcv_y[way, x].astype(F32)
        return total

    def fold(value):
        parts = [value[:, i : i + 128] for i in range(0, slice_width, 128)]
        return functools.reduce(lambda a, b: a + b, parts)

    def products_with(vectors, value):
        return [fold(vectors[c].astype(F32) * value) for c in range(4)]

    def add(left_list, right_list):
        return [a + b for a, b in zip(left_list, right_list)]

    first_products = [jnp.zeros((half_tok, 128), F32)] * 4
    for oy in (2, 1, 3):
        value = sum_x(oy)
        two_y[oy] = value.astype(BF16)
        begin(remote(two_y.at[oy], end_y.at[oy], eys_sem.at[oy], eyr_sem.at[oy], in_plane(xi, (yi + oy) % ny)))
        first_products = add(first_products, products_with(vec_y[(yi + oy) % ny], value))
    loss_wait(1)
    first_half = sum_x(0)
    first_products = add(first_products, products_with(vec_y[yi], first_half))
    column_sums = {}
    for ox in range(1, 4):
        column_sums[ox] = sum_y(ox)
        two_x[ox] = column_sums[ox].astype(BF16)
    second_half = sum_y(0)
    column_sums[0] = second_half
    near_products = [jnp.zeros((half_tok, 128), F32)] * 4
    away_products = near_products
    for ox in range(4):
        x = (xi + ox) % 4
        found = products_with(vec_x[x], column_sums[ox])
        same = x // 2 == xh
        near_products = [a + jnp.where(same, b, 0.0) for a, b in zip(near_products, found)]
        away_products = [a + jnp.where(same, 0.0, b) for a, b in zip(away_products, found)]

    def message(first_part, second_part):
        columns = [
            jnp.sum(jnp.concatenate([a, b], axis=0), axis=1, keepdims=True) for a, b in zip(first_part, second_part)
        ]
        return to_rows(columns, 8)

    away = message([jnp.zeros((half_tok, 128), F32)] * 4, away_products)
    close = message(first_products, near_products)
    told[0] = jnp.where(xh == 0, close, away)
    told[1] = jnp.where(xh == 0, away, close)

    def told_send(i, carry):
        to = (me + i) % plane
        remote(told.at[to // nv], heard.at[me], tos_sem.at[i], tor_sem.at[i], plane_peer(to)).start()
        return carry

    def told_wait(i, carry):
        src = (me + plane - i) % plane
        remote(heard.at[src], heard.at[src], tos_sem.at[i], tor_sem.at[i], mate).wait_recv()
        remote(told.at[0], heard.at[me], tos_sem.at[i], tor_sem.at[i], mate).wait_send()
        return carry

    lax.fori_loop(1, plane, told_send, 0)
    for ox in (2, 1, 3):
        begin(remote(two_x.at[ox], end_x.at[ox], exs_sem.at[ox], exr_sem.at[ox], in_plane((xi + ox) % 4, yi)))
    heard[me] = close

    def slice_sent(i, carry):
        for kind in range(3):
            for way in (0, 1):
                stage_x(kind, way, i).wait_send()
                stage_y(kind, way, i).wait_send()
        return carry

    lax.fori_loop(0, ny, slice_sent, 0)

    loss_wait(2)
    for oy in range(1, ny):
        remote(end_y.at[oy], end_y.at[oy], eys_sem.at[oy], eyr_sem.at[oy], mate).wait_recv()
        first_half = first_half + end_y[oy].astype(F32)
    for ox in range(1, 4):
        remote(end_x.at[ox], end_x.at[ox], exs_sem.at[ox], exr_sem.at[ox], mate).wait_recv()
        second_half = second_half + end_x[ox].astype(F32)
    cotangent = jnp.concatenate([first_half.astype(BF16), second_half.astype(BF16)], axis=0)

    lax.fori_loop(1, plane, told_wait, 0)
    found = heard[0]
    for i in range(1, plane):
        found = found + heard[i]
    d0, d1, d2, d3 = (found[c : c + 1] / width for c in range(4))
    e10, e20, e30, e21, e31, e32 = (cross_rows[c : c + 1] / width for c in range(6))
    s3 = d3
    s2 = d2 - s3 * e32
    s1 = d1 - s3 * e31 - s2 * e21
    s0 = d0 - s3 * e30 - s2 * e20 - s1 * e10
    pull = to_columns(inv_rows[0:4] ** 3 * jnp.concatenate([s0, s1, s2, s3], axis=0))
    value = cotangent

    def hand_out(slot_index):
        pltpu.make_async_copy(ys.at[core, slot_index], out.at[0, slot_index, core], loc_sem.at[slot_index]).start()
        begin(
            remote(
                ys.at[other, slot_index], out.at[0, slot_index, core], os_sem.at[slot_index], or_sem.at[slot_index], mate
            )
        )

    for c in (3, 2, 1, 0):
        grad = heads_dot(value, ws[SPAN_AT[c]], True)
        fresh = value.astype(F32) + inv[c] * gain(c) * grad - saved(c) * pull[:, c : c + 1]
        value = fresh.astype(BF16)
        ys[SPAN_AT[c]] = value
        if c == 2:
            hand_out(1)
    hand_out(0)
    for k in range(3, half + 1):
        loss_wait(k)
    loss_total = losses[0]
    for i in range(1, nz):
        loss_total = loss_total + losses[i]
    loss_ref[0, 0] = jnp.max(loss_total) / (4 * tok * nz)
    for slot_index in (1, 0):
        pltpu.make_async_copy(
            ys.at[core, slot_index], out.at[0, slot_index, core], loc_sem.at[slot_index]
        ).wait()
        slot = out.at[0, slot_index, other]
        remote(slot, slot, os_sem.at[slot_index], or_sem.at[slot_index], mate).wait_recv()
    for copy in sent:
        copy.wait_send()


def solution(mesh):
    n_seq, n_voc = mesh.shape["seq"], mesh.shape["vocab"]
    nz = n_seq // 2

    def per_device(hidden, head_weight, teacher_logits, targets, span_inputs, span_gains, span_weights):
        _, tok, width = hidden.shape
        rows, shard = head_weight.shape
        cols = shard // 2
        slice_width = span_inputs.shape[4]
        heads = span_weights.shape[2]
        plane = 2 * n_voc
        half = nz // 2
        dma = pltpu.SemaphoreType.DMA
        any_space = pl.BlockSpec(memory_space=pl.ANY)
        operands = [
            pltpu.with_memory_space_constraint(a, pltpu.HBM)
            for a in (hidden, head_weight, teacher_logits, targets, span_inputs, span_gains, span_weights)
        ]
        grads, loss = pl.pallas_call(
            functools.partial(kernel, nz, n_voc),
            out_shape=(
                jax.ShapeDtypeStruct((1, 2, 2, tok, slice_width), BF16),
                jax.ShapeDtypeStruct((1, 1), F32),
            ),
            in_specs=[any_space] * 7,
            out_specs=(any_space, pl.BlockSpec(memory_space=pltpu.SMEM)),
            scratch_shapes=[
                pltpu.VMEM((2, width, cols), BF16),
                pltpu.VMEM((2, tok, width), BF16),
                pltpu.VMEM((2, 2, tok, cols), BF16),
                pltpu.VMEM((2, 2, tok), jnp.int32),
                pltpu.VMEM((2, 2 * tok, cols), F32),
                pltpu.VMEM((2, 2 * tok, cols), F32),
                pltpu.VMEM((2, 2 * tok, cols), BF16),
                pltpu.VMEM((plane, 8, 2 * tok), F32),
                pltpu.VMEM((4, n_voc // 2, tok // 2, slice_width), BF16),
                pltpu.VMEM((2, n_voc // 2, tok // 2, slice_width), BF16),
                pltpu.VMEM((2, n_voc // 2, tok // 4, slice_width), BF16),
                pltpu.VMEM((n_voc // 2, 4, tok // 2, slice_width), BF16),
                pltpu.VMEM((2, 4, tok // 2, slice_width), BF16),
                pltpu.VMEM((2, 4, tok // 4, slice_width), BF16),
                pltpu.VMEM((4, tok // 2, slice_width), BF16),
                pltpu.VMEM((4, tok // 2, slice_width), BF16),
                pltpu.VMEM((n_voc // 2, tok // 2, slice_width), BF16),
                pltpu.VMEM((n_voc // 2, tok // 2, slice_width), BF16),
                pltpu.VMEM((2, 2, tok, slice_width), BF16),
                pltpu.VMEM((2, 2, slice_width), F32),
                pltpu.VMEM((2, 2, heads, HEAD, HEAD), BF16),
                pltpu.VMEM((n_voc, 8, tok), F32),
                pltpu.VMEM((n_voc, 8, tok), F32),
                pltpu.VMEM((n_voc // 2, 4, tok // 2, slice_width), BF16),
                pltpu.VMEM((4, 4, tok // 2, slice_width), BF16),
                pltpu.VMEM((2, 8, tok), F32),
                pltpu.VMEM((plane, 8, tok), F32),
                pltpu.VMEM((2, 8, 128), F32),
                pltpu.VMEM((nz, 8, 128), F32),
                pltpu.VMEM((2, 2, tok, slice_width), BF16),
                dma((7,)),
                dma((2, 4 * half - 2)),
                dma((2, 4 * half - 2)),
                dma((4 * nz,)),
                dma((4 * nz,)),
                dma((10,)),
                dma((10,)),
                dma((plane,)),
                dma((plane,)),
                dma((3, 2, n_voc // 2)),
                dma((3, 2, n_voc // 2)),
                dma((3, 2, 4)),
                dma((3, 2, 4)),
                dma((4,)),
                dma((4,)),
                dma((n_voc // 2,)),
                dma((n_voc // 2,)),
                dma((n_voc,)),
                dma((n_voc,)),
                dma((n_voc,)),
                dma((n_voc,)),
                dma((2, half + 1)),
                dma((2, half + 1)),
                dma((n_voc // 2,)),
                dma((n_voc // 2,)),
                dma((4,)),
                dma((4,)),
                dma((plane,)),
                dma((plane,)),
                dma((2,)),
                dma((2,)),
            ],
            compiler_params=pltpu.CompilerParams(
                collective_id=0, has_side_effects=True, vmem_limit_bytes=48 * 1024 * 1024
            ),
        )(*operands)
        return grads, loss.reshape(())

    placed = (
        P(None, "seq", None),
        P("seq", ("section", "vocab")),
        P(None, "seq", ("section", "vocab")),
        P(None, "seq"),
        P("section", None, None, "seq", "vocab"),
        P("section", None, "vocab"),
        P("section", None, "vocab", None, None),
    )
    return jax.shard_map(
        per_device,
        mesh=mesh,
        in_specs=placed,
        out_specs=(P("section", None, None, "seq", "vocab"), P()),
        check_vma=False,
    )
```

```python
import functools

import jax
import jax.numpy as jnp
from jax import lax
from jax.experimental import pallas as pl
from jax.experimental.pallas import tpu as pltpu
from jax.sharding import PartitionSpec as P

MESH = pl.DeviceIdType.MESH
F32 = jnp.float32
BF16 = jnp.bfloat16
LOSS_SCALE = 16
CE_WEIGHT = 0.5
EPS = 1e-06
HEAD = 128
SPAN_AT = ((0, 0), (1, 0), (1, 1), (0, 1))


def to_rows(columns, height):
    count = columns[0].shape[0]
    lane = lax.broadcasted_iota(jnp.int32, (count, 128), 1)
    wide = jnp.zeros((count, 128), F32)
    for i, column in enumerate(columns):
        wide = jnp.where(lane == i, column, wide)
    return wide.T[:height]


def to_columns(rows):
    height, count = rows.shape
    return jnp.concatenate([rows, jnp.zeros((128 - height, count), F32)], axis=0).T


def heads_dot(left, weights, transposed):
    dims = (((1,), (1,)), ((), ())) if transposed else (((1,), (0,)), ((), ()))
    parts = []
    for h in range(weights.shape[0]):
        parts.append(
            lax.dot_general(left[:, h * HEAD : (h + 1) * HEAD], weights[h], dims, preferred_element_type=F32)
        )
    return jnp.concatenate(parts, axis=1)


def kernel(
    nz, nv,
    hidden, head, teacher, targets, xin, gains, wspan,
    out, loss_ref,
    wbuf, hid, tea, tgt, logits, texp, dlog, stats, snd_x, rcv_x, pass_x, snd_y, rcv_y, pass_y, two_x, end_x, two_y, end_y, xs, gs, ws,
    sq, dots, vec_y, vec_x, told, heard, own_loss, losses, ys,
    loc_sem, zs_sem, zr_sem, ds_sem, dr_sem, ms_sem, mr_sem, sts_sem, str_sem, xs_sem, xr_sem, ys_sem, yr_sem,
    exs_sem, exr_sem, eys_sem, eyr_sem,    sqs_sem, sqr_sem, dos_sem, dor_sem, los_sem, lor_sem, vys_sem, vyr_sem, vxs_sem, vxr_sem, tos_sem, tor_sem, os_sem, or_sem,
):
    core = lax.axis_index("section")
    seq = lax.axis_index("seq")
    voc = lax.axis_index("vocab")
    z, xh = seq // 2, seq % 2
    xl = voc % 2
    other = 1 - core
    half = nz // 2
    tok, width = hid.shape[1], hid.shape[2]
    rows, cols = head.shape[0], wbuf.shape[2]
    slice_width = xs.shape[3]
    plane = 2 * nv
    me = xh * nv + voc
    half_tok = tok // 2
    ny = nv // 2
    xi, yi = xh * 2 + xl, voc // 2

    def at(c, zz, hh, v):
        return (c, zz * 2 + hh, v)

    def plane_peer(index):
        return at(core, z, index // nv, index % nv)

    def in_plane(x, y):
        return at(core, z, x // 2, y * 2 + x % 2)

    mate = at(other, z, xh, voc)
    partner = at(core, z, 1 - xh, voc)
    partner_mate = at(other, z, 1 - xh, voc)
    near = at(core, z, 1 - xh, voc + 1 - 2 * xl)
    right = at(core, (z + 1) % nz, xh, voc)
    left = at(core, (z + nz - 1) % nz, xh, voc)
    barrier = pltpu.get_barrier_semaphore()
    direct = [mate, partner_mate, right, left]
    for peer in direct:
        pl.semaphore_signal(barrier, inc=1, device_id=peer, device_id_type=MESH)

    def greet(i, carry):
        pl.semaphore_signal(barrier, inc=1, device_id=plane_peer((me + i) % plane), device_id_type=MESH)
        return carry

    lax.fori_loop(1, plane, greet, 0)
    pl.semaphore_wait(barrier, len(direct) + plane - 1)

    def remote(src, dst, send, recv, peer):
        return pltpu.make_async_remote_copy(
            src_ref=src, dst_ref=dst, send_sem=send, recv_sem=recv, device_id=peer, device_id_type=MESH
        )

    sent = []

    def begin(copy):
        copy.start()
        sent.append(copy)

    part_rows = rows // 2

    def part_at(section, delta, part):
        zz = lax.rem(z + delta + nz, nz)
        hh = xh if part < 2 else 1 - xh
        start = (zz * 2 + hh) * rows + (part % 2) * part_rows
        return wbuf.at[section, pl.ds(pl.multiple_of(start, part_rows), part_rows), :]

    def own_columns(hh):
        return pl.ds(pl.multiple_of(hh * cols, cols), cols)

    own_block = head.at[:, own_columns(xh)]

    def own_part(part, hh):
        return head.at[pl.ds(part * part_rows, part_rows), own_columns(hh)]

    ring_parts = [
        [(k, part) for k in range(1, half) for part in range(4)] + [(half, 2 * way), (half, 2 * way + 1)]
        for way in (0, 1)
    ]
    ring_count = len(ring_parts[0])
    ring_copies = [[], []]

    def ring_send(way, i):
        k, part = ring_parts[way][i]
        slot = part_at(core, -(k - 1) if way == 0 else k - 1, part)
        src = own_part(part, xh) if k == 1 and part < 2 else slot
        held = []
        if k > 1:
            held = ring_wait(way, ring_parts[way].index((k - 1, part)))
        if i >= 3:
            ring_copies[way][i - 3].wait_send()
        copy = remote(src, slot, zs_sem.at[way, i], zr_sem.at[way, i], right if way == 0 else left)
        copy.start()
        ring_copies[way].append(copy)
        for come in held:
            mate_send(*come)

    arrived = [0, 0]

    def ring_wait(way, i):
        come = []
        while arrived[way] <= i:
            j = arrived[way]
            k, part = ring_parts[way][j]
            delta = -k if way == 0 else k
            slot = part_at(core, delta, part)
            remote(slot, slot, zs_sem.at[way, j], zr_sem.at[way, j], right).wait_recv()
            come.append((delta, part))
            arrived[way] += 1
        return come

    def mate_send(delta, part):
        slot = part_at(core, delta, part)
        src = own_part(part, xh) if delta == 0 and part < 2 else slot
        i = (delta % nz) * 4 + part
        begin(remote(src, slot, ds_sem.at[i], dr_sem.at[i], mate))

    def mate_wait(delta, part):
        slot = part_at(other, delta, part)
        i = (delta % nz) * 4 + part
        remote(slot, slot, ds_sem.at[i], dr_sem.at[i], mate).wait_recv()

    def partner_send(part):
        slot = part_at(core, 0, part)
        copy = remote(own_part(part, 1 - xh), slot, ms_sem.at[9 * part], mr_sem.at[9 * part], partner)
        copy.start()
        return copy

    def partner_wait(part):
        slot = part_at(core, 0, part + 2)
        remote(slot, slot, ms_sem.at[9 * part], mr_sem.at[9 * part], partner).wait_recv()
        mate_send(0, part + 2)

    my_rows = wbuf.at[core, pl.ds(pl.multiple_of(seq * rows, rows), rows), :]
    first = partner_send(0)
    for i in (0, 1):
        for way in (0, 1):
            ring_send(way, i)
        mate_send(0, i)

    local = [
        pltpu.make_async_copy(own_block, my_rows, loc_sem.at[0]),
        pltpu.make_async_copy(xin.at[0, :, core], xs.at[core], loc_sem.at[1]),
        pltpu.make_async_copy(gains.at[0], gs.at[core], loc_sem.at[2]),
        pltpu.make_async_copy(wspan.at[0], ws.at[core], loc_sem.at[3]),
        pltpu.make_async_copy(hidden.at[core], hid.at[xh], loc_sem.at[4]),
        pltpu.make_async_copy(teacher.at[core, :, own_columns(xh)], tea.at[core, xh], loc_sem.at[5]),
        pltpu.make_async_copy(targets, tgt.at[xh], loc_sem.at[6]),
    ]
    for copy in local:
        copy.start()
    begin(remote(xin.at[0, :, other], xs.at[core], ms_sem.at[1], mr_sem.at[1], mate))
    begin(remote(gains.at[0], gs.at[core], ms_sem.at[2], mr_sem.at[2], mate))
    begin(remote(wspan.at[0], ws.at[core], ms_sem.at[3], mr_sem.at[3], mate))
    begin(remote(teacher.at[other, :, own_columns(xh)], tea.at[core, xh], ms_sem.at[4], mr_sem.at[4], mate))

    first.wait_send()
    second = partner_send(1)
    partner_wait(0)
    for way in (0, 1):
        ring_send(way, 2)
    second.wait_send()
    begin(remote(hidden.at[core], hid.at[xh], ms_sem.at[5], mr_sem.at[5], near))
    begin(remote(targets, tgt.at[xh], ms_sem.at[6], mr_sem.at[6], partner))
    begin(remote(teacher.at[core, :, own_columns(1 - xh)], tea.at[core, xh], ms_sem.at[7], mr_sem.at[7], partner))
    begin(
        remote(teacher.at[other, :, own_columns(1 - xh)], tea.at[core, xh], ms_sem.at[8], mr_sem.at[8], partner_mate)
    )

    for copy in local:
        copy.wait()
    remote(xs.at[other], xs.at[other], ms_sem.at[1], mr_sem.at[1], mate).wait_recv()
    remote(gs.at[other], gs.at[other], ms_sem.at[2], mr_sem.at[2], mate).wait_recv()
    remote(ws.at[other], ws.at[other], ms_sem.at[3], mr_sem.at[3], mate).wait_recv()

    def saved(c):
        return xs[SPAN_AT[c]].astype(F32)

    def gain(c):
        section, slot_index = SPAN_AT[c]
        return gs[section, slot_index : slot_index + 1, :]

    def exchange(buf, send_sems, recv_sems):
        def send(i, carry):
            peer = at(core, z, xh, (voc + i) % nv)
            remote(buf.at[voc], buf.at[voc], send_sems.at[i], recv_sems.at[i], peer).start()
            return carry

        lax.fori_loop(1, nv, send, 0)

    def exchange_wait(buf, send_sems, recv_sems):
        def wait(i, carry):
            src = (voc + nv - i) % nv
            remote(buf.at[src], buf.at[src], send_sems.at[i], recv_sems.at[i], mate).wait_recv()
            remote(buf.at[voc], buf.at[voc], send_sems.at[i], recv_sems.at[i], mate).wait_send()
            return carry

        lax.fori_loop(1, nv, wait, 0)
        total = buf[0]
        for i in range(1, nv):
            total = total + buf[i]
        return total

    squares = []
    for c in range(4):
        value = saved(c)
        squares.append(jnp.sum(value * value, axis=1, keepdims=True))
    sq[voc] = to_rows(squares, 8)
    exchange(sq, sqs_sem, sqr_sem)
    def multiply(delta, first=False):
        zz = lax.rem(z + delta + nz, nz)
        span = pl.ds(pl.multiple_of(zz * 2 * rows, 2 * rows), 2 * rows)
        left_part = hid[:, :, span].reshape(2 * tok, 2 * rows)
        for s in (core, other):
            if s is other:
                for part in range(4):
                    mate_wait(delta, part)
            product = jnp.dot(left_part, wbuf[s, span, :], preferred_element_type=F32)
            if first:
                logits[s] = product
            else:
                logits[s] += product

    def hidden_wait():
        slot = hid.at[1 - xh]
        remote(slot, slot, ms_sem.at[5], mr_sem.at[5], near).wait_recv()

    def span_ready():
        inv_rows = lax.rsqrt(exchange_wait(sq, sqs_sem, sqr_sem) / width + EPS)
        total = to_columns(inv_rows)
        inv = [total[:, c : c + 1] for c in range(4)]

        def back(c, value):
            return value + inv[c] * heads_dot((value * gain(c)).astype(BF16), ws[SPAN_AT[c]], False)

        def inner(c, value):
            return jnp.sum(saved(c) * inv[c] ** 3 * value, axis=1, keepdims=True)

        products = []
        for c in range(4):
            value = heads_dot((saved(c) * gain(c)).astype(BF16), ws[SPAN_AT[c]], False)
            for upper in range(c + 1, 4):
                products.append(inner(upper, value))
                value = back(upper, value)
            vec_y[yi, c] = value[:half_tok].astype(BF16)
            vec_x[xi, c] = value[half_tok:].astype(BF16)
        dots[voc] = to_rows(products, 8)
        exchange(dots, dos_sem, dor_sem)
        return inv, inv_rows

    def vectors_y_send():
        for oy in range(1, ny):
            begin(remote(vec_y.at[yi], vec_y.at[yi], vys_sem.at[oy], vyr_sem.at[oy], in_plane(xi, (yi + oy) % ny)))

    def vectors_x_send():
        for ox in range(1, 4):
            begin(remote(vec_x.at[xi], vec_x.at[xi], vxs_sem.at[ox], vxr_sem.at[ox], in_plane((xi + ox) % 4, yi)))

    def vectors_wait():
        for oy in range(1, ny):
            slot = vec_y.at[(yi + ny - oy) % ny]
            remote(slot, slot, vys_sem.at[oy], vyr_sem.at[oy], mate).wait_recv()
        for ox in range(1, 4):
            slot = vec_x.at[(xi + 4 - ox) % 4]
            remote(slot, slot, vxs_sem.at[ox], vxr_sem.at[ox], mate).wait_recv()

    def teacher_ready():
        pairs = ((other, xh, 4, mate), (core, 1 - xh, 7, partner), (other, 1 - xh, 8, partner_mate))
        for s, hh, i, peer in pairs:
            slot = tea.at[s, hh]
            remote(slot, slot, ms_sem.at[i], mr_sem.at[i], peer).wait_recv()
        slot = tgt.at[1 - xh]
        remote(slot, slot, ms_sem.at[6], mr_sem.at[6], partner).wait_recv()
        values = [tea[s].reshape(2 * tok, cols).astype(F32) for s in (0, 1)]
        top = jnp.max(jnp.maximum(values[0], values[1]), axis=1, keepdims=True)
        total = jnp.zeros((2 * tok, 1), F32)
        for s in (0, 1):
            value = jnp.exp(values[s] - top)
            texp[s] = value
            total += jnp.sum(value, axis=1, keepdims=True)
        return top, total

    partner_wait(1)
    for way in (0, 1):
        ring_send(way, 3)
    for i in range(4, ring_count):
        for way in (0, 1):
            ring_send(way, i)
        if i == 5:
            inv, inv_rows = span_ready()
            vectors_y_send()
        if i == ring_count - 2:
            teacher_top, teacher_total = teacher_ready()
            hidden_wait()
            vectors_x_send()
            multiply(0, first=True)
            for d in range(1, half - 2):
                multiply(-d)
                multiply(d)
    for i in range(ring_count - 4, ring_count):
        for way in (0, 1):
            for come in ring_wait(way, i):
                mate_send(*come)
        if i == ring_count - 4:
            for d in range(max(1, half - 2), half - 1):
                multiply(-d)
                multiply(d)
        if i == ring_count - 3:
            multiply(1 - half)
            multiply(half - 1)
    multiply(half)

    def target_column():
        parts = []
        for hh in (0, 1):
            row = jnp.where(core == 0, tgt[hh, 0:1, :], tgt[hh, 1:2, :])
            parts.append(jnp.broadcast_to(row, (128, tok)).T[:, 0:1])
        return jnp.concatenate(parts, axis=0)

    wanted = target_column()

    def hit(s):
        start = (s * nv + voc) * 2 * cols + xh * cols
        return wanted - start == lax.broadcasted_iota(jnp.int32, (2 * tok, cols), 1)

    student_top = jnp.max(jnp.maximum(logits[0], logits[1]), axis=1, keepdims=True)
    student_total = jnp.zeros((2 * tok, 1), F32)
    cross = jnp.zeros((2 * tok, 1), F32)
    target_logit = jnp.zeros((2 * tok, 1), F32)
    for s in (0, 1):
        value = logits[s]
        cross += jnp.sum(texp[s] * (tea[s].reshape(2 * tok, cols).astype(F32) - value), axis=1, keepdims=True)
        target_logit += jnp.sum(jnp.where(hit(s), value, 0.0), axis=1, keepdims=True)
        value = jnp.exp(value - student_top)
        logits[s] = value
        student_total += jnp.sum(value, axis=1, keepdims=True)
    stats[me] = to_rows([student_top, student_total, teacher_top, teacher_total, cross, target_logit], 8)

    def stats_send(i, carry):
        peer = plane_peer((me + i) % plane)
        remote(stats.at[me], stats.at[me], sts_sem.at[i], str_sem.at[i], peer).start()
        return carry

    def stats_wait(i, carry):
        src = (me + plane - i) % plane
        remote(stats.at[src], stats.at[src], sts_sem.at[i], str_sem.at[i], mate).wait_recv()
        remote(stats.at[me], stats.at[me], sts_sem.at[i], str_sem.at[i], mate).wait_send()
        return carry

    lax.fori_loop(1, plane, stats_send, 0)
    for copies in ring_copies:
        for copy in copies[-3:]:
            copy.wait_send()
    for copy in sent:
        copy.wait_send()
    sent.clear()
    lax.fori_loop(1, plane, stats_wait, 0)
    top_s, top_t = stats[0, 0:1, :], stats[0, 2:3, :]
    for i in range(1, plane):
        top_s = jnp.maximum(top_s, stats[i, 0:1, :])
        top_t = jnp.maximum(top_t, stats[i, 2:3, :])
    sum_s, sum_t, sum_x, sum_l = (jnp.zeros_like(top_s) for _ in range(4))
    for i in range(plane):
        part = stats[i]
        sum_s += part[1:2] * jnp.exp(part[0:1] - top_s)
        factor = jnp.exp(part[2:3] - top_t)
        sum_t += part[3:4] * factor
        sum_x += part[4:5] * factor
        sum_l += part[5:6]
    lse_s = top_s + jnp.log(sum_s)
    lse_t = top_t + jnp.log(sum_t)
    terms = sum_x / sum_t - lse_t + lse_s + CE_WEIGHT * (lse_s - sum_l)
    scales = to_columns(jnp.concatenate([lse_s, lse_t], axis=0))
    student_scale = jnp.exp(student_top - scales[:, 0:1])
    teacher_scale = jnp.exp(teacher_top - scales[:, 1:2])

    own_loss[0] = jnp.broadcast_to(jnp.sum(terms, axis=1, keepdims=True), (8, 128))
    begin(remote(own_loss.at[0], own_loss.at[1], los_sem.at[0, 0], lor_sem.at[0, 0], mate))

    def loss_start():
        remote(own_loss.at[1], own_loss.at[1], los_sem.at[0, 0], lor_sem.at[0, 0], mate).wait_recv()
        losses[z] = own_loss[0] + own_loss[1]
        loss_send(1)

    def loss_send(k):
        for way, peer in ((0, right), (1, left)):
            if k < half or way == 0:
                slot = losses.at[(z + nz - (k - 1)) % nz if way == 0 else (z + k - 1) % nz]
                begin(remote(slot, slot, los_sem.at[way, k], lor_sem.at[way, k], peer))

    def loss_wait(k):
        for way in (0, 1):
            if k < half or way == 0:
                slot = losses.at[(z + nz - k) % nz if way == 0 else (z + k) % nz]
                remote(slot, slot, los_sem.at[way, k], lor_sem.at[way, k], right).wait_recv()
        if k < half:
            loss_send(k + 1)

    for s in (0, 1):
        value = (1.0 + CE_WEIGHT) * (logits[s] * student_scale) - texp[s] * teacher_scale
        value = value - jnp.where(hit(s), CE_WEIGHT, 0.0)
        dlog[s] = (LOSS_SCALE * value).astype(BF16)

    quarter = tok // 4
    upper, lower = pl.ds(0, quarter), pl.ds(quarter, quarter)
    nt = (((1,), (1,)), ((), ()))

    def x_peer(step):
        return in_plane((xi + step + 4) % 4, yi)

    def y_peer(step):
        return in_plane(xi, (yi + step + ny) % ny)

    def stage_x(kind, way, y):
        step = 1 - 2 * way
        part = (upper, lower)[way if kind != 1 else 1 - way]
        source = snd_x.at[(xi + 2) % 4 if kind == 0 else (xi + step + 4) % 4, y, part]
        target = pass_x.at[way, y] if kind == 0 else rcv_x.at[way, y, part]
        return remote(source, target, xs_sem.at[kind, way, y], xr_sem.at[kind, way, y], x_peer(step))

    def stage_y(kind, way, x):
        step = 1 - 2 * way
        part = (upper, lower)[way if kind != 1 else 1 - way]
        source = snd_y.at[(yi + 2) % ny if kind == 0 else (yi + step + ny) % ny, x, part]
        target = pass_y.at[way, x] if kind == 0 else rcv_y.at[way, x, part]
        return remote(source, target, ys_sem.at[kind, way, x], yr_sem.at[kind, way, x], y_peer(step))

    def offset(i):
        return jnp.where(i == 0, 2, jnp.where(i == 1, 1, jnp.where(i == 2, 3, 0)))

    def slice_turn(i, carry):
        oy = offset(i // 2)
        y = (yi + oy) % ny
        lo = (xl + i) % 2
        v = y * 2 + lo
        span = pl.ds(pl.multiple_of(v * slice_width, slice_width), slice_width)
        part = lax.dot_general(dlog[0], wbuf[0, span, :], nt, preferred_element_type=F32)
        part += lax.dot_general(dlog[1], wbuf[1, span, :], nt, preferred_element_type=F32)
        part = part.astype(BF16)
        for hh in (0, 1):
            x = hh * 2 + lo
            snd_x[x, y] = part[hh * tok : hh * tok + half_tok]
            snd_y[y, x] = part[hh * tok + half_tok : (hh + 1) * tok]

        @pl.when(i % 2 == 0)
        def _():
            for way in (0, 1):
                stage_x(0, way, y).start()

        @pl.when(i % 2 == 1)
        def _():
            for way in (0, 1):
                stage_x(1, way, y).start()

        for hh in (0, 1):

            @pl.when(oy == 2)
            def _():
                for way in (0, 1):
                    stage_y(0, way, hh * 2 + lo).start()

            @pl.when(oy == 1)
            def _():
                stage_y(1, 0, hh * 2 + lo).start()

            @pl.when(oy == 3)
            def _():
                stage_y(1, 1, hh * 2 + lo).start()

        return carry

    lax.fori_loop(0, nv, slice_turn, 0)

    def pass_turn(i, carry):
        y = (yi + offset(i)) % ny
        for way in (0, 1):
            step = 1 - 2 * way
            part = (upper, lower)[way]
            stage_x(0, way, y).wait_recv()
            x = (xi + step + 4) % 4
            total = snd_x[x, y, part].astype(F32) + pass_x[way, y].astype(F32)
            snd_x[x, y, part] = total.astype(BF16)
            stage_x(2, way, y).start()
            stage_y(0, way, i).wait_recv()
            to = (yi + step + ny) % ny
            total = snd_y[to, i, part].astype(F32) + pass_y[way, i].astype(F32)
            snd_y[to, i, part] = total.astype(BF16)
            stage_y(2, way, i).start()
        return carry

    lax.fori_loop(0, ny, pass_turn, 0)
    loss_start()
    vectors_wait()
    cross_rows = exchange_wait(dots, dos_sem, dor_sem)

    def sum_x(oy):
        y = (yi + oy) % ny
        total = snd_x[xi, y].astype(F32)
        for way in (0, 1):
            for kind in (1, 2):
                stage_x(kind, way, y).wait_recv()
            total = total + rcv_x[way, y].astype(F32)
        return total

    def sum_y(ox):
        x = (xi + ox) % 4
        total = snd_y[yi, x].astype(F32)
        for way in (0, 1):
            for kind in (1, 2):
                stage_y(kind, way, x).wait_recv()
            total = total + rcv_y[way, x].astype(F32)
        return total

    def fold(value):
        parts = [value[:, i : i + 128] for i in range(0, slice_width, 128)]
        return functools.reduce(lambda a, b: a + b, parts)

    def products_with(vectors, value):
        return [fold(vectors[c].astype(F32) * value) for c in range(4)]

    def add(left_list, right_list):
        return [a + b for a, b in zip(left_list, right_list)]

    first_products = [jnp.zeros((half_tok, 128), F32)] * 4
    for oy in (2, 1, 3):
        value = sum_x(oy)
        two_y[oy] = value.astype(BF16)
        begin(remote(two_y.at[oy], end_y.at[oy], eys_sem.at[oy], eyr_sem.at[oy], in_plane(xi, (yi + oy) % ny)))
        first_products = add(first_products, products_with(vec_y[(yi + oy) % ny], value))
    loss_wait(1)
    first_half = sum_x(0)
    first_products = add(first_products, products_with(vec_y[yi], first_half))
    column_sums = {}
    for ox in range(1, 4):
        column_sums[ox] = sum_y(ox)
        two_x[ox] = column_sums[ox].astype(BF16)
    second_half = sum_y(0)
    column_sums[0] = second_half
    near_products = [jnp.zeros((half_tok, 128), F32)] * 4
    away_products = near_products
    for ox in range(4):
        x = (xi + ox) % 4
        found = products_with(vec_x[x], column_sums[ox])
        same = x // 2 == xh
        near_products = [a + jnp.where(same, b, 0.0) for a, b in zip(near_products, found)]
        away_products = [a + jnp.where(same, 0.0, b) for a, b in zip(away_products, found)]

    def message(first_part, second_part):
        columns = [
            jnp.sum(jnp.concatenate([a, b], axis=0), axis=1, keepdims=True) for a, b in zip(first_part, second_part)
        ]
        return to_rows(columns, 8)

    away = message([jnp.zeros((half_tok, 128), F32)] * 4, away_products)
    close = message(first_products, near_products)
    told[0] = jnp.where(xh == 0, close, away)
    told[1] = jnp.where(xh == 0, away, close)

    def told_send(i, carry):
        to = (me + i) % plane
        remote(told.at[to // nv], heard.at[me], tos_sem.at[i], tor_sem.at[i], plane_peer(to)).start()
        return carry

    def told_wait(i, carry):
        src = (me + plane - i) % plane
        remote(heard.at[src], heard.at[src], tos_sem.at[i], tor_sem.at[i], mate).wait_recv()
        remote(told.at[0], heard.at[me], tos_sem.at[i], tor_sem.at[i], mate).wait_send()
        return carry

    lax.fori_loop(1, plane, told_send, 0)
    for ox in (2, 1, 3):
        begin(remote(two_x.at[ox], end_x.at[ox], exs_sem.at[ox], exr_sem.at[ox], in_plane((xi + ox) % 4, yi)))
    heard[me] = close

    def slice_sent(i, carry):
        for kind in range(3):
            for way in (0, 1):
                stage_x(kind, way, i).wait_send()
                stage_y(kind, way, i).wait_send()
        return carry

    lax.fori_loop(0, ny, slice_sent, 0)

    loss_wait(2)
    for oy in range(1, ny):
        remote(end_y.at[oy], end_y.at[oy], eys_sem.at[oy], eyr_sem.at[oy], mate).wait_recv()
        first_half = first_half + end_y[oy].astype(F32)
    for ox in range(1, 4):
        remote(end_x.at[ox], end_x.at[ox], exs_sem.at[ox], exr_sem.at[ox], mate).wait_recv()
        second_half = second_half + end_x[ox].astype(F32)
    cotangent = jnp.concatenate([first_half.astype(BF16), second_half.astype(BF16)], axis=0)

    lax.fori_loop(1, plane, told_wait, 0)
    found = heard[0]
    for i in range(1, plane):
        found = found + heard[i]
    d0, d1, d2, d3 = (found[c : c + 1] / width for c in range(4))
    e10, e20, e30, e21, e31, e32 = (cross_rows[c : c + 1] / width for c in range(6))
    s3 = d3
    s2 = d2 - s3 * e32
    s1 = d1 - s3 * e31 - s2 * e21
    s0 = d0 - s3 * e30 - s2 * e20 - s1 * e10
    pull = to_columns(inv_rows[0:4] ** 3 * jnp.concatenate([s0, s1, s2, s3], axis=0))
    value = cotangent

    def hand_out(slot_index):
        pltpu.make_async_copy(ys.at[core, slot_index], out.at[0, slot_index, core], loc_sem.at[slot_index]).start()
        begin(
            remote(
                ys.at[other, slot_index], out.at[0, slot_index, core], os_sem.at[slot_index], or_sem.at[slot_index], mate
            )
        )

    for c in (3, 2, 1, 0):
        grad = heads_dot(value, ws[SPAN_AT[c]], True)
        fresh = value.astype(F32) + inv[c] * gain(c) * grad - saved(c) * pull[:, c : c + 1]
        value = fresh.astype(BF16)
        ys[SPAN_AT[c]] = value
        if c == 2:
            hand_out(1)
    hand_out(0)
    for k in range(3, half + 1):
        loss_wait(k)
    loss_total = losses[0]
    for i in range(1, nz):
        loss_total = loss_total + losses[i]
    loss_ref[0, 0] = jnp.max(loss_total) / (4 * tok * nz)
    for slot_index in (1, 0):
        pltpu.make_async_copy(
            ys.at[core, slot_index], out.at[0, slot_index, core], loc_sem.at[slot_index]
        ).wait()
        slot = out.at[0, slot_index, other]
        remote(slot, slot, os_sem.at[slot_index], or_sem.at[slot_index], mate).wait_recv()
    for copy in sent:
        copy.wait_send()


def solution(mesh):
    n_seq, n_voc = mesh.shape["seq"], mesh.shape["vocab"]
    nz = n_seq // 2

    def per_device(hidden, head_weight, teacher_logits, targets, span_inputs, span_gains, span_weights):
        _, tok, width = hidden.shape
        rows, shard = head_weight.shape
        cols = shard // 2
        slice_width = span_inputs.shape[4]
        heads = span_weights.shape[2]
        plane = 2 * n_voc
        half = nz // 2
        dma = pltpu.SemaphoreType.DMA
        any_space = pl.BlockSpec(memory_space=pl.ANY)
        operands = [
            pltpu.with_memory_space_constraint(a, pltpu.HBM)
            for a in (hidden, head_weight, teacher_logits, targets, span_inputs, span_gains, span_weights)
        ]
        grads, loss = pl.pallas_call(
            functools.partial(kernel, nz, n_voc),
            out_shape=(
                jax.ShapeDtypeStruct((1, 2, 2, tok, slice_width), BF16),
                jax.ShapeDtypeStruct((1, 1), F32),
            ),
            in_specs=[any_space] * 7,
            out_specs=(any_space, pl.BlockSpec(memory_space=pltpu.SMEM)),
            scratch_shapes=[
                pltpu.VMEM((2, width, cols), BF16),
                pltpu.VMEM((2, tok, width), BF16),
                pltpu.VMEM((2, 2, tok, cols), BF16),
                pltpu.VMEM((2, 2, tok), jnp.int32),
                pltpu.VMEM((2, 2 * tok, cols), F32),
                pltpu.VMEM((2, 2 * tok, cols), F32),
                pltpu.VMEM((2, 2 * tok, cols), BF16),
                pltpu.VMEM((plane, 8, 2 * tok), F32),
                pltpu.VMEM((4, n_voc // 2, tok // 2, slice_width), BF16),
                pltpu.VMEM((2, n_voc // 2, tok // 2, slice_width), BF16),
                pltpu.VMEM((2, n_voc // 2, tok // 4, slice_width), BF16),
                pltpu.VMEM((n_voc // 2, 4, tok // 2, slice_width), BF16),
                pltpu.VMEM((2, 4, tok // 2, slice_width), BF16),
                pltpu.VMEM((2, 4, tok // 4, slice_width), BF16),
                pltpu.VMEM((4, tok // 2, slice_width), BF16),
                pltpu.VMEM((4, tok // 2, slice_width), BF16),
                pltpu.VMEM((n_voc // 2, tok // 2, slice_width), BF16),
                pltpu.VMEM((n_voc // 2, tok // 2, slice_width), BF16),
                pltpu.VMEM((2, 2, tok, slice_width), BF16),
                pltpu.VMEM((2, 2, slice_width), F32),
                pltpu.VMEM((2, 2, heads, HEAD, HEAD), BF16),
                pltpu.VMEM((n_voc, 8, tok), F32),
                pltpu.VMEM((n_voc, 8, tok), F32),
                pltpu.VMEM((n_voc // 2, 4, tok // 2, slice_width), BF16),
                pltpu.VMEM((4, 4, tok // 2, slice_width), BF16),
                pltpu.VMEM((2, 8, tok), F32),
                pltpu.VMEM((plane, 8, tok), F32),
                pltpu.VMEM((2, 8, 128), F32),
                pltpu.VMEM((nz, 8, 128), F32),
                pltpu.VMEM((2, 2, tok, slice_width), BF16),
                dma((7,)),
                dma((2, 4 * half - 2)),
                dma((2, 4 * half - 2)),
                dma((4 * nz,)),
                dma((4 * nz,)),
                dma((10,)),
                dma((10,)),
                dma((plane,)),
                dma((plane,)),
                dma((3, 2, n_voc // 2)),
                dma((3, 2, n_voc // 2)),
                dma((3, 2, 4)),
                dma((3, 2, 4)),
                dma((4,)),
                dma((4,)),
                dma((n_voc // 2,)),
                dma((n_voc // 2,)),
                dma((n_voc,)),
                dma((n_voc,)),
                dma((n_voc,)),
                dma((n_voc,)),
                dma((2, half + 1)),
                dma((2, half + 1)),
                dma((n_voc // 2,)),
                dma((n_voc // 2,)),
                dma((4,)),
                dma((4,)),
                dma((plane,)),
                dma((plane,)),
                dma((2,)),
                dma((2,)),
            ],
            compiler_params=pltpu.CompilerParams(
                collective_id=0, has_side_effects=True, vmem_limit_bytes=48 * 1024 * 1024
            ),
        )(*operands)
        return grads, loss.reshape(())

    placed = (
        P(None, "seq", None),
        P("seq", ("section", "vocab")),
        P(None, "seq", ("section", "vocab")),
        P(None, "seq"),
        P("section", None, None, "seq", "vocab"),
        P("section", None, "vocab"),
        P("section", None, "vocab", None, None),
    )
    return jax.shard_map(
        per_device,
        mesh=mesh,
        in_specs=placed,
        out_specs=(P("section", None, None, "seq", "vocab"), P()),
        check_vma=False,
    )
```
